32 devices in a mesh: gx: 4 (over y, x), gy: 2 (over core), gz: 4 (over z).
Axes of the slice: x: 2, y: 2, z: 4, core: 2. Of those that a mesh axis runs over, the one named last changes fastest.
Arguments:
- right_side: float32 [32, 64, 512], P('gx', 'gy', 'gz'), may hold values from -8 to 8
- alpha_coef: float32 [32, 64, 512], P('gx', 'gy', 'gz'), may hold values from 0.25 to 4
- beta_coef: float32 [32, 64, 512], P('gx', 'gy', 'gz'), may hold values from 0.25 to 4
Outputs:
- solution_field: float32 [32, 64, 512], P('gx', 'gy', 'gz')
- residual_field: float32 [32, 64, 512], P('gx', 'gy', 'gz')
The draws below stay inside these ranges and needn't reach their ends.
All inputs are finite; a program needn't handle non-finite values.
Results may differ from the reference program's by a relative error of at most 0.0003.
Values sent between devices are 32-bit elements; how exact they have to be, the bound alone decides.
No kernel may reach another device: no remote copies, remote signals or barrier semaphores. Data moves between devices by JAX's collectives and lax.ppermute only.
A program may use at most 64 MiB of HBM per device.

```python
import math
import jax
import jax.numpy as jnp

LEVELS = 3
SWEEPS = 4
BOTTOM = 12
NX = 32
NY = 64
NZ = 512


def levels(stream_key, shape, split, least, top_value):
    def one(position, blocks):
        draws = jax.random.uniform(jax.random.fold_in(jax.random.fold_in(stream_key, 6), position), (blocks,), jnp.float32, least / len(split), top_value / len(split))
        return jnp.repeat(jnp.exp(draws), shape[position] // blocks).reshape((-1,) + (1,) * (len(shape) - position - 1))

    loudness = one(*split[0])
    for cut in split[1:]:
        loudness = loudness * one(*cut)
    return loudness


def scatter_about(own_key, dims, deviation, bound, split=(), dtype=jnp.bfloat16):
    result = jax.random.normal(own_key, dims, jnp.float32) * deviation
    if len(split) > 0:
        result = levels(own_key, dims, split, -0.22, 0.18) * result
    return jnp.clip(result, min=-bound, max=bound).astype(dtype)


def setup_inputs(seed: int = 0) -> dict:
    seeds = jax.random.split(jax.random.key(seed), 4)
    right_side = scatter_about(seeds[0], (NX, NY, NZ), 1.0, 8.0, ((0, 4), (1, 2), (2, 4)), jnp.float32)
    alpha_coef = jnp.clip(jnp.exp(math.log(4.0) - 2.7725887 * jax.random.uniform(seeds[1], (NX, NY, NZ), jnp.float32) ** levels(seeds[1], (NX, NY, NZ), ((0, 4), (1, 2), (2, 4)), -0.2, 0.2)), 0.25, 4.0)
    beta_coef = jnp.clip(jnp.exp(math.log(4.0) - 2.7725887 * jax.random.uniform(seeds[2], (NX, NY, NZ), jnp.float32) ** levels(seeds[2], (NX, NY, NZ), ((0, 4), (1, 2), (2, 4)), -0.2, 0.2)), 0.25, 4.0)
    return dict(right_side=right_side, alpha_coef=alpha_coef, beta_coef=beta_coef)


SHIFT_BASE = 0.01
UPPER_EIG = 2.0
SMOOTH_LOWER = 0.25
BOTTOM_LOWER = 0.02


def split_padded(padded):
    return (padded[:-2, 1:-1, 1:-1], padded[2:, 1:-1, 1:-1],
            padded[1:-1, :-2, 1:-1], padded[1:-1, 2:, 1:-1],
            padded[1:-1, 1:-1, :-2], padded[1:-1, 1:-1, 2:])


def zero_pad(field):
    return jnp.pad(field, 1)


def level_operator(beta_level, alpha_level, padded_beta, shift):
    coeffs = tuple(0.5 * (beta_level + other) for other in split_padded(padded_beta))
    diagonal = shift * alpha_level
    for coeff in coeffs:
        diagonal = diagonal + coeff
    return coeffs, diagonal


def apply_operator(field, operator, pad_field):
    coeffs, diagonal = operator
    others = split_padded(pad_field(field))
    total = coeffs[0] * others[0]
    for index in range(1, 6):
        total = total + coeffs[index] * others[index]
    return diagonal * field - total


def chebyshev(iterate, rhs_level, operator, count, lower, zero_start, pad_field):
    diagonal = operator[1]
    center = (UPPER_EIG + lower) / 2.0
    half_width = (UPPER_EIG - lower) / 2.0
    sigma_ratio = center / half_width
    rho_old = 1.0 / sigma_ratio
    if zero_start:
        remain = rhs_level
    else:
        remain = rhs_level - apply_operator(iterate, operator, pad_field)
    update = remain / diagonal / center
    iterate = iterate + update
    for sweep_index in range(count - 1):
        remain = rhs_level - apply_operator(iterate, operator, pad_field)
        rho_new = 1.0 / (2.0 * sigma_ratio - rho_old)
        update = (rho_new * rho_old) * update + (2.0 * rho_new / half_width) * (remain / diagonal)
        iterate = iterate + update
        rho_old = rho_new
    return iterate


def restrict_mean(field):
    first, second, third = field.shape
    blocks = field.reshape(first // 2, 2, second // 2, 2, third // 2, 2)
    return jnp.sum(blocks, axis=(1, 3, 5)) * 0.125


def prolong_copy(field):
    return jnp.repeat(jnp.repeat(jnp.repeat(field, 2, axis=0), 2, axis=1), 2, axis=2)


def reference(right_side, alpha_coef, beta_coef):
    betas = [beta_coef]
    alphas = [alpha_coef]
    for level in range(LEVELS):
        betas.append(restrict_mean(betas[-1]))
        alphas.append(restrict_mean(alphas[-1]))
    operators = [level_operator(betas[level], alphas[level], zero_pad(betas[level]), SHIFT_BASE * 4.0 ** level)
                 for level in range(LEVELS + 1)]
    rhs_levels = [right_side]
    smoothed = []
    for level in range(LEVELS):
        iterate = chebyshev(jnp.zeros_like(rhs_levels[level]), rhs_levels[level], operators[level],
                            SWEEPS, SMOOTH_LOWER, True, zero_pad)
        remain = rhs_levels[level] - apply_operator(iterate, operators[level], zero_pad)
        smoothed.append(iterate)
        rhs_levels.append(4.0 * restrict_mean(remain))
    correction = chebyshev(jnp.zeros_like(rhs_levels[LEVELS]), rhs_levels[LEVELS], operators[LEVELS],
                           BOTTOM, BOTTOM_LOWER, True, zero_pad)
    for level in range(LEVELS - 1, -1, -1):
        start_field = smoothed[level] + prolong_copy(correction)
        correction = chebyshev(start_field, rhs_levels[level], operators[level],
                               SWEEPS, SMOOTH_LOWER, False, zero_pad)
    residual_field = right_side - apply_operator(correction, operators[0], zero_pad)
    return correction, residual_field
```

```python
import jax
import jax.numpy as jnp
from jax import lax
from jax.experimental import pallas as pl
from jax.experimental.pallas import tpu as pltpu
from jax.sharding import PartitionSpec as P

LEVELS = 3
SWEEPS = 4
BOTTOM = 12


SHIFT_BASE = 0.01
UPPER_EIG = 2.0
SMOOTH_LOWER = 0.25
BOTTOM_LOWER = 0.02


def with_halo(block, sides, width):
    for axis, dim in sides:
        count = lax.axis_size(axis)
        forward = [(i, i + 1) for i in range(count - 1)]
        backward = [(target, source) for source, target in forward]
        low = lax.ppermute(
            lax.slice_in_dim(block, block.shape[dim] - width, None, axis=dim), axis, forward
        )
        high = lax.ppermute(lax.slice_in_dim(block, 0, width, axis=dim), axis, backward)
        block = jnp.concatenate([low, block, high], axis=dim)
    return block


def partner_2(array, axis, distance):
    return lax.ppermute(array, axis, [(i, i ^ 1 << distance) for i in range(lax.axis_size(axis))])


def split_padded(padded):
    return (
        padded[:-2, 1:-1, 1:-1],
        padded[2:, 1:-1, 1:-1],
        padded[1:-1, :-2, 1:-1],
        padded[1:-1, 2:, 1:-1],
        padded[1:-1, 1:-1, :-2],
        padded[1:-1, 1:-1, 2:],
    )


def zero_pad(field):
    return jnp.pad(field, 1)


def rim_iterate(field):
    return with_halo(field, (("gx", 0), ("gy", 1), ("gz", 2)), 1)


def rim_coefficient(field):
    return with_halo(field, (("gx", 0), ("gy", 1), ("gz", 2)), 1)


def level_operator(beta_level, alpha_level, padded_beta, shift):
    coeffs = tuple((0.5 * (beta_level + other) for other in split_padded(padded_beta)))
    diagonal = shift * alpha_level
    for coeff in coeffs:
        diagonal = diagonal + coeff
    return (coeffs, diagonal)


def apply_operator(field, operator, pad_field):
    coeffs, diagonal = operator
    others = split_padded(pad_field(field))
    total = coeffs[0] * others[0]
    for index in range(1, 6):
        total = total + coeffs[index] * others[index]
    return diagonal * field - total


def chebyshev(iterate, rhs_level, operator, count, lower, zero_start, pad_field):
    diagonal = operator[1]
    center = (UPPER_EIG + lower) / 2.0
    half_width = (UPPER_EIG - lower) / 2.0
    sigma_ratio = center / half_width
    rho_old = 1.0 / sigma_ratio
    if zero_start:
        remain = rhs_level
    else:
        remain = rhs_level - apply_operator(iterate, operator, pad_field)
    update = remain / diagonal / center
    iterate = iterate + update
    for sweep_index in range(count - 1):
        remain = rhs_level - apply_operator(iterate, operator, pad_field)
        rho_new = 1.0 / (2.0 * sigma_ratio - rho_old)
        update = rho_new * rho_old * update + 2.0 * rho_new / half_width * (remain / diagonal)
        iterate = iterate + update
        rho_old = rho_new
    return iterate


def restrict_mean(field):
    first, second, third = field.shape
    blocks = field.reshape(first // 2, 2, second // 2, 2, third // 2, 2)
    return jnp.sum(blocks, axis=(1, 3, 5)) * 0.125


def prolong_copy(field):
    return jnp.repeat(jnp.repeat(jnp.repeat(field, 2, axis=0), 2, axis=1), 2, axis=2)


def join_partner(packed, partner, device_index, bit_index, dim):
    position = device_index // 2**bit_index % 2
    lower_first = jnp.concatenate([packed, partner], axis=dim)
    upper_first = jnp.concatenate([partner, packed], axis=dim)
    return jnp.where(position == 0, lower_first, upper_first)


def shards(right_side, alpha_coef, beta_coef):
    betas = [beta_coef]
    alphas = [alpha_coef]
    for level in range(LEVELS):
        betas.append(restrict_mean(betas[-1]))
        alphas.append(restrict_mean(alphas[-1]))
    operators = []
    for level in range(LEVELS):
        padded_beta = rim_coefficient(betas[level])
        operators.append(
            level_operator(betas[level], alphas[level], padded_beta, SHIFT_BASE * 4.0**level)
        )
    rhs_levels = [right_side]
    smoothed = []
    for level in range(LEVELS):
        iterate = chebyshev(
            jnp.zeros_like(rhs_levels[level]),
            rhs_levels[level],
            operators[level],
            SWEEPS,
            SMOOTH_LOWER,
            True,
            rim_iterate,
        )
        remain = rhs_levels[level] - apply_operator(iterate, operators[level], rim_iterate)
        smoothed.append(iterate)
        rhs_levels.append(4.0 * restrict_mean(remain))
    coarse_rhs = rhs_levels[LEVELS]
    local_shape = coarse_rhs.shape
    packed = jnp.stack([coarse_rhs, betas[LEVELS], alphas[LEVELS]])
    index_x = lax.axis_index("gx")
    index_y = lax.axis_index("gy")
    index_z = lax.axis_index("gz")
    for bit_index in range(lax.axis_size("gx").bit_length() - 1):
        partner = partner_2(packed, "gx", bit_index)
        packed = join_partner(packed, partner, index_x, bit_index, 1)
    for bit_index in range(lax.axis_size("gy").bit_length() - 1):
        partner = partner_2(packed, "gy", bit_index)
        packed = join_partner(packed, partner, index_y, bit_index, 2)
    for bit_index in range(lax.axis_size("gz").bit_length() - 1):
        partner = partner_2(packed, "gz", bit_index)
        packed = join_partner(packed, partner, index_z, bit_index, 3)
    whole_rhs = packed[0]
    whole_beta = packed[1]
    whole_alpha = packed[2]
    bottom_operator = level_operator(
        whole_beta, whole_alpha, zero_pad(whole_beta), SHIFT_BASE * 4.0**LEVELS
    )
    whole_correction = chebyshev(
        jnp.zeros_like(whole_rhs), whole_rhs, bottom_operator, BOTTOM, BOTTOM_LOWER, True, zero_pad
    )
    starts = (index_x * local_shape[0], index_y * local_shape[1], index_z * local_shape[2])
    correction = lax.dynamic_slice(whole_correction, starts, local_shape)
    for level in range(LEVELS - 1, -1, -1):
        start_field = smoothed[level] + prolong_copy(correction)
        correction = chebyshev(
            start_field,
            rhs_levels[level],
            operators[level],
            SWEEPS,
            SMOOTH_LOWER,
            False,
            rim_iterate,
        )
    residual_field = right_side - apply_operator(correction, operators[0], rim_iterate)
    return (correction, residual_field)


GX, GY, GZ = 4, 2, 4
BLOCK = (8, 32, 128)
RING = ("gx", "gy")
ALL = ("gx", "gy", "gz")
TILE = (8, 128)
PLANES = 24
PLANES1 = 12


def chunk_of(x, y, z):
    natural = 2 * (x ^ (x >> 1)) + y
    return natural + (z % 2) * (7 - 2 * natural)


def position():
    return lax.axis_index("gx"), lax.axis_index("gy"), lax.axis_index("gz")


def swap_pairs(odd):
    place = {}
    for x in range(GX):
        for y in range(GY):
            for z in range(GZ):
                place[8 * z + chunk_of(x, y, z)] = (x * GY + y) * GZ + z
    count = len(place)
    if odd:
        pairs = [(i, i + 1) for i in range(1, count - 1, 2)]
    else:
        pairs = [(i, i + 1) for i in range(0, count, 2)]
    return [(place[a], place[b]) for a, b in pairs] + [(place[b], place[a]) for a, b in pairs]


def lane_ids():
    return lax.broadcasted_iota(jnp.int32, TILE, 1)


def row_ids():
    return lax.broadcasted_iota(jnp.int32, TILE, 0)


def lanes(value, shift):
    return pltpu.roll(value, shift % 128, value.ndim - 1)


def rows(value, shift):
    return pltpu.roll(value, shift % 8, value.ndim - 2)


def regroup(tiles, axis, width, ids):
    move = lanes if axis == 1 else rows
    low = (ids // width) % 2 == 0
    high = (ids // (2 * width)) % 2 == 0
    a, b, c, d = tiles
    a, b = jnp.where(low, a, move(b, width)), jnp.where(low, move(a, -width), b)
    c, d = jnp.where(low, c, move(d, width)), jnp.where(low, move(c, -width), d)
    a, c = jnp.where(high, a, move(c, 2 * width)), jnp.where(high, move(a, -2 * width), c)
    b, d = jnp.where(high, b, move(d, 2 * width)), jnp.where(high, move(b, -2 * width), d)
    return [a, b, c, d]


def depth_of(k, group):
    half, part = group // 2, group % 2
    plane = k + 4 * part
    return 15 - plane if half else plane


def pack_kernel(b_ref, alpha_ref, beta_ref, out_ref, turned, staged):
    z = lax.axis_index("gz")
    lane = lane_ids()
    for a, ref in enumerate((b_ref, alpha_ref, beta_ref)):
        for xg in range(2):
            slot = turned.at[2 * a + xg]
            slot[...] = ref[4 * xg : 4 * xg + 4].reshape(128, 128).T
            for k in range(4):
                tiles = [slot[pl.ds(depth_of(k, g), 8, stride=16), :] for g in range(4)]
                for x4, tile in enumerate(regroup(tiles, 1, 32, lane)):
                    staged[pl.ds(a * 32 + k * 8 + 2 * x4 + xg, 8, stride=96), :] = tile
    for x in range(GX):
        for y in range(GY):
            start = pl.multiple_of(chunk_of(x, y, z) * 96, 96)
            out_ref[x * GY + y] = staged[pl.ds(start, 96), :]


def pack(b, alpha, beta):
    return pl.pallas_call(
        pack_kernel,
        out_shape=jax.ShapeDtypeStruct((8, 96, 128), jnp.float32),
        in_specs=[pl.BlockSpec(memory_space=pltpu.VMEM)] * 3,
        out_specs=pl.BlockSpec(memory_space=pltpu.VMEM),
        scratch_shapes=[pltpu.VMEM((6, 128, 128), jnp.float32), pltpu.VMEM((768, 128), jnp.float32)],
        name="pack",
    )(b, alpha, beta)


def slab_kernel(in_ref, out_ref):
    lane, row = lane_ids(), row_ids()
    low = (lane // 32) % 2 == 0
    for a in range(3):
        for k in range(4):
            part = ([], [])
            for x in range(GX):
                first = in_ref[2 * x, pl.ds(a * 32 + k * 8, 8), :]
                second = in_ref[2 * x + 1, pl.ds(a * 32 + k * 8, 8), :]
                part[0].append(jnp.where(low, first, lanes(second, 32)))
                part[1].append(jnp.where(low, lanes(first, -32), second))
            for pp in range(2):
                for xv, tile in enumerate(regroup(part[pp], 0, 2, row)):
                    out_ref[a, k + 4 * pp, xv] = tile


def to_slab(received):
    return pl.pallas_call(
        slab_kernel,
        out_shape=jax.ShapeDtypeStruct((3, 8, 4) + TILE, jnp.float32),
        in_specs=[pl.BlockSpec(memory_space=pltpu.VMEM)],
        out_specs=pl.BlockSpec(memory_space=pltpu.VMEM),
        name="to_slab",
    )(received)


class Planes:
    def __init__(self, upper, cut, lower=None, base=0):
        self.upper, self.cut, self.lower, self.base = upper, cut, lower, base

    def __getitem__(self, p):
        return self.upper[p - self.cut] if p >= self.cut else self.lower[p - self.base]

    def __setitem__(self, p, value):
        if p >= self.cut:
            self.upper[p - self.cut] = value
        else:
            self.lower[p - self.base] = value


def x_up(value):
    return jnp.concatenate([value[1:], rows(value[:1], -1)], axis=0)


def x_down(value):
    return jnp.concatenate([rows(value[-1:], 1), value[:-1]], axis=0)


def couple(v, p, cx, cy, cz, dup):
    here, by_x, by_y = v[p], cx[p], cy[p]
    total = by_x * x_up(here) + x_down(by_x * here)
    total = total + (by_y * lanes(here, -dup) + lanes(by_y * here, dup))
    return total + (cz[p] * v[p - 1] + cz[p + 1] * v[p + 1])


def chebyshev_factors(count, lower):
    center = (UPPER_EIG + lower) / 2.0
    half_width = (UPPER_EIG - lower) / 2.0
    ratio = center / half_width
    old = 1.0 / ratio
    out = [(0.0, 1.0 / center)]
    for _ in range(count - 1):
        new = 1.0 / (2.0 * ratio - old)
        out.append((new * old, 2.0 * new / half_width))
        old = new
    return out


def smooth(v_pair, d, b, dinv, coeffs, factors, first, last, dup):
    old, new = v_pair
    for number, (carry, gain) in enumerate(factors):
        for p in range(first + number, last):
            t = (b[p] + couple(old, p, *coeffs, dup)) * dinv[p] - old[p]
            step = gain * t if carry == 0.0 else carry * d[p] + gain * t
            if number + 1 < len(factors):
                d[p] = step
            new[p] = old[p] + step
        new[last] = lanes(new[last - 1], 64)
        old, new = new, old
    return old


def level_coefficients(beta, alpha, first, last, shift, dup, cx, cy, cz, dinv, diag, ends, seam):
    lane, row = lane_ids(), row_ids()
    groups = beta[first].shape[0]
    y_last = (lane % 64) // dup == 64 // dup - 1
    y_first = (lane % 64) // dup == 0
    y_rim = jnp.where(y_last | y_first, 0.5, 0.0)
    rim = [y_rim] * groups
    rim[0] = rim[0] + jnp.where(row == 0, 0.5, 0.0)
    rim[-1] = rim[-1] + jnp.where(row == 7, 0.5, 0.0)
    rim = jnp.stack(rim)
    face = 0.5 * (beta[first - 1] + beta[first])
    for p in range(first, last):
        here = beta[p]
        by_x = 0.5 * (here + x_up(here))
        by_x = jnp.concatenate([by_x[:-1], jnp.where(row == 7, 0.0, by_x[-1:])], axis=0)
        by_y = jnp.where(y_last, 0.0, 0.5 * (here + lanes(here, -dup)))
        after = beta[p + 1] if p + 1 < last else lanes(here, 64)
        next_face = 0.5 * (here + after)
        total = shift * alpha[p] + by_x + x_down(by_x)
        total = total + (by_y + lanes(by_y, dup)) + here * rim + (face + next_face)
        cx[p], cy[p] = by_x, by_y
        cz[p] = face * ends if p == seam else face
        if diag is not None and p >= seam:
            diag[p] = total
        dinv[p] = 1.0 / jnp.where(total > 0.0, total, 1.0)
        face = next_face
    cz[last] = face


def restrict_pair(first, second, dup):
    lane = lane_ids()
    total = first + second
    groups = total.shape[0]
    total = jnp.concatenate([total[i : i + 1] + total[i + 1 : i + 2] for i in range(0, groups, 2)], axis=0)
    return total + jnp.where((lane // dup) % 2 == 0, lanes(total, -dup), lanes(total, dup))


def halo_masks():
    x, y, z = position()
    chunk = chunk_of(x, y, z)
    half = lane_ids() // 64
    return chunk, (half + chunk % 2) == 1


def ends_factor():
    x, y, z = position()
    slab = 8 * z + chunk_of(x, y, z)
    half = lane_ids() // 64
    end = ((half == 0) & (slab == 0)) | ((half == 1) & (slab == 8 * GZ - 1))
    return jnp.where(end, 0.0, 1.0)


def down_kernel(
    own, even, odd,
    gather, rim, u0, b0, dinv0, diag0, cx0, cy0, cz0, u1, b1, dinv1, cx1, cy1, cz1,
    beta_s, alpha_s, b_s, dinv_s, cx_s, cy_s, cz_s, v_a, v_b, d_s,
    beta1_s, alpha1_s, b1_s, w_a, w_b, e_s,
):
    lane = lane_ids()
    _, from_even = halo_masks()
    ends = ends_factor()

    def field(a, p):
        if p >= 16:
            return own[a, p - 16]
        if p >= 8:
            return lanes(jnp.where(from_even, odd[a, 15 - p], even[a, 15 - p]), 64)
        return jnp.where(from_even, even[a, p], odd[a, p])

    for p in range(PLANES):
        beta_s[p] = field(2, p)
        alpha_s[p] = field(1, p)
    b = Planes(b0, 12, b_s)
    for p in range(4, PLANES):
        b[p] = field(0, p)
    cx, cy, cz = Planes(cx0, 12, cx_s), Planes(cy0, 12, cy_s), Planes(cz0, 12, cz_s)
    dinv = Planes(dinv0, 12, dinv_s)
    diag = Planes(diag0, 16)
    level_coefficients(beta_s, alpha_s, 4, PLANES, SHIFT_BASE, 1, cx, cy, cz, dinv, diag, ends, 16)
    diag_all = lambda p: diag[p]

    factors = chebyshev_factors(SWEEPS, SMOOTH_LOWER)
    for p in range(4, PLANES):
        start = factors[0][1] * (b[p] * dinv[p])
        v_a[p] = start
        d_s[p] = start
    v_a[PLANES] = lanes(v_a[PLANES - 1], 64)
    v = smooth((v_a, v_b), d_s, b, dinv, (cx, cy, cz), factors[1:], 5, PLANES, 1)
    for p in range(8):
        u0[p] = v[16 + p]

    def residual(v, p, b, dinv, coeffs, dup):
        return ((b[p] + couple(v, p, *coeffs, dup)) * dinv[p] - v[p]) / dinv[p]

    b_one = Planes(b1, 8, b1_s)
    for p in range(4, PLANES1):
        pair = [residual(v, 2 * p + i, b, dinv, (cx, cy, cz), 1) for i in range(2)]
        b_one[p] = 0.5 * restrict_pair(*pair, 1)
    for p in range(PLANES1):
        beta1_s[p] = 0.125 * restrict_pair(beta_s[2 * p], beta_s[2 * p + 1], 1)
        alpha1_s[p] = 0.125 * restrict_pair(alpha_s[2 * p], alpha_s[2 * p + 1], 1)
    cx, cy, cz, dinv = Planes(cx1, 2), Planes(cy1, 2), Planes(cz1, 2), Planes(dinv1, 2)
    level_coefficients(beta1_s, alpha1_s, 2, PLANES1, SHIFT_BASE * 4.0, 2, cx, cy, cz, dinv, None, ends, 8)
    for p in range(4, PLANES1):
        start = factors[0][1] * (b_one[p] * dinv[p])
        w_a[p] = start
        e_s[p] = start
    w_a[PLANES1] = lanes(w_a[PLANES1 - 1], 64)
    w = smooth((w_a, w_b), e_s, b_one, dinv, (cx, cy, cz), factors[1:], 5, PLANES1, 2)
    for p in range(4):
        u1[p] = w[8 + p]
        rim[20 + 2 * p : 22 + 2 * p] = jnp.where(lane % 2 == 0, w[8 + p], b_one[8 + p])
    for p in range(5):
        rim[4 * p : 4 * p + 4] = u0[p]
    for p in range(2):
        pair = [residual(w, 8 + 2 * p + i, b_one, dinv, (cx, cy, cz), 2) for i in range(2)]
        b_two = 0.5 * restrict_pair(*pair, 2)
        beta_two = 0.125 * restrict_pair(beta1_s[8 + 2 * p], beta1_s[9 + 2 * p], 2)
        alpha_two = 0.125 * restrict_pair(alpha1_s[8 + 2 * p], alpha1_s[9 + 2 * p], 2)
        tile = jnp.where(lane % 4 == 0, b_two, jnp.where(lane % 4 == 1, beta_two, alpha_two))
        for block in range(GX * GZ):
            gather[block, p] = tile[0]


def shape_of(*dims):
    return jax.ShapeDtypeStruct(dims + TILE, jnp.float32)


def scratch(*dims):
    return pltpu.VMEM(dims + TILE, jnp.float32)


def down(own, even, odd):
    out_shape = [
        shape_of(GX * GZ, 2), shape_of(28), shape_of(8, 4),
        shape_of(12, 4), shape_of(12, 4), shape_of(8, 4), shape_of(12, 4), shape_of(12, 4), shape_of(13, 4),
        shape_of(4, 2), shape_of(4, 2), shape_of(10, 2), shape_of(10, 2), shape_of(10, 2), shape_of(11, 2),
    ]
    vmem = pl.BlockSpec(memory_space=pltpu.VMEM)
    return pl.pallas_call(
        down_kernel,
        out_shape=out_shape,
        in_specs=[vmem] * 3,
        out_specs=[vmem] * len(out_shape),
        scratch_shapes=[
            scratch(24, 4), scratch(24, 4), scratch(12, 4), scratch(12, 4), scratch(12, 4), scratch(12, 4), scratch(12, 4),
            scratch(25, 4), scratch(25, 4), scratch(24, 4),
            scratch(12, 2), scratch(12, 2), scratch(8, 2), scratch(13, 2), scratch(13, 2), scratch(12, 2),
        ],
        compiler_params=pltpu.CompilerParams(vmem_limit_bytes=32 * 2**20),
        name="down_strokes",
    )(own, even, odd)


def outer(value, half):
    before = jnp.concatenate([lanes(value[-1:], 1), value[:-1]], axis=0)
    after = jnp.concatenate([value[1:], lanes(value[:1], -1)], axis=0)
    return jnp.where(half == 0, before, after)


def coarse_kernel(
    mine, other, rim_even, rim_odd, u0, b0, dinv0, diag0, cx0, cy0, cz0, u1, b1, dinv1, cx1, cy1, cz1,
    out, cores, e2_s, v_a, v_b, d_s, w_a, w_b, e_s, bx_s, uz_s, got,
):
    lane, row = lane_ids(), row_ids()
    half = lane // 64
    x, y, z = position()
    cores[y] = mine[...]
    cores[1 - y] = other[...]

    def collect(f):
        planes = []
        for p in range(2):
            tiles = []
            for group in range(8):
                tile = None
                for q in range(GZ):
                    natural = 7 - group if q % 2 else group
                    rank, core = natural // 2, natural % 2
                    piece = lanes(cores[core, (rank ^ (rank >> 1)) * GZ + q, p], q - f)
                    tile = piece if tile is None else jnp.where(lane % 4 == q, piece, tile)
                tiles.append(tile)
            planes.append(jnp.stack(tiles))
        return planes

    b_two, beta_two, alpha_two = collect(0), collect(1), collect(2)
    slab = lax.broadcasted_iota(jnp.int32, (8,) + TILE, 0)
    end = ((slab == 0) & (lane % 4 == 0) & (half == 0)) | ((slab == 7) & (lane % 4 == 3) & (half == 1))

    def sides(beta, dx, dy):
        x_last, x_first = row >= 8 - dx, row < dx
        place = (lane % 64) // dy
        y_last, y_first = place == 64 // dy - 1, place == 0
        by_x = jnp.where(x_last, 0.0, 0.5 * (beta + rows(beta, -dx)))
        by_y = jnp.where(y_last, 0.0, 0.5 * (beta + lanes(beta, -dy)))
        rim = jnp.where(x_last | x_first, 0.5, 0.0) + jnp.where(y_last | y_first, 0.5, 0.0)
        return by_x, by_y, (by_x + rows(by_x, dx)) + (by_y + lanes(by_y, dy)) + beta * rim

    def flat(v, by_x, by_y, dx, dy):
        total = by_x * rows(v, -dx) + rows(by_x * v, dx)
        return total + (by_y * lanes(v, -dy) + lanes(by_y * v, dy))

    x0, y0, s0 = sides(beta_two[0], 1, 4)
    x1, y1, s1 = sides(beta_two[1], 1, 4)
    middle = 0.5 * (beta_two[0] + beta_two[1])
    inner = 0.5 * (beta_two[1] + lanes(beta_two[1], 64))
    edge = 0.5 * (beta_two[0] + jnp.where(end, 0.0, outer(lanes(beta_two[0], 64), half)))
    rim2 = jnp.where(end, 0.0, edge)
    shift = SHIFT_BASE * 16.0
    diag_a = shift * alpha_two[0] + s0 + (middle + edge)
    diag_b = shift * alpha_two[1] + s1 + (middle + inner)
    inv_a, inv_b = 1.0 / diag_a, 1.0 / diag_b

    def apply_two(va, vb):
        ta = flat(va, x0, y0, 1, 4) + (middle * vb + rim2 * outer(lanes(va, 64), half))
        tb = flat(vb, x1, y1, 1, 4) + (middle * va + inner * lanes(vb, 64))
        return ta, tb

    def sweeps_two(va, vb, da, db, factors):
        for carry, gain in factors:
            ta, tb = apply_two(va, vb)
            ta = (b_two[0] + ta) * inv_a - va
            tb = (b_two[1] + tb) * inv_b - vb
            if carry == 0.0:
                da, db = gain * ta, gain * tb
            else:
                da, db = carry * da + gain * ta, carry * db + gain * tb
            va, vb = va + da, vb + db
        return va, vb

    factors = chebyshev_factors(SWEEPS, SMOOTH_LOWER)
    da, db = factors[0][1] * (b_two[0] * inv_a), factors[0][1] * (b_two[1] * inv_b)
    ua, ub = sweeps_two(da, db, da, db, factors[1:])
    ta, tb = apply_two(ua, ub)

    def restrict_whole(first, second):
        total = first + second
        total = total + jnp.where(row % 2 == 0, rows(total, -1), rows(total, 1))
        return total + jnp.where((lane // 4) % 2 == 0, lanes(total, -4), lanes(total, 4))

    b_low = 0.5 * restrict_whole(b_two[0] + ta - diag_a * ua, b_two[1] + tb - diag_b * ub)
    beta_low = 0.125 * restrict_whole(beta_two[0], beta_two[1])
    alpha_low = 0.125 * restrict_whole(alpha_two[0], alpha_two[1])

    x_low, y_low, s_low = sides(beta_low, 2, 8)
    turned = lanes(beta_low, 64)
    inner_low = 0.5 * (beta_low + turned)
    edge_low = 0.5 * (beta_low + jnp.where(end, 0.0, outer(turned, half)))
    rim_low = jnp.where(end, 0.0, edge_low)
    diag_low = SHIFT_BASE * 64.0 * alpha_low + s_low + (inner_low + edge_low)
    inv_low = 1.0 / diag_low
    step = None
    v = None
    for carry, gain in chebyshev_factors(BOTTOM, BOTTOM_LOWER):
        if v is None:
            step = gain * (b_low * inv_low)
            v = step
            continue
        turned = lanes(v, 64)
        total = flat(v, x_low, y_low, 2, 8) + (inner_low * turned + rim_low * outer(turned, half))
        step = carry * step + gain * ((b_low + total) * inv_low - v)
        v = v + step
    va, vb = sweeps_two(ua + v, ub + v, None, None, factors)
    for group in range(8):
        e2_s[group, 0] = va[group]
        e2_s[group, 1] = vb[group]

    chunk = chunk_of(x, y, z)
    place = 8 * z + chunk

    def fetch(offset):
        index = jnp.clip(place + offset, 0, 8 * GZ - 1)
        out = []
        for p in range(2):
            tile = pltpu.roll(e2_s[index % 8, p], (128 - index // 8) % 128, 1)
            tile = jnp.where(lane % 4 == 0, tile, 0.0)
            tile = tile + lanes(tile, 1)
            out.append(tile + lanes(tile, 2))
        return out

    below, here, above = fetch(-1), fetch(0), fetch(1)
    first = half == 0
    e_two = [
        jnp.where(first, below[0], above[0]),
        jnp.where(first, below[1], above[1]),
        lanes(jnp.where(first, above[1], below[1]), 64),
        lanes(jnp.where(first, above[0], below[0]), 64),
        here[0],
        here[1],
    ]
    _, from_even = halo_masks()

    for p in range(1, 8):
        if p >= 4:
            k = 7 - p
            both = lanes(jnp.where(from_even, rim_odd[20 + 2 * k : 22 + 2 * k], rim_even[20 + 2 * k : 22 + 2 * k]), 64)
        else:
            both = jnp.where(from_even, rim_even[20 + 2 * p : 22 + 2 * p], rim_odd[20 + 2 * p : 22 + 2 * p])
        w_a[p] = jnp.where(lane % 2 == 0, both, lanes(both, 1)) + e_two[p // 2]
        if p >= 2:
            bx_s[p] = jnp.where(lane % 2 == 0, lanes(both, -1), both)
    for p in range(8, PLANES1):
        w_a[p] = u1[p - 8] + e_two[p // 2]
    w_a[PLANES1] = lanes(w_a[PLANES1 - 1], 64)
    b_one = Planes(b1, 8, bx_s)
    coeffs = (Planes(cx1, 2), Planes(cy1, 2), Planes(cz1, 2))
    w = smooth((w_a, w_b), e_s, b_one, Planes(dinv1, 2), coeffs, factors, 2, PLANES1, 2)

    for p in range(11, PLANES):
        if p >= 16:
            start = u0[p - 16]
        else:
            k = 4 * (15 - p)
            start = lanes(jnp.where(from_even, rim_odd[k : k + 4], rim_even[k : k + 4]), 64)
        e_one = w[p // 2]
        e_one = jnp.concatenate([e_one[:1], e_one[:1], e_one[1:], e_one[1:]], axis=0)
        v_a[p] = start + e_one
    v_a[PLANES] = lanes(v_a[PLANES - 1], 64)
    b = Planes(b0, 12)
    coeffs = (Planes(cx0, 12), Planes(cy0, 12), Planes(cz0, 12))
    v = smooth((v_a, v_b), d_s, b, Planes(dinv0, 12), coeffs, factors, 12, PLANES, 1)
    low = (lane // 32) % 2 == 0
    for k in range(4):
        for o in range(2):
            parts = []
            for pp in range(2):
                p = 16 + k + 4 * pp
                value = v[p] if o == 0 else (b[p] + couple(v, p, *coeffs, 1)) - diag0[p - 16] * v[p]
                parts.append(regroup([value[i] for i in range(4)], 0, 2, row))
            for i in range(GX):
                one, two = parts[0][i], parts[1][i]
                out[2 * i, pl.ds(o * 32 + k * 8, 8), :] = jnp.where(low, one, lanes(two, 32))
                out[2 * i + 1, pl.ds(o * 32 + k * 8, 8), :] = jnp.where(low, lanes(one, -32), two)


def coarse_and_up(mine, other, rim_even, rim_odd, kept):
    vmem = pl.BlockSpec(memory_space=pltpu.VMEM)
    operands = (mine, other, rim_even, rim_odd, *kept)
    return pl.pallas_call(
        coarse_kernel,
        out_shape=jax.ShapeDtypeStruct((8, 64, 128), jnp.float32),
        in_specs=[vmem] * len(operands),
        out_specs=vmem,
        scratch_shapes=[
            scratch(2, GX * GZ, 2), scratch(8, 2), scratch(25, 4), scratch(25, 4), scratch(24, 4),
            scratch(13, 2), scratch(13, 2), scratch(12, 2), scratch(8, 2), scratch(1), scratch(1),
        ],
        compiler_params=pltpu.CompilerParams(vmem_limit_bytes=32 * 2**20),
        name="coarse_and_up",
    )(*operands)


def unpack_kernel(in_ref, v_ref, r_ref, turned, staged):
    z = lax.axis_index("gz")
    lane = lane_ids()
    for x in range(GX):
        for y in range(GY):
            start = pl.multiple_of(chunk_of(x, y, z) * 64, 64)
            staged[pl.ds(start, 64), :] = in_ref[x * GY + y]
    for o, ref in enumerate((v_ref, r_ref)):
        for xg in range(2):
            slot = turned.at[2 * o + xg]
            for k in range(4):
                tiles = [staged[pl.ds(o * 32 + k * 8 + 2 * x4 + xg, 8, stride=64), :] for x4 in range(4)]
                for g, tile in enumerate(regroup(tiles, 1, 32, lane)):
                    slot[pl.ds(depth_of(k, g), 8, stride=16), :] = tile
            ref[4 * xg : 4 * xg + 4] = slot[...].T.reshape(4, 32, 128)


def unpack(received):
    vmem = pl.BlockSpec(memory_space=pltpu.VMEM)
    return pl.pallas_call(
        unpack_kernel,
        out_shape=[jax.ShapeDtypeStruct(BLOCK, jnp.float32)] * 2,
        in_specs=[vmem],
        out_specs=[vmem] * 2,
        scratch_shapes=[pltpu.VMEM((4, 128, 128), jnp.float32), pltpu.VMEM((512, 128), jnp.float32)],
        name="unpack",
    )(received)


def slab_shards(right_side, alpha_coef, beta_coef):
    even_pairs, odd_pairs = swap_pairs(False), swap_pairs(True)
    packed = pack(right_side, alpha_coef, beta_coef)
    own = to_slab(lax.all_to_all(packed, RING, 0, 0))
    even = lax.ppermute(own, ALL, even_pairs)
    odd = lax.ppermute(own, ALL, odd_pairs)
    gather, rim, *kept = down(own, even, odd)
    rim_even = lax.ppermute(rim, ALL, even_pairs)
    rim_odd = lax.ppermute(rim, ALL, odd_pairs)
    mine = lax.all_to_all(gather, ("gx", "gz"), 0, 0)
    other = lax.ppermute(mine, "gy", [(0, 1), (1, 0)])
    result = coarse_and_up(mine, other, rim_even, rim_odd, kept)
    return tuple(unpack(lax.all_to_all(result, RING, 0, 0)))


def solution(mesh):
    spec = P("gx", "gy", "gz")
    plain = jax.shard_map(shards, mesh=mesh, in_specs=(spec,) * 3, out_specs=(spec,) * 2, check_vma=False)
    slabs = jax.shard_map(slab_shards, mesh=mesh, in_specs=(spec,) * 3, out_specs=(spec,) * 2, check_vma=False)
    sizes = tuple(mesh.shape[axis] for axis in ALL)

    def run(right_side, alpha_coef, beta_coef):
        block = tuple(n // size for n, size in zip(right_side.shape, sizes))
        fits = sizes == (GX, GY, GZ) and block == BLOCK
        return (slabs if fits else plain)(right_side, alpha_coef, beta_coef)

    return run
```

```python
import jax
import jax.numpy as jnp
from jax import lax
from jax.experimental import pallas as pl
from jax.experimental.pallas import tpu as pltpu
from jax.sharding import PartitionSpec as P

LEVELS = 3
SWEEPS = 4
BOTTOM = 12


SHIFT_BASE = 0.01
UPPER_EIG = 2.0
SMOOTH_LOWER = 0.25
BOTTOM_LOWER = 0.02


def with_halo(block, sides, width):
    for axis, dim in sides:
        count = lax.axis_size(axis)
        forward = [(i, i + 1) for i in range(count - 1)]
        backward = [(target, source) for source, target in forward]
        low = lax.ppermute(
            lax.slice_in_dim(block, block.shape[dim] - width, None, axis=dim), axis, forward
        )
        high = lax.ppermute(lax.slice_in_dim(block, 0, width, axis=dim), axis, backward)
        block = jnp.concatenate([low, block, high], axis=dim)
    return block


def partner_2(array, axis, distance):
    return lax.ppermute(array, axis, [(i, i ^ 1 << distance) for i in range(lax.axis_size(axis))])


def split_padded(padded):
    return (
        padded[:-2, 1:-1, 1:-1],
        padded[2:, 1:-1, 1:-1],
        padded[1:-1, :-2, 1:-1],
        padded[1:-1, 2:, 1:-1],
        padded[1:-1, 1:-1, :-2],
        padded[1:-1, 1:-1, 2:],
    )


def zero_pad(field):
    return jnp.pad(field, 1)


def rim_iterate(field):
    return with_halo(field, (("gx", 0), ("gy", 1), ("gz", 2)), 1)


def rim_coefficient(field):
    return with_halo(field, (("gx", 0), ("gy", 1), ("gz", 2)), 1)


def level_operator(beta_level, alpha_level, padded_beta, shift):
    coeffs = tuple((0.5 * (beta_level + other) for other in split_padded(padded_beta)))
    diagonal = shift * alpha_level
    for coeff in coeffs:
        diagonal = diagonal + coeff
    return (coeffs, diagonal)


def apply_operator(field, operator, pad_field):
    coeffs, diagonal = operator
    others = split_padded(pad_field(field))
    total = coeffs[0] * others[0]
    for index in range(1, 6):
        total = total + coeffs[index] * others[index]
    return diagonal * field - total


def chebyshev(iterate, rhs_level, operator, count, lower, zero_start, pad_field):
    diagonal = operator[1]
    center = (UPPER_EIG + lower) / 2.0
    half_width = (UPPER_EIG - lower) / 2.0
    sigma_ratio = center / half_width
    rho_old = 1.0 / sigma_ratio
    if zero_start:
        remain = rhs_level
    else:
        remain = rhs_level - apply_operator(iterate, operator, pad_field)
    update = remain / diagonal / center
    iterate = iterate + update
    for sweep_index in range(count - 1):
        remain = rhs_level - apply_operator(iterate, operator, pad_field)
        rho_new = 1.0 / (2.0 * sigma_ratio - rho_old)
        update = rho_new * rho_old * update + 2.0 * rho_new / half_width * (remain / diagonal)
        iterate = iterate + update
        rho_old = rho_new
    return iterate


def restrict_mean(field):
    first, second, third = field.shape
    blocks = field.reshape(first // 2, 2, second // 2, 2, third // 2, 2)
    return jnp.sum(blocks, axis=(1, 3, 5)) * 0.125


def prolong_copy(field):
    return jnp.repeat(jnp.repeat(jnp.repeat(field, 2, axis=0), 2, axis=1), 2, axis=2)


def join_partner(packed, partner, device_index, bit_index, dim):
    position = device_index // 2**bit_index % 2
    lower_first = jnp.concatenate([packed, partner], axis=dim)
    upper_first = jnp.concatenate([partner, packed], axis=dim)
    return jnp.where(position == 0, lower_first, upper_first)


def shards(right_side, alpha_coef, beta_coef):
    betas = [beta_coef]
    alphas = [alpha_coef]
    for level in range(LEVELS):
        betas.append(restrict_mean(betas[-1]))
        alphas.append(restrict_mean(alphas[-1]))
    operators = []
    for level in range(LEVELS):
        padded_beta = rim_coefficient(betas[level])
        operators.append(
            level_operator(betas[level], alphas[level], padded_beta, SHIFT_BASE * 4.0**level)
        )
    rhs_levels = [right_side]
    smoothed = []
    for level in range(LEVELS):
        iterate = chebyshev(
            jnp.zeros_like(rhs_levels[level]),
            rhs_levels[level],
            operators[level],
            SWEEPS,
            SMOOTH_LOWER,
            True,
            rim_iterate,
        )
        remain = rhs_levels[level] - apply_operator(iterate, operators[level], rim_iterate)
        smoothed.append(iterate)
        rhs_levels.append(4.0 * restrict_mean(remain))
    coarse_rhs = rhs_levels[LEVELS]
    local_shape = coarse_rhs.shape
    packed = jnp.stack([coarse_rhs, betas[LEVELS], alphas[LEVELS]])
    index_x = lax.axis_index("gx")
    index_y = lax.axis_index("gy")
    index_z = lax.axis_index("gz")
    for bit_index in range(lax.axis_size("gx").bit_length() - 1):
        partner = partner_2(packed, "gx", bit_index)
        packed = join_partner(packed, partner, index_x, bit_index, 1)
    for bit_index in range(lax.axis_size("gy").bit_length() - 1):
        partner = partner_2(packed, "gy", bit_index)
        packed = join_partner(packed, partner, index_y, bit_index, 2)
    for bit_index in range(lax.axis_size("gz").bit_length() - 1):
        partner = partner_2(packed, "gz", bit_index)
        packed = join_partner(packed, partner, index_z, bit_index, 3)
    whole_rhs = packed[0]
    whole_beta = packed[1]
    whole_alpha = packed[2]
    bottom_operator = level_operator(
        whole_beta, whole_alpha, zero_pad(whole_beta), SHIFT_BASE * 4.0**LEVELS
    )
    whole_correction = chebyshev(
        jnp.zeros_like(whole_rhs), whole_rhs, bottom_operator, BOTTOM, BOTTOM_LOWER, True, zero_pad
    )
    starts = (index_x * local_shape[0], index_y * local_shape[1], index_z * local_shape[2])
    correction = lax.dynamic_slice(whole_correction, starts, local_shape)
    for level in range(LEVELS - 1, -1, -1):
        start_field = smoothed[level] + prolong_copy(correction)
        correction = chebyshev(
            start_field,
            rhs_levels[level],
            operators[level],
            SWEEPS,
            SMOOTH_LOWER,
            False,
            rim_iterate,
        )
    residual_field = right_side - apply_operator(correction, operators[0], rim_iterate)
    return (correction, residual_field)


GX, GY, GZ = 4, 2, 4
BLOCK = (8, 32, 128)
RING = ("gx", "gy")
ALL = ("gx", "gy", "gz")
TILE = (8, 128)
PLANES = 24
PLANES1 = 12


def chunk_of(x, y, z):
    natural = 2 * (x ^ (x >> 1)) + y
    return natural + (z % 2) * (7 - 2 * natural)


def position():
    return lax.axis_index("gx"), lax.axis_index("gy"), lax.axis_index("gz")


def swap_pairs(odd):
    place = {}
    for x in range(GX):
        for y in range(GY):
            for z in range(GZ):
                place[8 * z + chunk_of(x, y, z)] = (x * GY + y) * GZ + z
    count = len(place)
    if odd:
        pairs = [(i, i + 1) for i in range(1, count - 1, 2)]
    else:
        pairs = [(i, i + 1) for i in range(0, count, 2)]
    return [(place[a], place[b]) for a, b in pairs] + [(place[b], place[a]) for a, b in pairs]


def lane_ids():
    return lax.broadcasted_iota(jnp.int32, TILE, 1)


def row_ids():
    return lax.broadcasted_iota(jnp.int32, TILE, 0)


def lanes(value, shift):
    return pltpu.roll(value, shift % 128, value.ndim - 1)


def rows(value, shift):
    return pltpu.roll(value, shift % 8, value.ndim - 2)


def regroup(tiles, axis, width, ids):
    move = lanes if axis == 1 else rows
    low = (ids // width) % 2 == 0
    high = (ids // (2 * width)) % 2 == 0
    a, b, c, d = tiles
    a, b = jnp.where(low, a, move(b, width)), jnp.where(low, move(a, -width), b)
    c, d = jnp.where(low, c, move(d, width)), jnp.where(low, move(c, -width), d)
    a, c = jnp.where(high, a, move(c, 2 * width)), jnp.where(high, move(a, -2 * width), c)
    b, d = jnp.where(high, b, move(d, 2 * width)), jnp.where(high, move(b, -2 * width), d)
    return [a, b, c, d]


def depth_of(k, group):
    half, part = group // 2, group % 2
    plane = k + 4 * part
    return 15 - plane if half else plane


def pack_kernel(fields, out_ref, turned, staged):
    z = lax.axis_index("gz")
    lane = lane_ids()
    for a in range(3):
        for xg in range(2):
            slot = turned.at[2 * a + xg]
            slot[...] = fields[a, 4 * xg : 4 * xg + 4].reshape(128, 128).T
            for k in range(4):
                tiles = [slot[pl.ds(depth_of(k, g), 8, stride=16), :] for g in range(4)]
                for x4, tile in enumerate(regroup(tiles, 1, 32, lane)):
                    staged[pl.ds(a * 32 + k * 8 + 2 * x4 + xg, 8, stride=96), :] = tile
    for x in range(GX):
        for y in range(GY):
            start = pl.multiple_of(chunk_of(x, y, z) * 96, 96)
            out_ref[x * GY + y] = staged[pl.ds(start, 96), :]


def pack(fields):
    return pl.pallas_call(
        pack_kernel,
        out_shape=jax.ShapeDtypeStruct((8, 96, 128), jnp.float32),
        in_specs=[pl.BlockSpec(memory_space=pltpu.VMEM)],
        out_specs=pl.BlockSpec(memory_space=pltpu.VMEM),
        scratch_shapes=[pltpu.VMEM((6, 128, 128), jnp.float32), pltpu.VMEM((768, 128), jnp.float32)],
        compiler_params=pltpu.CompilerParams(vmem_limit_bytes=4 * 2**20),
        name="pack",
    )(fields)


def slab_kernel(in_ref, out_ref):
    lane, row = lane_ids(), row_ids()
    low = (lane // 32) % 2 == 0
    for a in range(3):
        for k in range(4):
            part = ([], [])
            for x in range(GX):
                first = in_ref[2 * x, pl.ds(a * 32 + k * 8, 8), :]
                second = in_ref[2 * x + 1, pl.ds(a * 32 + k * 8, 8), :]
                part[0].append(jnp.where(low, first, lanes(second, 32)))
                part[1].append(jnp.where(low, lanes(first, -32), second))
            for pp in range(2):
                for xv, tile in enumerate(regroup(part[pp], 0, 2, row)):
                    out_ref[a, k + 4 * pp, xv] = tile


def to_slab(received):
    return pl.pallas_call(
        slab_kernel,
        out_shape=jax.ShapeDtypeStruct((3, 8, 4) + TILE, jnp.float32),
        in_specs=[pl.BlockSpec(memory_space=pltpu.VMEM)],
        out_specs=pl.BlockSpec(memory_space=pltpu.VMEM),
        compiler_params=pltpu.CompilerParams(vmem_limit_bytes=4 * 2**20),
        name="to_slab",
    )(received)


class Planes:
    def __init__(self, upper, cut, lower=None, base=0):
        self.upper, self.cut, self.lower, self.base = upper, cut, lower, base

    def __getitem__(self, p):
        return self.upper[p - self.cut] if p >= self.cut else self.lower[p - self.base]

    def __setitem__(self, p, value):
        if p >= self.cut:
            self.upper[p - self.cut] = value
        else:
            self.lower[p - self.base] = value


def x_up(value):
    return jnp.concatenate([value[1:], rows(value[:1], -1)], axis=0)


def x_down(value):
    return jnp.concatenate([rows(value[-1:], 1), value[:-1]], axis=0)


def couple(v, p, cx, cy, cz, dup):
    here, by_x, by_y = v[p], cx[p], cy[p]
    total = by_x * x_up(here) + x_down(by_x * here)
    total = total + (by_y * lanes(here, -dup) + lanes(by_y * here, dup))
    return total + (cz[p] * v[p - 1] + cz[p + 1] * v[p + 1])


def chebyshev_factors(count, lower):
    center = (UPPER_EIG + lower) / 2.0
    half_width = (UPPER_EIG - lower) / 2.0
    ratio = center / half_width
    old = 1.0 / ratio
    out = [(0.0, 1.0 / center)]
    for _ in range(count - 1):
        new = 1.0 / (2.0 * ratio - old)
        out.append((new * old, 2.0 * new / half_width))
        old = new
    return out


def smooth(v_pair, d, b, dinv, coeffs, factors, first, last, dup):
    old, new = v_pair
    for number, (carry, gain) in enumerate(factors):
        for p in range(first + number, last):
            t = (b[p] + couple(old, p, *coeffs, dup)) * dinv[p] - old[p]
            step = gain * t if carry == 0.0 else carry * d[p] + gain * t
            if number + 1 < len(factors):
                d[p] = step
            new[p] = old[p] + step
        new[last] = lanes(new[last - 1], 64)
        old, new = new, old
    return old


def level_coefficients(beta, alpha, first, last, shift, dup, cx, cy, cz, dinv, diag, ends, seam):
    lane, row = lane_ids(), row_ids()
    groups = beta[first].shape[0]
    y_last = (lane % 64) // dup == 64 // dup - 1
    y_first = (lane % 64) // dup == 0
    y_rim = jnp.where(y_last | y_first, 0.5, 0.0)
    rim = [y_rim] * groups
    rim[0] = rim[0] + jnp.where(row == 0, 0.5, 0.0)
    rim[-1] = rim[-1] + jnp.where(row == 7, 0.5, 0.0)
    rim = jnp.stack(rim)
    face = 0.5 * (beta[first - 1] + beta[first])
    for p in range(first, last):
        here = beta[p]
        by_x = 0.5 * (here + x_up(here))
        by_x = jnp.concatenate([by_x[:-1], jnp.where(row == 7, 0.0, by_x[-1:])], axis=0)
        by_y = jnp.where(y_last, 0.0, 0.5 * (here + lanes(here, -dup)))
        after = beta[p + 1] if p + 1 < last else lanes(here, 64)
        next_face = 0.5 * (here + after)
        total = shift * alpha[p] + by_x + x_down(by_x)
        total = total + (by_y + lanes(by_y, dup)) + here * rim + (face + next_face)
        cx[p], cy[p] = by_x, by_y
        cz[p] = face * ends if p == seam else face
        if diag is not None and p >= seam:
            diag[p] = total
        dinv[p] = 1.0 / jnp.where(total > 0.0, total, 1.0)
        face = next_face
    cz[last] = face


def restrict_pair(first, second, dup):
    lane = lane_ids()
    total = first + second
    groups = total.shape[0]
    total = jnp.concatenate([total[i : i + 1] + total[i + 1 : i + 2] for i in range(0, groups, 2)], axis=0)
    return total + jnp.where((lane // dup) % 2 == 0, lanes(total, -dup), lanes(total, dup))


def halo_masks():
    x, y, z = position()
    chunk = chunk_of(x, y, z)
    half = lane_ids() // 64
    return chunk, (half + chunk % 2) == 1


def ends_factor():
    x, y, z = position()
    slab = 8 * z + chunk_of(x, y, z)
    half = lane_ids() // 64
    end = ((half == 0) & (slab == 0)) | ((half == 1) & (slab == 8 * GZ - 1))
    return jnp.where(end, 0.0, 1.0)


def down_kernel(
    own, even, odd,
    gather, rim, u0, b0, dinv0, diag0, cx0, cy0, cz0, u1, b1, dinv1, cx1, cy1, cz1,
    beta_s, alpha_s, b_s, dinv_s, cx_s, cy_s, cz_s, v_a, v_b, d_s,
    beta1_s, alpha1_s, b1_s, w_a, w_b, e_s,
):
    lane = lane_ids()
    _, from_even = halo_masks()
    ends = ends_factor()

    def field(a, p):
        if p >= 16:
            return own[a, p - 16]
        if p >= 8:
            return lanes(jnp.where(from_even, odd[a, 15 - p], even[a, 15 - p]), 64)
        return jnp.where(from_even, even[a, p], odd[a, p])

    for p in range(PLANES):
        beta_s[p] = field(2, p)
        alpha_s[p] = field(1, p)
    b = Planes(b0, 12, b_s)
    for p in range(4, PLANES):
        b[p] = field(0, p)
    cx, cy, cz = Planes(cx0, 12, cx_s), Planes(cy0, 12, cy_s), Planes(cz0, 12, cz_s)
    dinv = Planes(dinv0, 12, dinv_s)
    diag = Planes(diag0, 16)
    level_coefficients(beta_s, alpha_s, 4, PLANES, SHIFT_BASE, 1, cx, cy, cz, dinv, diag, ends, 16)
    diag_all = lambda p: diag[p]

    factors = chebyshev_factors(SWEEPS, SMOOTH_LOWER)
    for p in range(4, PLANES):
        start = factors[0][1] * (b[p] * dinv[p])
        v_a[p] = start
        d_s[p] = start
    v_a[PLANES] = lanes(v_a[PLANES - 1], 64)
    v = smooth((v_a, v_b), d_s, b, dinv, (cx, cy, cz), factors[1:], 5, PLANES, 1)
    for p in range(8):
        u0[p] = v[16 + p]

    def residual(v, p, b, dinv, coeffs, dup):
        return ((b[p] + couple(v, p, *coeffs, dup)) * dinv[p] - v[p]) / dinv[p]

    b_one = Planes(b1, 8, b1_s)
    for p in range(4, PLANES1):
        pair = [residual(v, 2 * p + i, b, dinv, (cx, cy, cz), 1) for i in range(2)]
        b_one[p] = 0.5 * restrict_pair(*pair, 1)
    for p in range(PLANES1):
        beta1_s[p] = 0.125 * restrict_pair(beta_s[2 * p], beta_s[2 * p + 1], 1)
        alpha1_s[p] = 0.125 * restrict_pair(alpha_s[2 * p], alpha_s[2 * p + 1], 1)
    cx, cy, cz, dinv = Planes(cx1, 2), Planes(cy1, 2), Planes(cz1, 2), Planes(dinv1, 2)
    level_coefficients(beta1_s, alpha1_s, 2, PLANES1, SHIFT_BASE * 4.0, 2, cx, cy, cz, dinv, None, ends, 8)
    for p in range(4, PLANES1):
        start = factors[0][1] * (b_one[p] * dinv[p])
        w_a[p] = start
        e_s[p] = start
    w_a[PLANES1] = lanes(w_a[PLANES1 - 1], 64)
    w = smooth((w_a, w_b), e_s, b_one, dinv, (cx, cy, cz), factors[1:], 5, PLANES1, 2)
    for p in range(4):
        u1[p] = w[8 + p]
        rim[20 + 2 * p : 22 + 2 * p] = jnp.where(lane % 2 == 0, w[8 + p], b_one[8 + p])
    for p in range(5):
        rim[4 * p : 4 * p + 4] = u0[p]
    for p in range(2):
        pair = [residual(w, 8 + 2 * p + i, b_one, dinv, (cx, cy, cz), 2) for i in range(2)]
        b_two = 0.5 * restrict_pair(*pair, 2)
        beta_two = 0.125 * restrict_pair(beta1_s[8 + 2 * p], beta1_s[9 + 2 * p], 2)
        alpha_two = 0.125 * restrict_pair(alpha1_s[8 + 2 * p], alpha1_s[9 + 2 * p], 2)
        tile = jnp.where(lane % 4 == 0, b_two, jnp.where(lane % 4 == 1, beta_two, alpha_two))
        for block in range(GX * GZ):
            gather[block, p] = tile[0]


def shape_of(*dims):
    return jax.ShapeDtypeStruct(dims + TILE, jnp.float32)


def scratch(*dims):
    return pltpu.VMEM(dims + TILE, jnp.float32)


def down(own, even, odd):
    out_shape = [
        shape_of(GX * GZ, 2), shape_of(36), shape_of(8, 4),
        shape_of(12, 4), shape_of(12, 4), shape_of(8, 4), shape_of(12, 4), shape_of(12, 4), shape_of(13, 4),
        shape_of(4, 2), shape_of(4, 2), shape_of(10, 2), shape_of(10, 2), shape_of(10, 2), shape_of(11, 2),
    ]
    vmem = pl.BlockSpec(memory_space=pltpu.VMEM)
    return pl.pallas_call(
        down_kernel,
        out_shape=out_shape,
        in_specs=[vmem] * 3,
        out_specs=[vmem] * len(out_shape),
        scratch_shapes=[
            scratch(24, 4), scratch(24, 4), scratch(12, 4), scratch(12, 4), scratch(12, 4), scratch(12, 4), scratch(12, 4),
            scratch(25, 4), scratch(25, 4), scratch(24, 4),
            scratch(12, 2), scratch(12, 2), scratch(8, 2), scratch(13, 2), scratch(13, 2), scratch(12, 2),
        ],
        compiler_params=pltpu.CompilerParams(vmem_limit_bytes=16 * 2**20),
        name="down_strokes",
    )(own, even, odd)


def outer(value, half):
    before = jnp.concatenate([lanes(value[-1:], 1), value[:-1]], axis=0)
    after = jnp.concatenate([value[1:], lanes(value[:1], -1)], axis=0)
    return jnp.where(half == 0, before, after)


def coarse_kernel(
    mine, other, rim_even, rim_odd, u0, b0, dinv0, diag0, cx0, cy0, cz0, u1, b1, dinv1, cx1, cy1, cz1,
    out, cores, e2_s, v_a, v_b, d_s, w_a, w_b, e_s, bx_s, uz_s, got,
):
    lane, row = lane_ids(), row_ids()
    half = lane // 64
    x, y, z = position()
    cores[y] = mine[...]
    cores[1 - y] = other[...]

    def collect(f):
        planes = []
        for p in range(2):
            tiles = []
            for group in range(8):
                tile = None
                for q in range(GZ):
                    natural = 7 - group if q % 2 else group
                    rank, core = natural // 2, natural % 2
                    piece = lanes(cores[core, (rank ^ (rank >> 1)) * GZ + q, p], q - f)
                    tile = piece if tile is None else jnp.where(lane % 4 == q, piece, tile)
                tiles.append(tile)
            planes.append(jnp.stack(tiles))
        return planes

    b_two, beta_two, alpha_two = collect(0), collect(1), collect(2)
    slab = lax.broadcasted_iota(jnp.int32, (8,) + TILE, 0)
    end = ((slab == 0) & (lane % 4 == 0) & (half == 0)) | ((slab == 7) & (lane % 4 == 3) & (half == 1))

    def sides(beta, dx, dy):
        x_last, x_first = row >= 8 - dx, row < dx
        place = (lane % 64) // dy
        y_last, y_first = place == 64 // dy - 1, place == 0
        by_x = jnp.where(x_last, 0.0, 0.5 * (beta + rows(beta, -dx)))
        by_y = jnp.where(y_last, 0.0, 0.5 * (beta + lanes(beta, -dy)))
        rim = jnp.where(x_last | x_first, 0.5, 0.0) + jnp.where(y_last | y_first, 0.5, 0.0)
        return by_x, by_y, (by_x + rows(by_x, dx)) + (by_y + lanes(by_y, dy)) + beta * rim

    def flat(v, by_x, by_y, dx, dy):
        total = by_x * rows(v, -dx) + rows(by_x * v, dx)
        return total + (by_y * lanes(v, -dy) + lanes(by_y * v, dy))

    x0, y0, s0 = sides(beta_two[0], 1, 4)
    x1, y1, s1 = sides(beta_two[1], 1, 4)
    middle = 0.5 * (beta_two[0] + beta_two[1])
    inner = 0.5 * (beta_two[1] + lanes(beta_two[1], 64))
    edge = 0.5 * (beta_two[0] + jnp.where(end, 0.0, outer(lanes(beta_two[0], 64), half)))
    rim2 = jnp.where(end, 0.0, edge)
    shift = SHIFT_BASE * 16.0
    diag_a = shift * alpha_two[0] + s0 + (middle + edge)
    diag_b = shift * alpha_two[1] + s1 + (middle + inner)
    inv_a, inv_b = 1.0 / diag_a, 1.0 / diag_b

    def apply_two(va, vb):
        ta = flat(va, x0, y0, 1, 4) + (middle * vb + rim2 * outer(lanes(va, 64), half))
        tb = flat(vb, x1, y1, 1, 4) + (middle * va + inner * lanes(vb, 64))
        return ta, tb

    def sweeps_two(va, vb, da, db, factors):
        for carry, gain in factors:
            ta, tb = apply_two(va, vb)
            ta = (b_two[0] + ta) * inv_a - va
            tb = (b_two[1] + tb) * inv_b - vb
            if carry == 0.0:
                da, db = gain * ta, gain * tb
            else:
                da, db = carry * da + gain * ta, carry * db + gain * tb
            va, vb = va + da, vb + db
        return va, vb

    factors = chebyshev_factors(SWEEPS, SMOOTH_LOWER)
    da, db = factors[0][1] * (b_two[0] * inv_a), factors[0][1] * (b_two[1] * inv_b)
    ua, ub = sweeps_two(da, db, da, db, factors[1:])
    ta, tb = apply_two(ua, ub)

    def restrict_whole(first, second):
        total = first + second
        total = total + jnp.where(row % 2 == 0, rows(total, -1), rows(total, 1))
        return total + jnp.where((lane // 4) % 2 == 0, lanes(total, -4), lanes(total, 4))

    b_low = 0.5 * restrict_whole(b_two[0] + ta - diag_a * ua, b_two[1] + tb - diag_b * ub)
    beta_low = 0.125 * restrict_whole(beta_two[0], beta_two[1])
    alpha_low = 0.125 * restrict_whole(alpha_two[0], alpha_two[1])

    x_low, y_low, s_low = sides(beta_low, 2, 8)
    turned = lanes(beta_low, 64)
    inner_low = 0.5 * (beta_low + turned)
    edge_low = 0.5 * (beta_low + jnp.where(end, 0.0, outer(turned, half)))
    rim_low = jnp.where(end, 0.0, edge_low)
    diag_low = SHIFT_BASE * 64.0 * alpha_low + s_low + (inner_low + edge_low)
    inv_low = 1.0 / diag_low
    step = None
    v = None
    for carry, gain in chebyshev_factors(BOTTOM, BOTTOM_LOWER):
        if v is None:
            step = gain * (b_low * inv_low)
            v = step
            continue
        turned = lanes(v, 64)
        total = flat(v, x_low, y_low, 2, 8) + (inner_low * turned + rim_low * outer(turned, half))
        step = carry * step + gain * ((b_low + total) * inv_low - v)
        v = v + step
    va, vb = sweeps_two(ua + v, ub + v, None, None, factors)
    for group in range(8):
        e2_s[group, 0] = va[group]
        e2_s[group, 1] = vb[group]

    chunk = chunk_of(x, y, z)
    place = 8 * z + chunk

    def fetch(offset):
        index = jnp.clip(place + offset, 0, 8 * GZ - 1)
        out = []
        for p in range(2):
            tile = pltpu.roll(e2_s[index % 8, p], (128 - index // 8) % 128, 1)
            tile = jnp.where(lane % 4 == 0, tile, 0.0)
            tile = tile + lanes(tile, 1)
            out.append(tile + lanes(tile, 2))
        return out

    below, here, above = fetch(-1), fetch(0), fetch(1)
    first = half == 0
    e_two = [
        jnp.where(first, below[0], above[0]),
        jnp.where(first, below[1], above[1]),
        lanes(jnp.where(first, above[1], below[1]), 64),
        lanes(jnp.where(first, above[0], below[0]), 64),
        here[0],
        here[1],
    ]
    _, from_even = halo_masks()

    for p in range(1, 8):
        if p >= 4:
            k = 7 - p
            both = lanes(jnp.where(from_even, rim_odd[20 + 2 * k : 22 + 2 * k], rim_even[20 + 2 * k : 22 + 2 * k]), 64)
        else:
            both = jnp.where(from_even, rim_even[20 + 2 * p : 22 + 2 * p], rim_odd[20 + 2 * p : 22 + 2 * p])
        w_a[p] = jnp.where(lane % 2 == 0, both, lanes(both, 1)) + e_two[p // 2]
        if p >= 2:
            bx_s[p] = jnp.where(lane % 2 == 0, lanes(both, -1), both)
    for p in range(8, PLANES1):
        w_a[p] = u1[p - 8] + e_two[p // 2]
    w_a[PLANES1] = lanes(w_a[PLANES1 - 1], 64)
    b_one = Planes(b1, 8, bx_s)
    coeffs = (Planes(cx1, 2), Planes(cy1, 2), Planes(cz1, 2))
    w = smooth((w_a, w_b), e_s, b_one, Planes(dinv1, 2), coeffs, factors, 2, PLANES1, 2)

    for p in range(11, PLANES):
        if p >= 16:
            start = u0[p - 16]
        else:
            k = 4 * (15 - p)
            start = lanes(jnp.where(from_even, rim_odd[k : k + 4], rim_even[k : k + 4]), 64)
        e_one = w[p // 2]
        e_one = jnp.concatenate([e_one[:1], e_one[:1], e_one[1:], e_one[1:]], axis=0)
        v_a[p] = start + e_one
    v_a[PLANES] = lanes(v_a[PLANES - 1], 64)
    b = Planes(b0, 12)
    coeffs = (Planes(cx0, 12), Planes(cy0, 12), Planes(cz0, 12))
    v = smooth((v_a, v_b), d_s, b, Planes(dinv0, 12), coeffs, factors, 12, PLANES, 1)
    low = (lane // 32) % 2 == 0
    for k in range(4):
        for o in range(2):
            parts = []
            for pp in range(2):
                p = 16 + k + 4 * pp
                value = v[p] if o == 0 else (b[p] + couple(v, p, *coeffs, 1)) - diag0[p - 16] * v[p]
                parts.append(regroup([value[i] for i in range(4)], 0, 2, row))
            for i in range(GX):
                one, two = parts[0][i], parts[1][i]
                out[2 * i, pl.ds(o * 32 + k * 8, 8), :] = jnp.where(low, one, lanes(two, 32))
                out[2 * i + 1, pl.ds(o * 32 + k * 8, 8), :] = jnp.where(low, lanes(one, -32), two)


def coarse_and_up(mine, other, rim_even, rim_odd, kept):
    vmem = pl.BlockSpec(memory_space=pltpu.VMEM)
    operands = (mine, other, rim_even, rim_odd, *kept)
    return pl.pallas_call(
        coarse_kernel,
        out_shape=jax.ShapeDtypeStruct((8, 64, 128), jnp.float32),
        in_specs=[vmem] * len(operands),
        out_specs=vmem,
        scratch_shapes=[
            scratch(2, GX * GZ, 2), scratch(8, 2), scratch(25, 4), scratch(25, 4), scratch(24, 4),
            scratch(13, 2), scratch(13, 2), scratch(12, 2), scratch(8, 2), scratch(1), scratch(1),
        ],
        compiler_params=pltpu.CompilerParams(vmem_limit_bytes=16 * 2**20),
        name="coarse_and_up",
    )(*operands)


def unpack_kernel(in_ref, v_ref, r_ref, fields, turned, staged, left):
    z = lax.axis_index("gz")
    lane = lane_ids()
    for x in range(GX):
        for y in range(GY):
            start = pl.multiple_of(chunk_of(x, y, z) * 64, 64)
            staged[pl.ds(start, 64), :] = in_ref[x * GY + y]
    copies = [pltpu.make_async_copy(fields.at[o], ref, left.at[o]) for o, ref in enumerate((v_ref, r_ref))]
    for o, copy in enumerate(copies):
        for xg in range(2):
            slot = turned.at[2 * o + xg]
            for k in range(4):
                tiles = [staged[pl.ds(o * 32 + k * 8 + 2 * x4 + xg, 8, stride=64), :] for x4 in range(4)]
                for g, tile in enumerate(regroup(tiles, 1, 32, lane)):
                    slot[pl.ds(depth_of(k, g), 8, stride=16), :] = tile
            fields[o, 4 * xg : 4 * xg + 4] = slot[...].T.reshape(4, 32, 128)
        copy.start()
    for copy in copies:
        copy.wait()


def unpack(received):
    vmem = pl.BlockSpec(memory_space=pltpu.VMEM)
    return pl.pallas_call(
        unpack_kernel,
        out_shape=[jax.ShapeDtypeStruct(BLOCK, jnp.float32)] * 2,
        in_specs=[vmem],
        out_specs=[pl.BlockSpec(memory_space=pltpu.HBM)] * 2,
        scratch_shapes=[
            pltpu.VMEM((2,) + BLOCK, jnp.float32),
            pltpu.VMEM((4, 128, 128), jnp.float32),
            pltpu.VMEM((512, 128), jnp.float32),
            pltpu.SemaphoreType.DMA((2,)),
        ],
        compiler_params=pltpu.CompilerParams(vmem_limit_bytes=4 * 2**20),
        name="unpack",
    )(received)


def slab_shards(right_side, alpha_coef, beta_coef):
    even_pairs, odd_pairs = swap_pairs(False), swap_pairs(True)
    packed = pack(jnp.stack([right_side, alpha_coef, beta_coef]))
    own = to_slab(lax.all_to_all(packed, RING, 0, 0))
    even = lax.ppermute(own, ALL, even_pairs)
    odd = lax.ppermute(own, ALL, odd_pairs)
    gather, rim, *kept = down(own, even, odd)
    rim_even = lax.ppermute(rim, ALL, even_pairs)
    rim_odd = lax.ppermute(rim, ALL, odd_pairs)
    mine = lax.all_to_all(gather, ("gx", "gz"), 0, 0)
    other = lax.ppermute(mine, "gy", [(0, 1), (1, 0)])
    result = coarse_and_up(mine, other, rim_even, rim_odd, kept)
    return tuple(unpack(lax.all_to_all(result, RING, 0, 0)))


def solution(mesh):
    spec = P("gx", "gy", "gz")
    plain = jax.shard_map(shards, mesh=mesh, in_specs=(spec,) * 3, out_specs=(spec,) * 2, check_vma=False)
    slabs = jax.shard_map(slab_shards, mesh=mesh, in_specs=(spec,) * 3, out_specs=(spec,) * 2, check_vma=False)
    sizes = tuple(mesh.shape[axis] for axis in ALL)

    def run(right_side, alpha_coef, beta_coef):
        block = tuple(n // size for n, size in zip(right_side.shape, sizes))
        fits = sizes == (GX, GY, GZ) and block == BLOCK
        return (slabs if fits else plain)(right_side, alpha_coef, beta_coef)

    return run
```

```python
import jax
import jax.numpy as jnp
from jax import lax
from jax.experimental import pallas as pl
from jax.experimental.pallas import tpu as pltpu
from jax.sharding import PartitionSpec as P

LEVELS = 3
SWEEPS = 4
BOTTOM = 12


SHIFT_BASE = 0.01
UPPER_EIG = 2.0
SMOOTH_LOWER = 0.25
BOTTOM_LOWER = 0.02


def with_halo(block, sides, width):
    for axis, dim in sides:
        count = lax.axis_size(axis)
        forward = [(i, i + 1) for i in range(count - 1)]
        backward = [(target, source) for source, target in forward]
        low = lax.ppermute(
            lax.slice_in_dim(block, block.shape[dim] - width, None, axis=dim), axis, forward
        )
        high = lax.ppermute(lax.slice_in_dim(block, 0, width, axis=dim), axis, backward)
        block = jnp.concatenate([low, block, high], axis=dim)
    return block


def partner_2(array, axis, distance):
    return lax.ppermute(array, axis, [(i, i ^ 1 << distance) for i in range(lax.axis_size(axis))])


def split_padded(padded):
    return (
        padded[:-2, 1:-1, 1:-1],
        padded[2:, 1:-1, 1:-1],
        padded[1:-1, :-2, 1:-1],
        padded[1:-1, 2:, 1:-1],
        padded[1:-1, 1:-1, :-2],
        padded[1:-1, 1:-1, 2:],
    )


def zero_pad(field):
    return jnp.pad(field, 1)


def rim_iterate(field):
    return with_halo(field, (("gx", 0), ("gy", 1), ("gz", 2)), 1)


def rim_coefficient(field):
    return with_halo(field, (("gx", 0), ("gy", 1), ("gz", 2)), 1)


def level_operator(beta_level, alpha_level, padded_beta, shift):
    coeffs = tuple((0.5 * (beta_level + other) for other in split_padded(padded_beta)))
    diagonal = shift * alpha_level
    for coeff in coeffs:
        diagonal = diagonal + coeff
    return (coeffs, diagonal)


def apply_operator(field, operator, pad_field):
    coeffs, diagonal = operator
    others = split_padded(pad_field(field))
    total = coeffs[0] * others[0]
    for index in range(1, 6):
        total = total + coeffs[index] * others[index]
    return diagonal * field - total


def chebyshev(iterate, rhs_level, operator, count, lower, zero_start, pad_field):
    diagonal = operator[1]
    center = (UPPER_EIG + lower) / 2.0
    half_width = (UPPER_EIG - lower) / 2.0
    sigma_ratio = center / half_width
    rho_old = 1.0 / sigma_ratio
    if zero_start:
        remain = rhs_level
    else:
        remain = rhs_level - apply_operator(iterate, operator, pad_field)
    update = remain / diagonal / center
    iterate = iterate + update
    for sweep_index in range(count - 1):
        remain = rhs_level - apply_operator(iterate, operator, pad_field)
        rho_new = 1.0 / (2.0 * sigma_ratio - rho_old)
        update = rho_new * rho_old * update + 2.0 * rho_new / half_width * (remain / diagonal)
        iterate = iterate + update
        rho_old = rho_new
    return iterate


def restrict_mean(field):
    first, second, third = field.shape
    blocks = field.reshape(first // 2, 2, second // 2, 2, third // 2, 2)
    return jnp.sum(blocks, axis=(1, 3, 5)) * 0.125


def prolong_copy(field):
    return jnp.repeat(jnp.repeat(jnp.repeat(field, 2, axis=0), 2, axis=1), 2, axis=2)


def join_partner(packed, partner, device_index, bit_index, dim):
    position = device_index // 2**bit_index % 2
    lower_first = jnp.concatenate([packed, partner], axis=dim)
    upper_first = jnp.concatenate([partner, packed], axis=dim)
    return jnp.where(position == 0, lower_first, upper_first)


def shards(right_side, alpha_coef, beta_coef):
    betas = [beta_coef]
    alphas = [alpha_coef]
    for level in range(LEVELS):
        betas.append(restrict_mean(betas[-1]))
        alphas.append(restrict_mean(alphas[-1]))
    operators = []
    for level in range(LEVELS):
        padded_beta = rim_coefficient(betas[level])
        operators.append(
            level_operator(betas[level], alphas[level], padded_beta, SHIFT_BASE * 4.0**level)
        )
    rhs_levels = [right_side]
    smoothed = []
    for level in range(LEVELS):
        iterate = chebyshev(
            jnp.zeros_like(rhs_levels[level]),
            rhs_levels[level],
            operators[level],
            SWEEPS,
            SMOOTH_LOWER,
            True,
            rim_iterate,
        )
        remain = rhs_levels[level] - apply_operator(iterate, operators[level], rim_iterate)
        smoothed.append(iterate)
        rhs_levels.append(4.0 * restrict_mean(remain))
    coarse_rhs = rhs_levels[LEVELS]
    local_shape = coarse_rhs.shape
    packed = jnp.stack([coarse_rhs, betas[LEVELS], alphas[LEVELS]])
    index_x = lax.axis_index("gx")
    index_y = lax.axis_index("gy")
    index_z = lax.axis_index("gz")
    for bit_index in range(lax.axis_size("gx").bit_length() - 1):
        partner = partner_2(packed, "gx", bit_index)
        packed = join_partner(packed, partner, index_x, bit_index, 1)
    for bit_index in range(lax.axis_size("gy").bit_length() - 1):
        partner = partner_2(packed, "gy", bit_index)
        packed = join_partner(packed, partner, index_y, bit_index, 2)
    for bit_index in range(lax.axis_size("gz").bit_length() - 1):
        partner = partner_2(packed, "gz", bit_index)
        packed = join_partner(packed, partner, index_z, bit_index, 3)
    whole_rhs = packed[0]
    whole_beta = packed[1]
    whole_alpha = packed[2]
    bottom_operator = level_operator(
        whole_beta, whole_alpha, zero_pad(whole_beta), SHIFT_BASE * 4.0**LEVELS
    )
    whole_correction = chebyshev(
        jnp.zeros_like(whole_rhs), whole_rhs, bottom_operator, BOTTOM, BOTTOM_LOWER, True, zero_pad
    )
    starts = (index_x * local_shape[0], index_y * local_shape[1], index_z * local_shape[2])
    correction = lax.dynamic_slice(whole_correction, starts, local_shape)
    for level in range(LEVELS - 1, -1, -1):
        start_field = smoothed[level] + prolong_copy(correction)
        correction = chebyshev(
            start_field,
            rhs_levels[level],
            operators[level],
            SWEEPS,
            SMOOTH_LOWER,
            False,
            rim_iterate,
        )
    residual_field = right_side - apply_operator(correction, operators[0], rim_iterate)
    return (correction, residual_field)


GX, GY, GZ = 4, 2, 4
BLOCK = (8, 32, 128)
RING = ("gx", "gy")
ALL = ("gx", "gy", "gz")
TILE = (8, 128)
PLANES = 24
PLANES1 = 12
SPAN, SPAN1, COEF_SPAN, COEF_SPAN1 = 2, 4, 2, 4


def chunk_of(x, y, z):
    natural = 2 * (x ^ (x >> 1)) + y
    return natural + (z % 2) * (7 - 2 * natural)


def position():
    return lax.axis_index("gx"), lax.axis_index("gy"), lax.axis_index("gz")


def swap_pairs(odd):
    place = {}
    for x in range(GX):
        for y in range(GY):
            for z in range(GZ):
                place[8 * z + chunk_of(x, y, z)] = (x * GY + y) * GZ + z
    count = len(place)
    if odd:
        pairs = [(i, i + 1) for i in range(1, count - 1, 2)]
    else:
        pairs = [(i, i + 1) for i in range(0, count, 2)]
    return [(place[a], place[b]) for a, b in pairs] + [(place[b], place[a]) for a, b in pairs]


def lane_ids():
    return lax.broadcasted_iota(jnp.int32, TILE, 1)


def row_ids():
    return lax.broadcasted_iota(jnp.int32, TILE, 0)


def lanes(value, shift):
    return pltpu.roll(value, shift % 128, value.ndim - 1)


def rows(value, shift):
    return pltpu.roll(value, shift % 8, value.ndim - 2)


def regroup(tiles, axis, width, ids):
    move = lanes if axis == 1 else rows
    low = (ids // width) % 2 == 0
    high = (ids // (2 * width)) % 2 == 0
    a, b, c, d = tiles
    a, b = jnp.where(low, a, move(b, width)), jnp.where(low, move(a, -width), b)
    c, d = jnp.where(low, c, move(d, width)), jnp.where(low, move(c, -width), d)
    a, c = jnp.where(high, a, move(c, 2 * width)), jnp.where(high, move(a, -2 * width), c)
    b, d = jnp.where(high, b, move(d, 2 * width)), jnp.where(high, move(b, -2 * width), d)
    return [a, b, c, d]


def depth_of(k, group):
    half, part = group // 2, group % 2
    plane = k + 4 * part
    return 15 - plane if half else plane


def pack_kernel(fields, out_ref, turned, staged):
    z = lax.axis_index("gz")
    lane = lane_ids()
    for a in range(3):
        for xg in range(2):
            slot = turned.at[2 * a + xg]
            slot[...] = fields[a, 4 * xg : 4 * xg + 4].reshape(128, 128).T
            for k in range(4):
                tiles = [slot[pl.ds(depth_of(k, g), 8, stride=16), :] for g in range(4)]
                for x4, tile in enumerate(regroup(tiles, 1, 32, lane)):
                    staged[pl.ds(a * 32 + k * 8 + 2 * x4 + xg, 8, stride=96), :] = tile
    for x in range(GX):
        for y in range(GY):
            start = pl.multiple_of(chunk_of(x, y, z) * 96, 96)
            out_ref[x * GY + y] = staged[pl.ds(start, 96), :]


def pack(fields):
    return pl.pallas_call(
        pack_kernel,
        out_shape=jax.ShapeDtypeStruct((8, 96, 128), jnp.float32),
        in_specs=[pl.BlockSpec(memory_space=pltpu.VMEM)],
        out_specs=pl.BlockSpec(memory_space=pltpu.VMEM),
        scratch_shapes=[pltpu.VMEM((6, 128, 128), jnp.float32), pltpu.VMEM((768, 128), jnp.float32)],
        compiler_params=pltpu.CompilerParams(vmem_limit_bytes=4 * 2**20),
        name="pack",
    )(fields)


def slab_kernel(in_ref, out_ref):
    lane, row = lane_ids(), row_ids()
    low = (lane // 32) % 2 == 0
    for a in range(3):
        for k in range(4):
            part = ([], [])
            for x in range(GX):
                first = in_ref[2 * x, pl.ds(a * 32 + k * 8, 8), :]
                second = in_ref[2 * x + 1, pl.ds(a * 32 + k * 8, 8), :]
                part[0].append(jnp.where(low, first, lanes(second, 32)))
                part[1].append(jnp.where(low, lanes(first, -32), second))
            for pp in range(2):
                for xv, tile in enumerate(regroup(part[pp], 0, 2, row)):
                    out_ref[a, k + 4 * pp, xv] = tile


def to_slab(received):
    return pl.pallas_call(
        slab_kernel,
        out_shape=shape_of(3, 8, 4),
        in_specs=[pl.BlockSpec(memory_space=pltpu.VMEM)],
        out_specs=pl.BlockSpec(memory_space=pltpu.VMEM),
        compiler_params=pltpu.CompilerParams(vmem_limit_bytes=4 * 2**20),
        name="to_slab",
    )(received)


class Planes:
    def __init__(self, *segments):
        self.segments = [(first, first + ref.shape[0], ref) for first, ref in segments]

    def find(self, p, q):
        for first, last, ref in self.segments:
            low, high = max(p, first), min(q, last)
            if low < high:
                yield low, high, ref, slice(low - first, high - first)

    def get(self, p, q):
        pieces = [ref[place] for _, _, ref, place in self.find(p, q)]
        return pieces[0] if len(pieces) == 1 else jnp.concatenate(pieces, axis=0)

    def put(self, p, value):
        for low, high, ref, place in self.find(p, p + value.shape[0]):
            ref[place] = value[low - p : high - p]


def spans(first, last, size):
    return [(p, min(p + size, last)) for p in range(first, last, size)]


def x_up(value):
    return jnp.concatenate([value[:, 1:], rows(value[:, :1], -1)], axis=1)


def x_down(value):
    return jnp.concatenate([rows(value[:, -1:], 1), value[:, :-1]], axis=1)


def couple(v, p, q, cx, cy, cz, dup):
    here, by_x, by_y = v.get(p, q), cx.get(p, q), cy.get(p, q)
    total = by_x * x_up(here) + x_down(by_x * here)
    total = total + (by_y * lanes(here, -dup) + lanes(by_y * here, dup))
    return total + (cz.get(p, q) * v.get(p - 1, q - 1) + cz.get(p + 1, q + 1) * v.get(p + 1, q + 1))


def chebyshev_factors(count, lower):
    center = (UPPER_EIG + lower) / 2.0
    half_width = (UPPER_EIG - lower) / 2.0
    ratio = center / half_width
    old = 1.0 / ratio
    out = [(0.0, 1.0 / center)]
    for _ in range(count - 1):
        new = 1.0 / (2.0 * ratio - old)
        out.append((new * old, 2.0 * new / half_width))
        old = new
    return out


def sweep(new, now, before, factor, b, dinv, coeffs, p, q, dup, size):
    carry, gain = factor
    for p, q in spans(p, q, size):
        base = (1.0 + carry - gain) * now.get(p, q)
        if carry != 0.0 and before is not None:
            base = base - carry * before.get(p, q)
        new.put(p, (b.get(p, q) + couple(now, p, q, *coeffs, dup)) * (gain * dinv.get(p, q)) + base)


def close(v, last):
    v.put(last, lanes(v.get(last - 1, last), 64))


def smooth(pair, b, dinv, coeffs, factors, first, last, dup, size):
    before, now, spare = pair
    for number, factor in enumerate(factors):
        new = spare if before is None else before
        sweep(new, now, before, factor, b, dinv, coeffs, first + number, last, dup, size)
        close(new, last)
        before, now = now, new
    return now


def inverse(value):
    guess = pl.reciprocal(value, approx=True)
    return guess * (2.0 - value * guess)


def level_coefficients(beta, alpha, first, last, shift, dup, cx, cy, cz, dinv, diag, ends, seam, size):
    lane, row = lane_ids(), row_ids()
    y_last = (lane % 64) // dup == 64 // dup - 1
    y_first = (lane % 64) // dup == 0
    x_rim = jnp.where(row == 0, 0.5, 0.0), jnp.where(row == 7, 0.5, 0.0)
    for p, q in spans(first, last, size):
        here = beta.get(p, q)
        by_x = 0.5 * (here + x_up(here))
        by_x = jnp.concatenate([by_x[:, :-1], jnp.where(row == 7, 0.0, by_x[:, -1:])], axis=1)
        above = jnp.where(y_last, 0.0, lanes(here, -dup))
        below = jnp.where(y_first, 0.0, lanes(here, dup))
        by_y = jnp.where(y_last, 0.0, 0.5 * (here + above))
        face = 0.5 * (beta.get(p - 1, q - 1) + here)
        total = shift * alpha.get(p, q) + (by_x + x_down(by_x)) + (here + 0.5 * (above + below))
        total = total + (face + 0.5 * (here + beta.get(p + 1, q + 1)))
        groups = [total[:, i : i + 1] for i in range(total.shape[1])]
        groups[0] = groups[0] + here[:, :1] * x_rim[0]
        groups[-1] = groups[-1] + here[:, -1:] * x_rim[1]
        total = jnp.concatenate(groups, axis=1)
        cx.put(p, by_x)
        cy.put(p, by_y)
        cz.put(p, face)
        diag.put(p, total)
        dinv.put(p, inverse(jnp.where(total > 0.0, total, 1.0)))
    if first <= seam < last:
        cz.put(seam, cz.get(seam, seam + 1) * ends)
    else:
        cz.put(last, 0.5 * (beta.get(last - 1, last) + beta.get(last, last + 1)))


def restrict_pair(first, second, dup):
    lane = lane_ids()
    total = first + second
    total = jnp.concatenate([total[:, i : i + 1] + total[:, i + 1 : i + 2] for i in range(0, total.shape[1], 2)], axis=1)
    return total + jnp.where((lane // dup) % 2 == 0, lanes(total, -dup), lanes(total, dup))


def restrict(take, p, q, dup):
    fine = take(2 * p, 2 * q)
    fine = fine.reshape((q - p, 2) + fine.shape[1:])
    return restrict_pair(fine[:, 0], fine[:, 1], dup)


def halo_masks():
    x, y, z = position()
    chunk = chunk_of(x, y, z)
    half = lane_ids() // 64
    return chunk, (half + chunk % 2) == 1


def ends_factor():
    x, y, z = position()
    slab = 8 * z + chunk_of(x, y, z)
    half = lane_ids() // 64
    end = ((half == 0) & (slab == 0)) | ((half == 1) & (slab == 8 * GZ - 1))
    return jnp.where(end, 0.0, 1.0)


def shape_of(*dims):
    return jax.ShapeDtypeStruct(dims + TILE, jnp.float32)


def scratch(*dims):
    return pltpu.VMEM(dims + TILE, jnp.float32)


def call(kernel, name, operands, out_shape, scratch_shapes, hbm_outputs=0):
    vmem = pl.BlockSpec(memory_space=pltpu.VMEM)
    return pl.pallas_call(
        kernel,
        out_shape=out_shape,
        in_specs=[vmem] * len(operands),
        out_specs=[pl.BlockSpec(memory_space=pl.ANY)] * hbm_outputs + [vmem] * (len(out_shape) - hbm_outputs),
        scratch_shapes=scratch_shapes,
        compiler_params=pltpu.CompilerParams(vmem_limit_bytes=16 * 2**20),
        name=name,
    )(*operands)


PRE_SHAPES = [(7, 4), (7, 4), (8, 4), (7, 4), (7, 4), (3, 2), (3, 2), (4, 2), (3, 2), (3, 2)]
MID_SHAPES = [(13, 4)] * 5 + [(7, 2)] * 5


def coefficient_planes(pre, mid):
    zero = [Planes(*([(4, mid[i])] if mid else []), *([(17, pre[i])] if pre else [])) for i in range(5)]
    one = [Planes(*([(2, mid[i])] if mid else []), *([(9, pre[i])] if pre else [])) for i in range(5, 10)]
    return zero, one


def pre_kernel(own, *refs):
    pre, (alpha1, beta1, v1, v2, v3, v4), (ghost, ghost1) = refs[:10], refs[10:16], refs[16:]
    zero, one = coefficient_planes(pre, None)
    alpha, beta = Planes((16, own.at[0])), Planes((16, own.at[1]), (24, ghost))
    alpha_one, beta_one = Planes((8, alpha1)), Planes((8, beta1), (12, ghost1))
    close(beta, PLANES)
    level_coefficients(beta, alpha, 17, PLANES, SHIFT_BASE, 1, *zero, None, 16, COEF_SPAN)
    beta_one.put(8, 0.125 * restrict(beta.get, 8, PLANES1, 1))
    alpha_one.put(8, 0.125 * restrict(alpha.get, 8, PLANES1, 1))
    close(beta_one, PLANES1)
    level_coefficients(beta_one, alpha_one, 9, PLANES1, SHIFT_BASE * 4.0, 2, *one, None, 8, COEF_SPAN1)
    b, coeffs, dinv = Planes((16, own.at[2])), zero[:3], zero[3]
    factors = chebyshev_factors(SWEEPS, SMOOTH_LOWER)
    iterates = [None, Planes((17, v1)), Planes((18, v2)), Planes((19, v3)), Planes((20, v4))]
    for p, q in spans(17, PLANES, 4):
        iterates[1].put(p, factors[0][1] * (b.get(p, q) * dinv.get(p, q)))
    close(iterates[1], PLANES)
    for i in range(2, 5):
        sweep(iterates[i], iterates[i - 1], iterates[i - 2], factors[i - 1], b, dinv, coeffs, 16 + i, PLANES, 1, SPAN)
        close(iterates[i], PLANES)


def mid_kernel(own, even, odd, *refs):
    beta1_own, alpha1_own, mid, (beta_s, alpha_s, beta1_s, alpha1_s) = refs[0], refs[1], refs[2:12], refs[12:]
    _, from_even = halo_masks()
    zero, one = coefficient_planes(None, mid)
    for p in range(16):
        alpha_s[p], beta_s[p] = (halo_plane(even.at[a], odd.at[a], p, 16, from_even) for a in range(2))
    beta, alpha = Planes((0, beta_s), (16, own.at[1])), Planes((0, alpha_s), (16, own.at[0]))
    ends = ends_factor()
    level_coefficients(beta, alpha, 4, 17, SHIFT_BASE, 1, *zero, ends, 16, COEF_SPAN)
    beta_one, alpha_one = Planes((0, beta1_s), (8, beta1_own)), Planes((0, alpha1_s), (8, alpha1_own))
    for p, q in spans(0, 8, 2):
        beta_one.put(p, 0.125 * restrict(beta.get, p, q, 1))
        alpha_one.put(p, 0.125 * restrict(alpha.get, p, q, 1))
    level_coefficients(beta_one, alpha_one, 2, 9, SHIFT_BASE * 4.0, 2, *one, ends, 8, COEF_SPAN1)


def halo_plane(even, odd, p, count, from_even):
    if p < count // 2:
        return jnp.where(from_even, even[p], odd[p])
    k = count - 1 - p
    return lanes(jnp.where(from_even, odd[k], even[k]), 64)


def post_kernel(own, even, odd, *refs):
    pre, (alpha1, beta1, v1, v2, v3, v4), mid = refs[:10], refs[10:16], refs[16:26]
    gather, rim, halo_b, late, u1, b1 = refs[26:32]
    f1, f2, f3, b1_s, w_a, w_b, tile_s, rim_s, sent = refs[32:]
    lane = lane_ids()
    _, from_even = halo_masks()
    zero, one = coefficient_planes(pre, mid)
    coeffs, dinv, diag = zero[:3], zero[3], zero[4]
    b = Planes((4, halo_b), (16, own.at[2]))
    for p in range(4, 16):
        b.put(p, halo_plane(even.at[2], odd.at[2], p, 16, from_even)[None])
    factors = chebyshev_factors(SWEEPS, SMOOTH_LOWER)
    iterates = [
        None,
        Planes((4, f1), (17, v1)),
        Planes((5, f2), (18, v2)),
        Planes((6, f3), (19, v3)),
        Planes((7, late), (20, v4)),
    ]
    for p, q in spans(4, 17, 4):
        iterates[1].put(p, factors[0][1] * (b.get(p, q) * dinv.get(p, q)))
    for i in range(2, 5):
        sweep(iterates[i], iterates[i - 1], iterates[i - 2], factors[i - 1], b, dinv, coeffs, 3 + i, 16 + i, 1, SPAN)
    v = iterates[4]
    rim_s[0:20] = v.get(16, 21).reshape((20,) + TILE)
    copies = [pltpu.make_async_copy(rim_s.at[0:20], rim.at[0:20], sent.at[0])]
    copies[0].start()

    def residual(v, b, diag, coeffs, dup):
        return lambda p, q: (b.get(p, q) + couple(v, p, q, *coeffs, dup)) - diag.get(p, q) * v.get(p, q)

    b_one = Planes((4, b1_s), (8, b1))
    for p in range(4, PLANES1):
        b_one.put(p, 0.5 * restrict(residual(v, b, diag, coeffs, 1), p, p + 1, 1))
    coeffs, dinv, diag = one[:3], one[3], one[4]
    w, spare = Planes((0, w_a)), Planes((0, w_b))
    w.put(4, factors[0][1] * (b_one.get(4, PLANES1) * dinv.get(4, PLANES1)))
    close(w, PLANES1)
    w = smooth((None, w, spare), b_one, dinv, coeffs, factors[1:], 5, PLANES1, 2, SPAN1)
    b_two = 0.5 * restrict(residual(w, b_one, diag, coeffs, 2), 4, 6, 2)
    beta_two = 0.125 * restrict(Planes((8, beta1)).get, 4, 6, 2)
    alpha_two = 0.125 * restrict(Planes((8, alpha1)).get, 4, 6, 2)
    tile_s[...] = jnp.where(lane % 4 == 0, b_two, jnp.where(lane % 4 == 1, beta_two, alpha_two))[:, 0]
    copies += [pltpu.make_async_copy(tile_s, gather.at[n], sent.at[n + 1]) for n in range(GX * GZ)]
    for copy in copies[1:]:
        copy.start()
    u1[...] = w.get(8, PLANES1)
    rim_s[20:28] = jnp.where(lane % 2 == 0, w.get(8, PLANES1), b_one.get(8, PLANES1)).reshape((8,) + TILE)
    copies.append(pltpu.make_async_copy(rim_s.at[20:28], rim.at[20:28], sent.at[GX * GZ + 1]))
    copies[-1].start()
    for copy in copies:
        copy.wait()


def down_pre(own):
    shapes = PRE_SHAPES + [(4, 2), (4, 2), (8, 4), (7, 4), (6, 4), (5, 4)]
    return call(pre_kernel, "down_pre", (own,), [shape_of(*n) for n in shapes], [scratch(1, 4), scratch(1, 2)])


def down_mid(own, even, odd, beta1, alpha1):
    return call(
        mid_kernel, "down_mid", (own, even, odd, beta1, alpha1), [shape_of(*n) for n in MID_SHAPES],
        [scratch(16, 4), scratch(16, 4), scratch(8, 2), scratch(8, 2)],
    )


def down_post(own, even, odd, pre, mid):
    shapes = [(GX * GZ, 2), (36,), (12, 4), (13, 4), (4, 2), (4, 2)]
    return call(
        post_kernel, "down_post", (own, even, odd, *pre, *mid), [shape_of(*n) for n in shapes],
        [
            scratch(13, 4), scratch(13, 4), scratch(13, 4), scratch(4, 2), scratch(13, 2), scratch(13, 2),
            scratch(2), scratch(28), pltpu.SemaphoreType.DMA((GX * GZ + 2,)),
        ],
        hbm_outputs=2,
    )


def outer(value, half):
    turned = lanes(value, 64)
    before = jnp.concatenate([lanes(value[-1:], 65), turned[:-1]], axis=0)
    after = jnp.concatenate([turned[1:], lanes(value[:1], 63)], axis=0)
    return jnp.where(half == 0, before, after), turned


def coarse_kernel(mine, other, out, cores, e2_s):
    lane, row = lane_ids(), row_ids()
    half = lane // 64
    x, y, z = position()
    cores[y] = mine[...]
    cores[1 - y] = other[...]

    def collect(f):
        planes = []
        for p in range(2):
            tiles = []
            for group in range(8):
                tile = None
                for q in range(GZ):
                    natural = 7 - group if q % 2 else group
                    rank, core = natural // 2, natural % 2
                    piece = lanes(cores[core, (rank ^ (rank >> 1)) * GZ + q, p], q - f)
                    tile = piece if tile is None else jnp.where(lane % 4 == q, piece, tile)
                tiles.append(tile)
            planes.append(jnp.stack(tiles))
        return planes

    b_two, beta_two, alpha_two = collect(0), collect(1), collect(2)
    slab = lax.broadcasted_iota(jnp.int32, (8,) + TILE, 0)
    end = ((slab == 0) & (lane % 4 == 0) & (half == 0)) | ((slab == 7) & (lane % 4 == 3) & (half == 1))

    def sides(beta, dx, dy):
        x_last, x_first = row >= 8 - dx, row < dx
        place = (lane % 64) // dy
        y_last, y_first = place == 64 // dy - 1, place == 0
        by_x = jnp.where(x_last, 0.0, 0.5 * (beta + rows(beta, -dx)))
        by_y = jnp.where(y_last, 0.0, 0.5 * (beta + lanes(beta, -dy)))
        rim = jnp.where(x_last | x_first, 0.5, 0.0) + jnp.where(y_last | y_first, 0.5, 0.0)
        return by_x, by_y, (by_x + rows(by_x, dx)) + (by_y + lanes(by_y, dy)) + beta * rim

    def scaled(by_x, by_y, inv, dx, dy):
        return by_x * inv, rows(by_x, dx) * inv, by_y * inv, lanes(by_y, dy) * inv

    def flat(v, coeffs, dx, dy):
        x_above, x_below, y_above, y_below = coeffs
        total = x_above * rows(v, -dx) + x_below * rows(v, dx)
        return total + (y_above * lanes(v, -dy) + y_below * lanes(v, dy))

    x0, y0, s0 = sides(beta_two[0], 1, 4)
    x1, y1, s1 = sides(beta_two[1], 1, 4)
    middle = 0.5 * (beta_two[0] + beta_two[1])
    inner = 0.5 * (beta_two[1] + lanes(beta_two[1], 64))
    edge = 0.5 * (beta_two[0] + jnp.where(end, 0.0, outer(beta_two[0], half)[0]))
    shift = SHIFT_BASE * 16.0
    diag_a = shift * alpha_two[0] + s0 + (middle + edge)
    diag_b = shift * alpha_two[1] + s1 + (middle + inner)
    inv_a, inv_b = inverse(diag_a), inverse(diag_b)
    flat_a, flat_b = scaled(x0, y0, inv_a, 1, 4), scaled(x1, y1, inv_b, 1, 4)
    middle_a, middle_b = middle * inv_a, middle * inv_b
    rim_a, inner_b = jnp.where(end, 0.0, edge) * inv_a, inner * inv_b
    rhs_a, rhs_b = b_two[0] * inv_a, b_two[1] * inv_b

    def apply_two(va, vb):
        ta = flat(va, flat_a, 1, 4) + (middle_a * vb + rim_a * outer(va, half)[0])
        tb = flat(vb, flat_b, 1, 4) + (middle_b * va + inner_b * lanes(vb, 64))
        return ta, tb

    def sweeps_two(before, now, factors):
        for carry, gain in factors:
            totals = apply_two(*now)
            new = []
            for v, old, rhs, total in zip(now, before or (None, None), (rhs_a, rhs_b), totals):
                base = (1.0 + carry - gain) * v + gain * rhs
                if carry != 0.0 and old is not None:
                    base = base - carry * old
                new.append(base + gain * total)
            before, now = now, new
        return now

    factors = chebyshev_factors(SWEEPS, SMOOTH_LOWER)
    ua, ub = sweeps_two(None, (factors[0][1] * rhs_a, factors[0][1] * rhs_b), factors[1:])
    ta, tb = apply_two(ua, ub)

    def restrict_whole(first, second):
        total = first + second
        total = total + jnp.where(row % 2 == 0, rows(total, -1), rows(total, 1))
        return total + jnp.where((lane // 4) % 2 == 0, lanes(total, -4), lanes(total, 4))

    b_low = 0.5 * restrict_whole(diag_a * (rhs_a + ta - ua), diag_b * (rhs_b + tb - ub))
    beta_low = 0.125 * restrict_whole(beta_two[0], beta_two[1])
    alpha_low = 0.125 * restrict_whole(alpha_two[0], alpha_two[1])

    x_low, y_low, s_low = sides(beta_low, 2, 8)
    beyond, turned = outer(beta_low, half)
    inner_low = 0.5 * (beta_low + turned)
    edge_low = 0.5 * (beta_low + jnp.where(end, 0.0, beyond))
    inv_low = inverse(SHIFT_BASE * 64.0 * alpha_low + s_low + (inner_low + edge_low))
    flat_low = scaled(x_low, y_low, inv_low, 2, 8)
    rim_low = jnp.where(end, 0.0, edge_low) * inv_low
    inner_low = inner_low * inv_low
    rhs_low = b_low * inv_low
    before = v = None
    for carry, gain in chebyshev_factors(BOTTOM, BOTTOM_LOWER):
        if v is None:
            v = gain * rhs_low
            continue
        beyond, turned = outer(v, half)
        base = (1.0 + carry - gain) * v + gain * rhs_low
        if before is not None:
            base = base - carry * before
        total = flat(v, flat_low, 2, 8) + (inner_low * turned + rim_low * beyond)
        before, v = v, base + gain * total
    va, vb = sweeps_two(None, (ua + v, ub + v), factors)
    for group in range(8):
        e2_s[group, 0] = va[group]
        e2_s[group, 1] = vb[group]

    chunk = chunk_of(x, y, z)
    place = 8 * z + chunk

    def fetch(offset):
        index = jnp.clip(place + offset, 0, 8 * GZ - 1)
        out = []
        for p in range(2):
            tile = pltpu.roll(e2_s[index % 8, p], (128 - index // 8) % 128, 1)
            tile = jnp.where(lane % 4 == 0, tile, 0.0)
            tile = tile + lanes(tile, 1)
            out.append(tile + lanes(tile, 2))
        return out

    below, here, above = fetch(-1), fetch(0), fetch(1)
    first = half == 0
    out[0] = jnp.where(first, below[0], above[0])
    out[1] = jnp.where(first, below[1], above[1])
    out[2] = lanes(jnp.where(first, above[1], below[1]), 64)
    out[3] = lanes(jnp.where(first, above[0], below[0]), 64)
    out[4] = here[0]
    out[5] = here[1]


def coarse(mine, other):
    vmem = pl.BlockSpec(memory_space=pltpu.VMEM)
    return pl.pallas_call(
        coarse_kernel,
        out_shape=shape_of(6),
        in_specs=[vmem] * 2,
        out_specs=vmem,
        scratch_shapes=[scratch(2, GX * GZ, 2), scratch(8, 2)],
        compiler_params=pltpu.CompilerParams(vmem_limit_bytes=8 * 2**20),
        name="coarse",
    )(mine, other)


def up_kernel(e_two, rim_even, rim_odd, own, halo_b, late, u1, b1, v4, *refs):
    pre, mid, (out, v_a, v_b, w_a, w_b, bx_s) = refs[:10], refs[10:20], refs[20:]
    zero, one = coefficient_planes(pre, mid)
    lane, row = lane_ids(), row_ids()
    _, from_even = halo_masks()
    factors = chebyshev_factors(SWEEPS, SMOOTH_LOWER)

    for p in range(1, 8):
        if p >= 4:
            k = 7 - p
            both = lanes(jnp.where(from_even, rim_odd[20 + 2 * k : 22 + 2 * k], rim_even[20 + 2 * k : 22 + 2 * k]), 64)
        else:
            both = jnp.where(from_even, rim_even[20 + 2 * p : 22 + 2 * p], rim_odd[20 + 2 * p : 22 + 2 * p])
        w_a[p] = jnp.where(lane % 2 == 0, both, lanes(both, 1)) + e_two[p // 2]
        if p >= 2:
            bx_s[p] = jnp.where(lane % 2 == 0, lanes(both, -1), both)
    for p in range(8, PLANES1):
        w_a[p] = u1[p - 8] + e_two[p // 2]
    w_a[PLANES1] = lanes(w_a[PLANES1 - 1], 64)
    pair = (Planes((0, w_b)), Planes((0, w_a)), None)
    w = smooth(pair, Planes((0, bx_s), (8, b1)), one[3], one[:3], factors, 2, PLANES1, 2, SPAN1)

    for p in range(11, PLANES):
        if p >= 16:
            start = Planes((7, late), (20, v4)).get(p, p + 1)[0]
        else:
            k = 4 * (15 - p)
            start = lanes(jnp.where(from_even, rim_odd[k : k + 4], rim_even[k : k + 4]), 64)
        e_one = w.get(p // 2, p // 2 + 1)[0]
        e_one = jnp.concatenate([e_one[:1], e_one[:1], e_one[1:], e_one[1:]], axis=0)
        v_a[p] = start + e_one
    v_a[PLANES] = lanes(v_a[PLANES - 1], 64)
    b, diag, coeffs = Planes((4, halo_b), (16, own.at[2])), zero[4], zero[:3]
    v = smooth((Planes((0, v_b)), Planes((0, v_a)), None), b, zero[3], coeffs, factors, 12, PLANES, 1, SPAN)
    low = (lane // 32) % 2 == 0
    for k in range(4):
        for o in range(2):
            parts = []
            for pp in range(2):
                p = 16 + k + 4 * pp
                value = v.get(p, p + 1)
                if o == 1:
                    value = (b.get(p, p + 1) + couple(v, p, p + 1, *coeffs, 1)) - diag.get(p, p + 1) * value
                parts.append(regroup([value[0, i] for i in range(4)], 0, 2, row))
            for i in range(GX):
                one, two = parts[0][i], parts[1][i]
                out[2 * i, pl.ds(o * 32 + k * 8, 8), :] = jnp.where(low, one, lanes(two, 32))
                out[2 * i + 1, pl.ds(o * 32 + k * 8, 8), :] = jnp.where(low, lanes(one, -32), two)


def up(*operands):
    return call(
        up_kernel, "up_strokes", operands, [jax.ShapeDtypeStruct((8, 64, 128), jnp.float32)],
        [scratch(25, 4), scratch(25, 4), scratch(13, 2), scratch(13, 2), scratch(8, 2)],
    )[0]


def unpack_kernel(in_ref, v_ref, r_ref, fields, turned, staged, left):
    z = lax.axis_index("gz")
    lane = lane_ids()
    for x in range(GX):
        for y in range(GY):
            start = pl.multiple_of(chunk_of(x, y, z) * 64, 64)
            staged[pl.ds(start, 64), :] = in_ref[x * GY + y]
    copies = [pltpu.make_async_copy(fields.at[o], ref, left.at[o]) for o, ref in enumerate((v_ref, r_ref))]
    for o, copy in enumerate(copies):
        for xg in range(2):
            slot = turned.at[2 * o + xg]
            for k in range(4):
                tiles = [staged[pl.ds(o * 32 + k * 8 + 2 * x4 + xg, 8, stride=64), :] for x4 in range(4)]
                for g, tile in enumerate(regroup(tiles, 1, 32, lane)):
                    slot[pl.ds(depth_of(k, g), 8, stride=16), :] = tile
            fields[o, 4 * xg : 4 * xg + 4] = slot[...].T.reshape(4, 32, 128)
        copy.start()
    for copy in copies:
        copy.wait()


def unpack(received):
    vmem = pl.BlockSpec(memory_space=pltpu.VMEM)
    return pl.pallas_call(
        unpack_kernel,
        out_shape=[jax.ShapeDtypeStruct(BLOCK, jnp.float32)] * 2,
        in_specs=[vmem],
        out_specs=[pl.BlockSpec(memory_space=pltpu.HBM)] * 2,
        scratch_shapes=[
            pltpu.VMEM((2,) + BLOCK, jnp.float32),
            pltpu.VMEM((4, 128, 128), jnp.float32),
            pltpu.VMEM((512, 128), jnp.float32),
            pltpu.SemaphoreType.DMA((2,)),
        ],
        compiler_params=pltpu.CompilerParams(vmem_limit_bytes=4 * 2**20),
        name="unpack",
    )(received)


def slab_shards(right_side, alpha_coef, beta_coef):
    even_pairs, odd_pairs = swap_pairs(False), swap_pairs(True)
    packed = pack(jnp.stack([alpha_coef, beta_coef, right_side]))
    own = to_slab(lax.all_to_all(packed, RING, 0, 0))
    even = lax.ppermute(own, ALL, even_pairs)
    odd = lax.ppermute(own, ALL, odd_pairs)
    found = down_pre(own)
    pre, alpha1, beta1, v4 = found[:10], found[10], found[11], found[15]
    mid = down_mid(own, even, odd, beta1, alpha1)
    gather, rim, halo_b, late, u1, b1 = down_post(own, even, odd, found, mid)
    rim_even = lax.ppermute(rim, ALL, even_pairs)
    rim_odd = lax.ppermute(rim, ALL, odd_pairs)
    mine = lax.all_to_all(gather, ("gx", "gz"), 0, 0)
    other = lax.ppermute(mine, "gy", [(0, 1), (1, 0)])
    kept = (own, halo_b, late, u1, b1, v4, *pre, *mid)
    result = up(coarse(mine, other), rim_even, rim_odd, *kept)
    return tuple(unpack(lax.all_to_all(result, RING, 0, 0)))


def solution(mesh):
    spec = P("gx", "gy", "gz")
    plain = jax.shard_map(shards, mesh=mesh, in_specs=(spec,) * 3, out_specs=(spec,) * 2, check_vma=False)
    slabs = jax.shard_map(slab_shards, mesh=mesh, in_specs=(spec,) * 3, out_specs=(spec,) * 2, check_vma=False)
    sizes = tuple(mesh.shape[axis] for axis in ALL)

    def run(right_side, alpha_coef, beta_coef):
        block = tuple(n // size for n, size in zip(right_side.shape, sizes))
        fits = sizes == (GX, GY, GZ) and block == BLOCK
        return (slabs if fits else plain)(right_side, alpha_coef, beta_coef)

    return run
```

```python
import jax
import jax.numpy as jnp
from jax import lax
from jax.experimental import pallas as pl
from jax.experimental.pallas import tpu as pltpu
from jax.sharding import PartitionSpec as P

LEVELS = 3
SWEEPS = 4
BOTTOM = 12


SHIFT_BASE = 0.01
UPPER_EIG = 2.0
SMOOTH_LOWER = 0.25
BOTTOM_LOWER = 0.02


def with_halo(block, sides, width):
    for axis, dim in sides:
        count = lax.axis_size(axis)
        forward = [(i, i + 1) for i in range(count - 1)]
        backward = [(target, source) for source, target in forward]
        low = lax.ppermute(
            lax.slice_in_dim(block, block.shape[dim] - width, None, axis=dim), axis, forward
        )
        high = lax.ppermute(lax.slice_in_dim(block, 0, width, axis=dim), axis, backward)
        block = jnp.concatenate([low, block, high], axis=dim)
    return block


def partner_2(array, axis, distance):
    return lax.ppermute(array, axis, [(i, i ^ 1 << distance) for i in range(lax.axis_size(axis))])


def split_padded(padded):
    return (
        padded[:-2, 1:-1, 1:-1],
        padded[2:, 1:-1, 1:-1],
        padded[1:-1, :-2, 1:-1],
        padded[1:-1, 2:, 1:-1],
        padded[1:-1, 1:-1, :-2],
        padded[1:-1, 1:-1, 2:],
    )


def zero_pad(field):
    return jnp.pad(field, 1)


def rim_iterate(field):
    return with_halo(field, (("gx", 0), ("gy", 1), ("gz", 2)), 1)


def rim_coefficient(field):
    return with_halo(field, (("gx", 0), ("gy", 1), ("gz", 2)), 1)


def level_operator(beta_level, alpha_level, padded_beta, shift):
    coeffs = tuple((0.5 * (beta_level + other) for other in split_padded(padded_beta)))
    diagonal = shift * alpha_level
    for coeff in coeffs:
        diagonal = diagonal + coeff
    return (coeffs, diagonal)


def apply_operator(field, operator, pad_field):
    coeffs, diagonal = operator
    others = split_padded(pad_field(field))
    total = coeffs[0] * others[0]
    for index in range(1, 6):
        total = total + coeffs[index] * others[index]
    return diagonal * field - total


def chebyshev(iterate, rhs_level, operator, count, lower, zero_start, pad_field):
    diagonal = operator[1]
    center = (UPPER_EIG + lower) / 2.0
    half_width = (UPPER_EIG - lower) / 2.0
    sigma_ratio = center / half_width
    rho_old = 1.0 / sigma_ratio
    if zero_start:
        remain = rhs_level
    else:
        remain = rhs_level - apply_operator(iterate, operator, pad_field)
    update = remain / diagonal / center
    iterate = iterate + update
    for sweep_index in range(count - 1):
        remain = rhs_level - apply_operator(iterate, operator, pad_field)
        rho_new = 1.0 / (2.0 * sigma_ratio - rho_old)
        update = rho_new * rho_old * update + 2.0 * rho_new / half_width * (remain / diagonal)
        iterate = iterate + update
        rho_old = rho_new
    return iterate


def restrict_mean(field):
    first, second, third = field.shape
    blocks = field.reshape(first // 2, 2, second // 2, 2, third // 2, 2)
    return jnp.sum(blocks, axis=(1, 3, 5)) * 0.125


def prolong_copy(field):
    return jnp.repeat(jnp.repeat(jnp.repeat(field, 2, axis=0), 2, axis=1), 2, axis=2)


def join_partner(packed, partner, device_index, bit_index, dim):
    position = device_index // 2**bit_index % 2
    lower_first = jnp.concatenate([packed, partner], axis=dim)
    upper_first = jnp.concatenate([partner, packed], axis=dim)
    return jnp.where(position == 0, lower_first, upper_first)


def shards(right_side, alpha_coef, beta_coef):
    betas = [beta_coef]
    alphas = [alpha_coef]
    for level in range(LEVELS):
        betas.append(restrict_mean(betas[-1]))
        alphas.append(restrict_mean(alphas[-1]))
    operators = []
    for level in range(LEVELS):
        padded_beta = rim_coefficient(betas[level])
        operators.append(
            level_operator(betas[level], alphas[level], padded_beta, SHIFT_BASE * 4.0**level)
        )
    rhs_levels = [right_side]
    smoothed = []
    for level in range(LEVELS):
        iterate = chebyshev(
            jnp.zeros_like(rhs_levels[level]),
            rhs_levels[level],
            operators[level],
            SWEEPS,
            SMOOTH_LOWER,
            True,
            rim_iterate,
        )
        remain = rhs_levels[level] - apply_operator(iterate, operators[level], rim_iterate)
        smoothed.append(iterate)
        rhs_levels.append(4.0 * restrict_mean(remain))
    coarse_rhs = rhs_levels[LEVELS]
    local_shape = coarse_rhs.shape
    packed = jnp.stack([coarse_rhs, betas[LEVELS], alphas[LEVELS]])
    index_x = lax.axis_index("gx")
    index_y = lax.axis_index("gy")
    index_z = lax.axis_index("gz")
    for bit_index in range(lax.axis_size("gx").bit_length() - 1):
        partner = partner_2(packed, "gx", bit_index)
        packed = join_partner(packed, partner, index_x, bit_index, 1)
    for bit_index in range(lax.axis_size("gy").bit_length() - 1):
        partner = partner_2(packed, "gy", bit_index)
        packed = join_partner(packed, partner, index_y, bit_index, 2)
    for bit_index in range(lax.axis_size("gz").bit_length() - 1):
        partner = partner_2(packed, "gz", bit_index)
        packed = join_partner(packed, partner, index_z, bit_index, 3)
    whole_rhs = packed[0]
    whole_beta = packed[1]
    whole_alpha = packed[2]
    bottom_operator = level_operator(
        whole_beta, whole_alpha, zero_pad(whole_beta), SHIFT_BASE * 4.0**LEVELS
    )
    whole_correction = chebyshev(
        jnp.zeros_like(whole_rhs), whole_rhs, bottom_operator, BOTTOM, BOTTOM_LOWER, True, zero_pad
    )
    starts = (index_x * local_shape[0], index_y * local_shape[1], index_z * local_shape[2])
    correction = lax.dynamic_slice(whole_correction, starts, local_shape)
    for level in range(LEVELS - 1, -1, -1):
        start_field = smoothed[level] + prolong_copy(correction)
        correction = chebyshev(
            start_field,
            rhs_levels[level],
            operators[level],
            SWEEPS,
            SMOOTH_LOWER,
            False,
            rim_iterate,
        )
    residual_field = right_side - apply_operator(correction, operators[0], rim_iterate)
    return (correction, residual_field)


GX, GY, GZ = 4, 2, 4
COUNT = GX * GY * GZ
RIM = 28
BLOCK = (8, 32, 128)
RING = ("gx", "gy")
ALL = ("gx", "gy", "gz")
TILE = (8, 128)
PLANES = 24
PLANES1 = 12
SPAN, SPAN1, COEF_SPAN, COEF_SPAN1 = 2, 4, 2, 4


def chunk_of(x, y, z):
    natural = 2 * (x ^ (x >> 1)) + y
    return natural + (z % 2) * (7 - 2 * natural)


def position():
    return lax.axis_index("gx"), lax.axis_index("gy"), lax.axis_index("gz")


def swap_pairs(odd):
    place = {}
    for x in range(GX):
        for y in range(GY):
            for z in range(GZ):
                place[8 * z + chunk_of(x, y, z)] = (x * GY + y) * GZ + z
    count = len(place)
    if odd:
        pairs = [(i, i + 1) for i in range(1, count - 1, 2)]
    else:
        pairs = [(i, i + 1) for i in range(0, count, 2)]
    return [(place[a], place[b]) for a, b in pairs] + [(place[b], place[a]) for a, b in pairs]


def lane_ids():
    return lax.broadcasted_iota(jnp.int32, TILE, 1)


def row_ids():
    return lax.broadcasted_iota(jnp.int32, TILE, 0)


def lanes(value, shift):
    return pltpu.roll(value, shift % 128, value.ndim - 1)


def rows(value, shift):
    return pltpu.roll(value, shift % 8, value.ndim - 2)


def regroup(tiles, axis, width, ids):
    move = lanes if axis == 1 else rows
    group = ids // width % 4
    odd, upper = group % 2 == 1, group >= 2
    a, b, c, d = tiles
    turned = move(jnp.where(odd, a, b), width)
    a, b = jnp.where(odd, turned, a), jnp.where(odd, b, turned)
    turned = move(jnp.where(odd, c, d), width)
    c, d = jnp.where(odd, turned, c), jnp.where(odd, d, turned)
    turned = move(jnp.where(upper, a, c), 2 * width)
    a, c = jnp.where(upper, turned, a), jnp.where(upper, c, turned)
    turned = move(jnp.where(upper, b, d), 2 * width)
    own = jnp.where(upper, d, b)
    inner = odd != upper
    return [a, jnp.where(inner, own, turned), c, jnp.where(inner, turned, own)]


def depth_of(k, group):
    half, part = group // 2, group % 2
    plane = k + 4 * part
    return 15 - plane if half else plane


def pack_kernel(fields, out_ref, turned, staged):
    z = lax.axis_index("gz")
    lane = lane_ids()
    for a in range(3):
        for xg in range(2):
            slot = turned.at[2 * a + xg]
            slot[...] = fields[a, 4 * xg : 4 * xg + 4].reshape(128, 128).T
            for k in range(4):
                tiles = [slot[pl.ds(depth_of(k, g), 8, stride=16), :] for g in range(4)]
                for x4, tile in enumerate(regroup(tiles, 1, 32, lane)):
                    staged[pl.ds(a * 32 + k * 8 + 2 * x4 + xg, 8, stride=96), :] = tile
    for x in range(GX):
        for y in range(GY):
            start = pl.multiple_of(chunk_of(x, y, z) * 96, 96)
            out_ref[x * GY + y] = staged[pl.ds(start, 96), :]


def pack(fields):
    return pl.pallas_call(
        pack_kernel,
        out_shape=jax.ShapeDtypeStruct((8, 96, 128), jnp.float32),
        in_specs=[pl.BlockSpec(memory_space=pltpu.VMEM)],
        out_specs=pl.BlockSpec(memory_space=pltpu.VMEM),
        scratch_shapes=[pltpu.VMEM((6, 128, 128), jnp.float32), pltpu.VMEM((768, 128), jnp.float32)],
        compiler_params=pltpu.CompilerParams(vmem_limit_bytes=4 * 2**20),
        name="pack",
    )(fields)


def shape_of(*dims):
    return jax.ShapeDtypeStruct(dims + TILE, jnp.float32)


def scratch(*dims):
    return pltpu.VMEM(dims + TILE, jnp.float32)


def halo_masks():
    x, y, z = position()
    chunk = chunk_of(x, y, z)
    half = lane_ids() // 64
    return chunk, (half + chunk % 2) == 1


PLACE = [(r, True) for r in range(6)] + [(4, False), (5, False), (3, False), (2, False), (1, False), (0, False)]
PLACE += [(6, False), (6, True)]
FIRST_TILE = (0, 6, 13)
MESSAGE = 19


def message(planes, near, count):
    tiles = [jnp.where(near, planes[t], planes[t + 4]) for t in range(4)]
    tiles += [jnp.where(near, planes[t], lanes(planes[t + 2], 64)) for t in (4, 5)]
    if count == 7:
        tiles.append(jnp.where(near, lanes(planes[2], 64), planes[3]))
    return tiles


def halo_plane(even, odd, a, r, from_even):
    tile, moved = PLACE[r]
    tile = FIRST_TILE[a] + tile
    if moved:
        return lanes(jnp.where(from_even, odd[tile], even[tile]), 64)
    return jnp.where(from_even, even[tile], odd[tile])


def slab_kernel(in_ref, out_ref, even_ref, odd_ref):
    lane, row = lane_ids(), row_ids()
    low = (lane // 32) % 2 == 0
    _, from_even = halo_masks()
    for a in range(3):
        planes = [None] * 8
        for k in range(4):
            part = ([], [])
            for x in range(GX):
                first = in_ref[2 * x, pl.ds(a * 32 + k * 8, 8), :]
                second = in_ref[2 * x + 1, pl.ds(a * 32 + k * 8, 8), :]
                part[0].append(jnp.where(low, first, lanes(second, 32)))
                part[1].append(jnp.where(low, lanes(first, -32), second))
            for pp in range(2):
                planes[k + 4 * pp] = jnp.stack(regroup(part[pp], 0, 2, row))
                out_ref[a, k + 4 * pp] = planes[k + 4 * pp]
        count = 7 if a == 1 else 6
        for near, ref in ((from_even, even_ref), (~from_even, odd_ref)):
            for t, tile in enumerate(message(planes, near, count)):
                ref[FIRST_TILE[a] + t] = tile


def to_slab(received):
    vmem = pl.BlockSpec(memory_space=pltpu.VMEM)
    return pl.pallas_call(
        slab_kernel,
        out_shape=[shape_of(3, 8, 4), shape_of(MESSAGE, 4), shape_of(MESSAGE, 4)],
        in_specs=[vmem],
        out_specs=[vmem] * 3,
        compiler_params=pltpu.CompilerParams(vmem_limit_bytes=4 * 2**20),
        name="to_slab",
    )(received)


class Planes:
    def __init__(self, *segments):
        self.segments = [(first, first + ref.shape[0], ref) for first, ref in segments]

    def find(self, p, q):
        for first, last, ref in self.segments:
            low, high = max(p, first), min(q, last)
            if low < high:
                yield low, high, ref, slice(low - first, high - first)

    def get(self, p, q):
        pieces = [ref[place] for _, _, ref, place in self.find(p, q)]
        return pieces[0] if len(pieces) == 1 else jnp.concatenate(pieces, axis=0)

    def put(self, p, value):
        for low, high, ref, place in self.find(p, p + value.shape[0]):
            ref[place] = value[low - p : high - p]


def spans(first, last, size):
    return [(p, min(p + size, last)) for p in range(first, last, size)]


def x_up(value):
    return jnp.concatenate([value[:, 1:], rows(value[:, :1], -1)], axis=1)


def x_down(value):
    return jnp.concatenate([rows(value[:, -1:], 1), value[:, :-1]], axis=1)


def couple(v, p, q, cx, cy, cz, dup):
    here, by_x, by_y = v.get(p, q), cx.get(p, q), cy.get(p, q)
    total = by_x * x_up(here) + x_down(by_x * here)
    total = total + (by_y * lanes(here, -dup) + lanes(by_y * here, dup))
    return total + (cz.get(p, q) * v.get(p - 1, q - 1) + cz.get(p + 1, q + 1) * v.get(p + 1, q + 1))


def chebyshev_factors(count, lower):
    center = (UPPER_EIG + lower) / 2.0
    half_width = (UPPER_EIG - lower) / 2.0
    ratio = center / half_width
    old = 1.0 / ratio
    out = [(0.0, 1.0 / center)]
    for _ in range(count - 1):
        new = 1.0 / (2.0 * ratio - old)
        out.append((new * old, 2.0 * new / half_width))
        old = new
    return out


def sweep(new, now, before, factor, b, dinv, coeffs, p, q, dup, size):
    carry, gain = factor
    for p, q in spans(p, q, size):
        base = (1.0 + carry - gain) * now.get(p, q)
        if carry != 0.0 and before is not None:
            base = base - carry * before.get(p, q)
        new.put(p, (b.get(p, q) + couple(now, p, q, *coeffs, dup)) * (gain * dinv.get(p, q)) + base)


def close(v, last):
    v.put(last, lanes(v.get(last - 1, last), 64))


def smooth(pair, b, dinv, coeffs, factors, first, last, dup, size):
    before, now, spare = pair
    for number, factor in enumerate(factors):
        new = spare if before is None else before
        sweep(new, now, before, factor, b, dinv, coeffs, first + number, last, dup, size)
        close(new, last)
        before, now = now, new
    return now


def inverse(value):
    guess = pl.reciprocal(value, approx=True)
    return guess * (2.0 - value * guess)


def level_coefficients(beta, alpha, first, last, shift, dup, cx, cy, cz, dinv, diag, ends, seam, size):
    lane, row = lane_ids(), row_ids()
    y_last = (lane % 64) // dup == 64 // dup - 1
    y_first = (lane % 64) // dup == 0
    x_rim = jnp.where(row == 0, 0.5, 0.0), jnp.where(row == 7, 0.5, 0.0)
    for p, q in spans(first, last, size):
        here = beta.get(p, q)
        by_x = 0.5 * (here + x_up(here))
        by_x = jnp.concatenate([by_x[:, :-1], jnp.where(row == 7, 0.0, by_x[:, -1:])], axis=1)
        above = jnp.where(y_last, 0.0, lanes(here, -dup))
        below = jnp.where(y_first, 0.0, lanes(here, dup))
        by_y = jnp.where(y_last, 0.0, 0.5 * (here + above))
        face = 0.5 * (beta.get(p - 1, q - 1) + here)
        total = shift * alpha.get(p, q) + (by_x + x_down(by_x)) + (here + 0.5 * (above + below))
        total = total + (face + 0.5 * (here + beta.get(p + 1, q + 1)))
        groups = [total[:, i : i + 1] for i in range(total.shape[1])]
        groups[0] = groups[0] + here[:, :1] * x_rim[0]
        groups[-1] = groups[-1] + here[:, -1:] * x_rim[1]
        total = jnp.concatenate(groups, axis=1)
        cx.put(p, by_x)
        cy.put(p, by_y)
        cz.put(p, face)
        diag.put(p, total)
        dinv.put(p, inverse(jnp.where(total > 0.0, total, 1.0)))
    if first <= seam < last:
        cz.put(seam, cz.get(seam, seam + 1) * ends)
    else:
        cz.put(last, 0.5 * (beta.get(last - 1, last) + beta.get(last, last + 1)))


def restrict_pair(first, second, dup):
    lane = lane_ids()
    total = first + second
    total = jnp.concatenate([total[:, i : i + 1] + total[:, i + 1 : i + 2] for i in range(0, total.shape[1], 2)], axis=1)
    return total + jnp.where((lane // dup) % 2 == 0, lanes(total, -dup), lanes(total, dup))


def restrict(take, p, q, dup):
    fine = take(2 * p, 2 * q)
    fine = fine.reshape((q - p, 2) + fine.shape[1:])
    return restrict_pair(fine[:, 0], fine[:, 1], dup)


def ends_factor():
    x, y, z = position()
    slab = 8 * z + chunk_of(x, y, z)
    half = lane_ids() // 64
    end = ((half == 0) & (slab == 0)) | ((half == 1) & (slab == 8 * GZ - 1))
    return jnp.where(end, 0.0, 1.0)


def call(kernel, name, operands, out_shape, scratch_shapes, hbm_outputs=0):
    vmem = pl.BlockSpec(memory_space=pltpu.VMEM)
    return pl.pallas_call(
        kernel,
        out_shape=out_shape,
        in_specs=[vmem] * len(operands),
        out_specs=[pl.BlockSpec(memory_space=pl.ANY)] * hbm_outputs + [vmem] * (len(out_shape) - hbm_outputs),
        scratch_shapes=scratch_shapes,
        compiler_params=pltpu.CompilerParams(vmem_limit_bytes=16 * 2**20),
        name=name,
    )(*operands)


PRE_SHAPES = [(7, 4), (7, 4), (8, 4), (7, 4), (7, 4), (3, 2), (3, 2), (4, 2), (3, 2), (3, 2)]
MID_SHAPES = [(13, 4)] * 5 + [(7, 2)] * 5


def coefficient_planes(pre, mid):
    zero = [Planes(*([(4, mid[i])] if mid else []), *([(17, pre[i])] if pre else [])) for i in range(5)]
    one = [Planes(*([(2, mid[i])] if mid else []), *([(9, pre[i])] if pre else [])) for i in range(5, 10)]
    return zero, one


def pre_kernel(own, *refs):
    pre, (alpha1, beta1, v1, v2, v3, v4), (ghost, ghost1) = refs[:10], refs[10:16], refs[16:]
    zero, one = coefficient_planes(pre, None)
    alpha, beta = Planes((16, own.at[0])), Planes((16, own.at[1]), (24, ghost))
    alpha_one, beta_one = Planes((8, alpha1)), Planes((8, beta1), (12, ghost1))
    close(beta, PLANES)
    level_coefficients(beta, alpha, 17, PLANES, SHIFT_BASE, 1, *zero, None, 16, COEF_SPAN)
    beta_one.put(8, 0.125 * restrict(beta.get, 8, PLANES1, 1))
    alpha_one.put(8, 0.125 * restrict(alpha.get, 8, PLANES1, 1))
    close(beta_one, PLANES1)
    level_coefficients(beta_one, alpha_one, 9, PLANES1, SHIFT_BASE * 4.0, 2, *one, None, 8, COEF_SPAN1)
    b, coeffs, dinv = Planes((16, own.at[2])), zero[:3], zero[3]
    factors = chebyshev_factors(SWEEPS, SMOOTH_LOWER)
    iterates = [None, Planes((17, v1)), Planes((18, v2)), Planes((19, v3)), Planes((20, v4))]
    for p, q in spans(17, PLANES, 4):
        iterates[1].put(p, factors[0][1] * (b.get(p, q) * dinv.get(p, q)))
    close(iterates[1], PLANES)
    for i in range(2, 5):
        sweep(iterates[i], iterates[i - 1], iterates[i - 2], factors[i - 1], b, dinv, coeffs, 16 + i, PLANES, 1, SPAN)
        close(iterates[i], PLANES)


def mid_kernel(own, even, odd, *refs):
    beta1_own, alpha1_own, mid, (beta_s, alpha_s, beta1_s, alpha1_s) = refs[0], refs[1], refs[2:12], refs[12:]
    _, from_even = halo_masks()
    zero, one = coefficient_planes(None, mid)
    for p in range(2, 16):
        beta_s[p] = halo_plane(even, odd, 1, 15 - p, from_even)
        if p >= 4:
            alpha_s[p] = halo_plane(even, odd, 0, 15 - p, from_even)
    beta, alpha = Planes((0, beta_s), (16, own.at[1])), Planes((0, alpha_s), (16, own.at[0]))
    ends = ends_factor()
    level_coefficients(beta, alpha, 4, 17, SHIFT_BASE, 1, *zero, ends, 16, COEF_SPAN)
    beta_one, alpha_one = Planes((0, beta1_s), (8, beta1_own)), Planes((0, alpha1_s), (8, alpha1_own))
    for p in range(1, 8):
        beta_one.put(p, 0.125 * restrict(beta.get, p, p + 1, 1))
        if p >= 2:
            alpha_one.put(p, 0.125 * restrict(alpha.get, p, p + 1, 1))
    level_coefficients(beta_one, alpha_one, 2, 9, SHIFT_BASE * 4.0, 2, *one, ends, 8, COEF_SPAN1)


def post_kernel(own, even, odd, *refs):
    pre, (alpha1, beta1, v1, v2, v3, v4), mid = refs[:10], refs[10:16], refs[16:26]
    gather, rim, halo_b, late, u1, b1 = refs[26:32]
    f1, f2, f3, b1_s, w_a, w_b, tile_s, rim_s, sent = refs[32:]
    lane = lane_ids()
    _, from_even = halo_masks()
    zero, one = coefficient_planes(pre, mid)
    coeffs, dinv, diag = zero[:3], zero[3], zero[4]
    b = Planes((4, halo_b), (16, own.at[2]))
    for p in range(4, 16):
        b.put(p, halo_plane(even, odd, 2, 15 - p, from_even)[None])
    factors = chebyshev_factors(SWEEPS, SMOOTH_LOWER)
    iterates = [
        None,
        Planes((4, f1), (17, v1)),
        Planes((5, f2), (18, v2)),
        Planes((6, f3), (19, v3)),
        Planes((7, late), (20, v4)),
    ]
    for p, q in spans(4, 17, 4):
        iterates[1].put(p, factors[0][1] * (b.get(p, q) * dinv.get(p, q)))
    for i in range(2, 5):
        sweep(iterates[i], iterates[i - 1], iterates[i - 2], factors[i - 1], b, dinv, coeffs, 3 + i, 16 + i, 1, SPAN)
    v = iterates[4]
    rim_s[0:20] = v.get(16, 21).reshape((20,) + TILE)
    copies = [pltpu.make_async_copy(rim_s.at[0:20], rim.at[0:20], sent.at[0])]
    copies[0].start()

    def residual(v, b, diag, coeffs, dup):
        return lambda p, q: (b.get(p, q) + couple(v, p, q, *coeffs, dup)) - diag.get(p, q) * v.get(p, q)

    b_one = Planes((4, b1_s), (8, b1))
    for p in range(4, PLANES1):
        b_one.put(p, 0.5 * restrict(residual(v, b, diag, coeffs, 1), p, p + 1, 1))
    coeffs, dinv, diag = one[:3], one[3], one[4]
    w, spare = Planes((0, w_a)), Planes((0, w_b))
    w.put(4, factors[0][1] * (b_one.get(4, PLANES1) * dinv.get(4, PLANES1)))
    close(w, PLANES1)
    w = smooth((None, w, spare), b_one, dinv, coeffs, factors[1:], 5, PLANES1, 2, SPAN1)
    b_two = 0.5 * restrict(residual(w, b_one, diag, coeffs, 2), 4, 6, 2)
    beta_two = 0.125 * restrict(Planes((8, beta1)).get, 4, 6, 2)
    alpha_two = 0.125 * restrict(Planes((8, alpha1)).get, 4, 6, 2)
    slot = lane % 4
    both = jnp.where(slot < 2, *(jnp.where(slot % 2 == 0, field[0, 0], field[1, 0]) for field in (b_two, beta_two)))
    last = jnp.where(slot % 2 == 0, alpha_two[0, 0], alpha_two[1, 0])
    last = jnp.where(slot[:4] < 2, last[:4], last[4:])
    for n in range(2):
        for i, part in enumerate((both[:4], both[4:], last)):
            tile_s[n, i] = part
    copies += [pltpu.make_async_copy(tile_s, gather.at[n : n + 2], sent.at[n + 1]) for n in range(0, COUNT, 2)]
    for copy in copies[1:]:
        copy.start()
    u1[...] = w.get(8, PLANES1)
    rim_s[20:28] = jnp.where(lane % 2 == 0, w.get(8, PLANES1), b_one.get(8, PLANES1)).reshape((8,) + TILE)
    copies.append(pltpu.make_async_copy(rim_s.at[20:28], rim.at[20:28], sent.at[COUNT + 1]))
    copies[-1].start()
    for copy in copies:
        copy.wait()


def down_pre(own):
    shapes = PRE_SHAPES + [(4, 2), (4, 2), (8, 4), (7, 4), (6, 4), (5, 4)]
    return call(pre_kernel, "down_pre", (own,), [shape_of(*n) for n in shapes], [scratch(1, 4), scratch(1, 2)])


def down_mid(own, even, odd, beta1, alpha1):
    return call(
        mid_kernel, "down_mid", (own, even, odd, beta1, alpha1), [shape_of(*n) for n in MID_SHAPES],
        [scratch(16, 4), scratch(16, 4), scratch(8, 2), scratch(8, 2)],
    )


def down_post(own, even, odd, pre, mid):
    shapes = [shape_of(*n) for n in ((RIM,), (12, 4), (13, 4), (4, 2), (4, 2))]
    return call(
        post_kernel, "down_post", (own, even, odd, *pre, *mid),
        [jax.ShapeDtypeStruct((COUNT, 3, 4, 128), jnp.float32), *shapes],
        [
            scratch(13, 4), scratch(13, 4), scratch(13, 4), scratch(4, 2), scratch(13, 2), scratch(13, 2),
            pltpu.VMEM((2, 3, 4, 128), jnp.float32), scratch(28), pltpu.SemaphoreType.DMA((COUNT + 2,)),
        ],
        hbm_outputs=2,
    )


def outer(value, half):
    turned = lanes(value, 64)
    before = jnp.concatenate([lanes(value[-1:], 65), turned[:-1]], axis=0)
    after = jnp.concatenate([turned[1:], lanes(value[:1], 63)], axis=0)
    return jnp.where(half == 0, before, after), turned


def coarse_kernel(gathered, out, tiles_s, e2_s):
    lane, row = lane_ids(), row_ids()
    half = lane // 64
    x, y, z = position()
    for n in range(COUNT):
        tiles_s[n, 0] = jnp.concatenate([gathered[n, 0], gathered[n, 1]], axis=0)
        tiles_s[n, 1] = jnp.concatenate([gathered[n, 2], lanes(gathered[n, 2], -2)], axis=0)

    def collect(tile, slot):
        out = []
        for group in range(8):
            joined = None
            for q in range(GZ):
                natural = 7 - group if q % 2 else group
                rank, core = natural // 2, natural % 2
                n = ((rank ^ (rank >> 1)) * GY + core) * GZ + q
                piece = tiles_s[n, tile] if q == slot else lanes(tiles_s[n, tile], q - slot)
                joined = piece if joined is None else jnp.where(lane % 4 == q, piece, joined)
            out.append(joined)
        return jnp.stack(out)

    b_two, beta_two, alpha_two = ([collect(tile, slot + p) for p in range(2)] for tile, slot in ((0, 0), (0, 2), (1, 0)))
    slab = lax.broadcasted_iota(jnp.int32, (8,) + TILE, 0)
    end = ((slab == 0) & (lane % 4 == 0) & (half == 0)) | ((slab == 7) & (lane % 4 == 3) & (half == 1))

    def sides(beta, dx, dy):
        x_last, x_first = row >= 8 - dx, row < dx
        place = (lane % 64) // dy
        y_last, y_first = place == 64 // dy - 1, place == 0
        by_x = jnp.where(x_last, 0.0, 0.5 * (beta + rows(beta, -dx)))
        by_y = jnp.where(y_last, 0.0, 0.5 * (beta + lanes(beta, -dy)))
        rim = jnp.where(x_last | x_first, 0.5, 0.0) + jnp.where(y_last | y_first, 0.5, 0.0)
        return by_x, by_y, (by_x + rows(by_x, dx)) + (by_y + lanes(by_y, dy)) + beta * rim

    def scaled(by_x, by_y, inv, dx, dy):
        return by_x * inv, rows(by_x, dx) * inv, by_y * inv, lanes(by_y, dy) * inv

    def flat(v, coeffs, dx, dy):
        x_above, x_below, y_above, y_below = coeffs
        total = x_above * rows(v, -dx) + x_below * rows(v, dx)
        return total + (y_above * lanes(v, -dy) + y_below * lanes(v, dy))

    x0, y0, s0 = sides(beta_two[0], 1, 4)
    x1, y1, s1 = sides(beta_two[1], 1, 4)
    middle = 0.5 * (beta_two[0] + beta_two[1])
    inner = 0.5 * (beta_two[1] + lanes(beta_two[1], 64))
    edge = 0.5 * (beta_two[0] + jnp.where(end, 0.0, outer(beta_two[0], half)[0]))
    shift = SHIFT_BASE * 16.0
    diag_a = shift * alpha_two[0] + s0 + (middle + edge)
    diag_b = shift * alpha_two[1] + s1 + (middle + inner)
    inv_a, inv_b = inverse(diag_a), inverse(diag_b)
    flat_a, flat_b = scaled(x0, y0, inv_a, 1, 4), scaled(x1, y1, inv_b, 1, 4)
    middle_a, middle_b = middle * inv_a, middle * inv_b
    rim_a, inner_b = jnp.where(end, 0.0, edge) * inv_a, inner * inv_b
    rhs_a, rhs_b = b_two[0] * inv_a, b_two[1] * inv_b

    def apply_two(va, vb):
        ta = flat(va, flat_a, 1, 4) + (middle_a * vb + rim_a * outer(va, half)[0])
        tb = flat(vb, flat_b, 1, 4) + (middle_b * va + inner_b * lanes(vb, 64))
        return ta, tb

    def sweeps_two(before, now, factors):
        for carry, gain in factors:
            totals = apply_two(*now)
            new = []
            for v, old, rhs, total in zip(now, before or (None, None), (rhs_a, rhs_b), totals):
                base = (1.0 + carry - gain) * v + gain * rhs
                if carry != 0.0 and old is not None:
                    base = base - carry * old
                new.append(base + gain * total)
            before, now = now, new
        return now

    factors = chebyshev_factors(SWEEPS, SMOOTH_LOWER)
    ua, ub = sweeps_two(None, (factors[0][1] * rhs_a, factors[0][1] * rhs_b), factors[1:])
    ta, tb = apply_two(ua, ub)

    def restrict_whole(first, second):
        total = first + second
        total = total + jnp.where(row % 2 == 0, rows(total, -1), rows(total, 1))
        return total + jnp.where((lane // 4) % 2 == 0, lanes(total, -4), lanes(total, 4))

    b_low = 0.5 * restrict_whole(diag_a * (rhs_a + ta - ua), diag_b * (rhs_b + tb - ub))
    beta_low = 0.125 * restrict_whole(beta_two[0], beta_two[1])
    alpha_low = 0.125 * restrict_whole(alpha_two[0], alpha_two[1])

    x_low, y_low, s_low = sides(beta_low, 2, 8)
    beyond, turned = outer(beta_low, half)
    inner_low = 0.5 * (beta_low + turned)
    edge_low = 0.5 * (beta_low + jnp.where(end, 0.0, beyond))
    inv_low = inverse(SHIFT_BASE * 64.0 * alpha_low + s_low + (inner_low + edge_low))
    flat_low = scaled(x_low, y_low, inv_low, 2, 8)
    rim_low = jnp.where(end, 0.0, edge_low) * inv_low
    inner_low = inner_low * inv_low
    rhs_low = b_low * inv_low
    before = v = None
    for carry, gain in chebyshev_factors(BOTTOM, BOTTOM_LOWER):
        if v is None:
            v = gain * rhs_low
            continue
        beyond, turned = outer(v, half)
        base = (1.0 + carry - gain) * v + gain * rhs_low
        if before is not None:
            base = base - carry * before
        total = flat(v, flat_low, 2, 8) + (inner_low * turned + rim_low * beyond)
        before, v = v, base + gain * total
    va, vb = sweeps_two(None, (ua + v, ub + v), factors)
    for group in range(8):
        e2_s[group, 0] = va[group]
        e2_s[group, 1] = vb[group]

    chunk = chunk_of(x, y, z)
    place = 8 * z + chunk

    def fetch(offset):
        index = jnp.clip(place + offset, 0, 8 * GZ - 1)
        out = []
        for p in range(2):
            tile = pltpu.roll(e2_s[index % 8, p], (128 - index // 8) % 128, 1)
            tile = jnp.where(lane % 4 == 0, tile, 0.0)
            tile = tile + lanes(tile, 1)
            out.append(tile + lanes(tile, 2))
        return out

    below, here, above = fetch(-1), fetch(0), fetch(1)
    first = half == 0
    out[0] = jnp.where(first, below[0], above[0])
    out[1] = jnp.where(first, below[1], above[1])
    out[2] = lanes(jnp.where(first, above[1], below[1]), 64)
    out[3] = lanes(jnp.where(first, above[0], below[0]), 64)
    out[4] = here[0]
    out[5] = here[1]


def coarse(gathered):
    vmem = pl.BlockSpec(memory_space=pltpu.VMEM)
    return pl.pallas_call(
        coarse_kernel,
        out_shape=shape_of(6),
        in_specs=[vmem],
        out_specs=vmem,
        scratch_shapes=[scratch(COUNT, 2), scratch(8, 2)],
        compiler_params=pltpu.CompilerParams(vmem_limit_bytes=8 * 2**20),
        name="coarse",
    )(gathered)


def up_kernel(e_two, rim_even, rim_odd, own, halo_b, late, u1, b1, v4, *refs):
    pre, mid, (out, v_a, v_b, w_a, w_b, bx_s) = refs[:10], refs[10:20], refs[20:]
    zero, one = coefficient_planes(pre, mid)
    lane, row = lane_ids(), row_ids()
    _, from_even = halo_masks()
    factors = chebyshev_factors(SWEEPS, SMOOTH_LOWER)

    for p in range(1, 8):
        if p >= 4:
            k = 7 - p
            both = lanes(jnp.where(from_even, rim_odd[20 + 2 * k : 22 + 2 * k], rim_even[20 + 2 * k : 22 + 2 * k]), 64)
        else:
            both = jnp.where(from_even, rim_even[20 + 2 * p : 22 + 2 * p], rim_odd[20 + 2 * p : 22 + 2 * p])
        w_a[p] = jnp.where(lane % 2 == 0, both, lanes(both, 1)) + e_two[p // 2]
        if p >= 2:
            bx_s[p] = jnp.where(lane % 2 == 0, lanes(both, -1), both)
    for p in range(8, PLANES1):
        w_a[p] = u1[p - 8] + e_two[p // 2]
    w_a[PLANES1] = lanes(w_a[PLANES1 - 1], 64)
    pair = (Planes((0, w_b)), Planes((0, w_a)), None)
    w = smooth(pair, Planes((0, bx_s), (8, b1)), one[3], one[:3], factors, 2, PLANES1, 2, SPAN1)

    for p in range(11, PLANES):
        if p >= 16:
            start = Planes((7, late), (20, v4)).get(p, p + 1)[0]
        else:
            k = 4 * (15 - p)
            start = lanes(jnp.where(from_even, rim_odd[k : k + 4], rim_even[k : k + 4]), 64)
        e_one = w.get(p // 2, p // 2 + 1)[0]
        e_one = jnp.concatenate([e_one[:1], e_one[:1], e_one[1:], e_one[1:]], axis=0)
        v_a[p] = start + e_one
    v_a[PLANES] = lanes(v_a[PLANES - 1], 64)
    b, diag, coeffs = Planes((4, halo_b), (16, own.at[2])), zero[4], zero[:3]
    v = smooth((Planes((0, v_b)), Planes((0, v_a)), None), b, zero[3], coeffs, factors, 12, PLANES, 1, SPAN)
    low = (lane // 32) % 2 == 0
    for k in range(4):
        for o in range(2):
            parts = []
            for pp in range(2):
                p = 16 + k + 4 * pp
                value = v.get(p, p + 1)
                if o == 1:
                    value = (b.get(p, p + 1) + couple(v, p, p + 1, *coeffs, 1)) - diag.get(p, p + 1) * value
                parts.append(regroup([value[0, i] for i in range(4)], 0, 2, row))
            for i in range(GX):
                one, two = parts[0][i], parts[1][i]
                out[2 * i, pl.ds(o * 32 + k * 8, 8), :] = jnp.where(low, one, lanes(two, 32))
                out[2 * i + 1, pl.ds(o * 32 + k * 8, 8), :] = jnp.where(low, lanes(one, -32), two)


def up(*operands):
    return call(
        up_kernel, "up_strokes", operands, [jax.ShapeDtypeStruct((8, 64, 128), jnp.float32)],
        [scratch(25, 4), scratch(25, 4), scratch(13, 2), scratch(13, 2), scratch(8, 2)],
    )[0]


def unpack_kernel(in_ref, v_ref, r_ref, fields, turned, staged, left):
    z = lax.axis_index("gz")
    lane = lane_ids()
    for x in range(GX):
        for y in range(GY):
            start = pl.multiple_of(chunk_of(x, y, z) * 64, 64)
            staged[pl.ds(start, 64), :] = in_ref[x * GY + y]
    copies = [pltpu.make_async_copy(fields.at[o], ref, left.at[o]) for o, ref in enumerate((v_ref, r_ref))]
    for o, copy in enumerate(copies):
        for xg in range(2):
            slot = turned.at[2 * o + xg]
            for k in range(4):
                tiles = [staged[pl.ds(o * 32 + k * 8 + 2 * x4 + xg, 8, stride=64), :] for x4 in range(4)]
                for g, tile in enumerate(regroup(tiles, 1, 32, lane)):
                    slot[pl.ds(depth_of(k, g), 8, stride=16), :] = tile
            fields[o, 4 * xg : 4 * xg + 4] = slot[...].T.reshape(4, 32, 128)
        copy.start()
    for copy in copies:
        copy.wait()


def unpack(received):
    vmem = pl.BlockSpec(memory_space=pltpu.VMEM)
    return pl.pallas_call(
        unpack_kernel,
        out_shape=[jax.ShapeDtypeStruct(BLOCK, jnp.float32)] * 2,
        in_specs=[vmem],
        out_specs=[pl.BlockSpec(memory_space=pltpu.HBM)] * 2,
        scratch_shapes=[
            pltpu.VMEM((2,) + BLOCK, jnp.float32),
            pltpu.VMEM((4, 128, 128), jnp.float32),
            pltpu.VMEM((512, 128), jnp.float32),
            pltpu.SemaphoreType.DMA((2,)),
        ],
        compiler_params=pltpu.CompilerParams(vmem_limit_bytes=4 * 2**20),
        name="unpack",
    )(received)


def slab_shards(right_side, alpha_coef, beta_coef):
    even_pairs, odd_pairs = swap_pairs(False), swap_pairs(True)
    packed = pack(jnp.stack([alpha_coef, beta_coef, right_side]))
    own, to_even, to_odd = to_slab(lax.all_to_all(packed, RING, 0, 0))
    even = lax.ppermute(to_even, ALL, even_pairs)
    odd = lax.ppermute(to_odd, ALL, odd_pairs)
    found = down_pre(own)
    pre, alpha1, beta1, v4 = found[:10], found[10], found[11], found[15]
    mid = down_mid(own, even, odd, beta1, alpha1)
    gather, rim, halo_b, late, u1, b1 = down_post(own, even, odd, found, mid)
    rim_even = lax.ppermute(rim, ALL, even_pairs)
    rim_odd = lax.ppermute(rim, ALL, odd_pairs)
    kept = (own, halo_b, late, u1, b1, v4, *pre, *mid)
    result = up(coarse(lax.all_to_all(gather, ALL, 0, 0)), rim_even, rim_odd, *kept)
    return tuple(unpack(lax.all_to_all(result, RING, 0, 0)))


def solution(mesh):
    spec = P("gx", "gy", "gz")
    plain = jax.shard_map(shards, mesh=mesh, in_specs=(spec,) * 3, out_specs=(spec,) * 2, check_vma=False)
    slabs = jax.shard_map(slab_shards, mesh=mesh, in_specs=(spec,) * 3, out_specs=(spec,) * 2, check_vma=False)
    sizes = tuple(mesh.shape[axis] for axis in ALL)

    def run(right_side, alpha_coef, beta_coef):
        block = tuple(n // size for n, size in zip(right_side.shape, sizes))
        fits = sizes == (GX, GY, GZ) and block == BLOCK
        return (slabs if fits else plain)(right_side, alpha_coef, beta_coef)

    return run
```

```python
import jax
import jax.numpy as jnp
from jax import lax
from jax.experimental import pallas as pl
from jax.experimental.pallas import tpu as pltpu
from jax.sharding import PartitionSpec as P

LEVELS = 3
SWEEPS = 4
BOTTOM = 12


SHIFT_BASE = 0.01
UPPER_EIG = 2.0
SMOOTH_LOWER = 0.25
BOTTOM_LOWER = 0.02


def with_halo(block, sides, width):
    for axis, dim in sides:
        count = lax.axis_size(axis)
        forward = [(i, i + 1) for i in range(count - 1)]
        backward = [(target, source) for source, target in forward]
        low = lax.ppermute(
            lax.slice_in_dim(block, block.shape[dim] - width, None, axis=dim), axis, forward
        )
        high = lax.ppermute(lax.slice_in_dim(block, 0, width, axis=dim), axis, backward)
        block = jnp.concatenate([low, block, high], axis=dim)
    return block


def partner_2(array, axis, distance):
    return lax.ppermute(array, axis, [(i, i ^ 1 << distance) for i in range(lax.axis_size(axis))])


def split_padded(padded):
    return (
        padded[:-2, 1:-1, 1:-1],
        padded[2:, 1:-1, 1:-1],
        padded[1:-1, :-2, 1:-1],
        padded[1:-1, 2:, 1:-1],
        padded[1:-1, 1:-1, :-2],
        padded[1:-1, 1:-1, 2:],
    )


def zero_pad(field):
    return jnp.pad(field, 1)


def rim_iterate(field):
    return with_halo(field, (("gx", 0), ("gy", 1), ("gz", 2)), 1)


def rim_coefficient(field):
    return with_halo(field, (("gx", 0), ("gy", 1), ("gz", 2)), 1)


def level_operator(beta_level, alpha_level, padded_beta, shift):
    coeffs = tuple((0.5 * (beta_level + other) for other in split_padded(padded_beta)))
    diagonal = shift * alpha_level
    for coeff in coeffs:
        diagonal = diagonal + coeff
    return (coeffs, diagonal)


def apply_operator(field, operator, pad_field):
    coeffs, diagonal = operator
    others = split_padded(pad_field(field))
    total = coeffs[0] * others[0]
    for index in range(1, 6):
        total = total + coeffs[index] * others[index]
    return diagonal * field - total


def chebyshev(iterate, rhs_level, operator, count, lower, zero_start, pad_field):
    diagonal = operator[1]
    center = (UPPER_EIG + lower) / 2.0
    half_width = (UPPER_EIG - lower) / 2.0
    sigma_ratio = center / half_width
    rho_old = 1.0 / sigma_ratio
    if zero_start:
        remain = rhs_level
    else:
        remain = rhs_level - apply_operator(iterate, operator, pad_field)
    update = remain / diagonal / center
    iterate = iterate + update
    for sweep_index in range(count - 1):
        remain = rhs_level - apply_operator(iterate, operator, pad_field)
        rho_new = 1.0 / (2.0 * sigma_ratio - rho_old)
        update = rho_new * rho_old * update + 2.0 * rho_new / half_width * (remain / diagonal)
        iterate = iterate + update
        rho_old = rho_new
    return iterate


def restrict_mean(field):
    first, second, third = field.shape
    blocks = field.reshape(first // 2, 2, second // 2, 2, third // 2, 2)
    return jnp.sum(blocks, axis=(1, 3, 5)) * 0.125


def prolong_copy(field):
    return jnp.repeat(jnp.repeat(jnp.repeat(field, 2, axis=0), 2, axis=1), 2, axis=2)


def join_partner(packed, partner, device_index, bit_index, dim):
    position = device_index // 2**bit_index % 2
    lower_first = jnp.concatenate([packed, partner], axis=dim)
    upper_first = jnp.concatenate([partner, packed], axis=dim)
    return jnp.where(position == 0, lower_first, upper_first)


def shards(right_side, alpha_coef, beta_coef):
    betas = [beta_coef]
    alphas = [alpha_coef]
    for level in range(LEVELS):
        betas.append(restrict_mean(betas[-1]))
        alphas.append(restrict_mean(alphas[-1]))
    operators = []
    for level in range(LEVELS):
        padded_beta = rim_coefficient(betas[level])
        operators.append(
            level_operator(betas[level], alphas[level], padded_beta, SHIFT_BASE * 4.0**level)
        )
    rhs_levels = [right_side]
    smoothed = []
    for level in range(LEVELS):
        iterate = chebyshev(
            jnp.zeros_like(rhs_levels[level]),
            rhs_levels[level],
            operators[level],
            SWEEPS,
            SMOOTH_LOWER,
            True,
            rim_iterate,
        )
        remain = rhs_levels[level] - apply_operator(iterate, operators[level], rim_iterate)
        smoothed.append(iterate)
        rhs_levels.append(4.0 * restrict_mean(remain))
    coarse_rhs = rhs_levels[LEVELS]
    local_shape = coarse_rhs.shape
    packed = jnp.stack([coarse_rhs, betas[LEVELS], alphas[LEVELS]])
    index_x = lax.axis_index("gx")
    index_y = lax.axis_index("gy")
    index_z = lax.axis_index("gz")
    for bit_index in range(lax.axis_size("gx").bit_length() - 1):
        partner = partner_2(packed, "gx", bit_index)
        packed = join_partner(packed, partner, index_x, bit_index, 1)
    for bit_index in range(lax.axis_size("gy").bit_length() - 1):
        partner = partner_2(packed, "gy", bit_index)
        packed = join_partner(packed, partner, index_y, bit_index, 2)
    for bit_index in range(lax.axis_size("gz").bit_length() - 1):
        partner = partner_2(packed, "gz", bit_index)
        packed = join_partner(packed, partner, index_z, bit_index, 3)
    whole_rhs = packed[0]
    whole_beta = packed[1]
    whole_alpha = packed[2]
    bottom_operator = level_operator(
        whole_beta, whole_alpha, zero_pad(whole_beta), SHIFT_BASE * 4.0**LEVELS
    )
    whole_correction = chebyshev(
        jnp.zeros_like(whole_rhs), whole_rhs, bottom_operator, BOTTOM, BOTTOM_LOWER, True, zero_pad
    )
    starts = (index_x * local_shape[0], index_y * local_shape[1], index_z * local_shape[2])
    correction = lax.dynamic_slice(whole_correction, starts, local_shape)
    for level in range(LEVELS - 1, -1, -1):
        start_field = smoothed[level] + prolong_copy(correction)
        correction = chebyshev(
            start_field,
            rhs_levels[level],
            operators[level],
            SWEEPS,
            SMOOTH_LOWER,
            False,
            rim_iterate,
        )
    residual_field = right_side - apply_operator(correction, operators[0], rim_iterate)
    return (correction, residual_field)


GX, GY, GZ = 4, 2, 4
COUNT = GX * GY * GZ
RIM = 28
BLOCK = (8, 32, 128)
RING = ("gx", "gy")
ALL = ("gx", "gy", "gz")
TILE = (8, 128)
PLANES = 24
PLANES1 = 12
SPAN, SPAN1, COEF_SPAN, COEF_SPAN1 = 2, 4, 2, 4


def chunk_of(x, y, z):
    natural = 2 * (x ^ (x >> 1)) + y
    return natural + (z % 2) * (7 - 2 * natural)


def position():
    return lax.axis_index("gx"), lax.axis_index("gy"), lax.axis_index("gz")


def swap_pairs(odd):
    place = {}
    for x in range(GX):
        for y in range(GY):
            for z in range(GZ):
                place[8 * z + chunk_of(x, y, z)] = (x * GY + y) * GZ + z
    count = len(place)
    if odd:
        pairs = [(i, i + 1) for i in range(1, count - 1, 2)]
    else:
        pairs = [(i, i + 1) for i in range(0, count, 2)]
    return [(place[a], place[b]) for a, b in pairs] + [(place[b], place[a]) for a, b in pairs]


def lane_ids():
    return lax.broadcasted_iota(jnp.int32, TILE, 1)


def row_ids():
    return lax.broadcasted_iota(jnp.int32, TILE, 0)


def lanes(value, shift):
    return pltpu.roll(value, shift % 128, value.ndim - 1)


def rows(value, shift):
    return pltpu.roll(value, shift % 8, value.ndim - 2)


def regroup(tiles, axis, width, ids):
    move = lanes if axis == 1 else rows
    group = ids // width % 4
    odd, upper = group % 2 == 1, group >= 2
    a, b, c, d = tiles
    turned = move(jnp.where(odd, a, b), width)
    a, b = jnp.where(odd, turned, a), jnp.where(odd, b, turned)
    turned = move(jnp.where(odd, c, d), width)
    c, d = jnp.where(odd, turned, c), jnp.where(odd, d, turned)
    turned = move(jnp.where(upper, a, c), 2 * width)
    a, c = jnp.where(upper, turned, a), jnp.where(upper, c, turned)
    turned = move(jnp.where(upper, b, d), 2 * width)
    own = jnp.where(upper, d, b)
    inner = odd != upper
    return [a, jnp.where(inner, own, turned), c, jnp.where(inner, turned, own)]


def depth_of(k, group):
    half, part = group // 2, group % 2
    plane = k + 4 * part
    return 15 - plane if half else plane


def pack_kernel(fields, out_ref, turned, staged):
    z = lax.axis_index("gz")
    lane = lane_ids()
    for a in range(3):
        for xg in range(2):
            slot = turned.at[2 * a + xg]
            slot[...] = fields[a, 4 * xg : 4 * xg + 4].reshape(128, 128).T
            for k in range(4):
                tiles = [slot[pl.ds(depth_of(k, g), 8, stride=16), :] for g in range(4)]
                for x4, tile in enumerate(regroup(tiles, 1, 32, lane)):
                    staged[pl.ds(a * 32 + k * 8 + 2 * x4 + xg, 8, stride=96), :] = tile
    for x in range(GX):
        for y in range(GY):
            start = pl.multiple_of(chunk_of(x, y, z) * 96, 96)
            out_ref[x * GY + y] = staged[pl.ds(start, 96), :]


def pack(fields):
    return pl.pallas_call(
        pack_kernel,
        out_shape=jax.ShapeDtypeStruct((8, 96, 128), jnp.float32),
        in_specs=[pl.BlockSpec(memory_space=pltpu.VMEM)],
        out_specs=pl.BlockSpec(memory_space=pltpu.VMEM),
        scratch_shapes=[pltpu.VMEM((6, 128, 128), jnp.float32), pltpu.VMEM((768, 128), jnp.float32)],
        compiler_params=pltpu.CompilerParams(vmem_limit_bytes=4 * 2**20),
        name="pack",
    )(fields)


def shape_of(*dims):
    return jax.ShapeDtypeStruct(dims + TILE, jnp.float32)


def scratch(*dims):
    return pltpu.VMEM(dims + TILE, jnp.float32)


def halo_masks():
    x, y, z = position()
    chunk = chunk_of(x, y, z)
    half = lane_ids() // 64
    return chunk, (half + chunk % 2) == 1


PLACE = [(r, True) for r in range(6)] + [(4, False), (5, False), (3, False), (2, False), (1, False), (0, False)]
PLACE += [(6, False), (6, True)]
FIRST_TILE = (0, 6, 13)
MESSAGE = 19


def message(planes, near, count):
    tiles = [jnp.where(near, planes[t], planes[t + 4]) for t in range(4)]
    tiles += [jnp.where(near, planes[t], lanes(planes[t + 2], 64)) for t in (4, 5)]
    if count == 7:
        tiles.append(jnp.where(near, lanes(planes[2], 64), planes[3]))
    return tiles


def halo_plane(even, odd, a, r, from_even):
    tile, moved = PLACE[r]
    tile = FIRST_TILE[a] + tile
    if moved:
        return lanes(jnp.where(from_even, odd[tile], even[tile]), 64)
    return jnp.where(from_even, even[tile], odd[tile])


def slab_kernel(in_ref, out_ref, even_ref, odd_ref):
    lane, row = lane_ids(), row_ids()
    low = (lane // 32) % 2 == 0
    _, from_even = halo_masks()
    for a in range(3):
        planes = [None] * 8
        for k in range(4):
            part = ([], [])
            for x in range(GX):
                first = in_ref[2 * x, pl.ds(a * 32 + k * 8, 8), :]
                second = in_ref[2 * x + 1, pl.ds(a * 32 + k * 8, 8), :]
                part[0].append(jnp.where(low, first, lanes(second, 32)))
                part[1].append(jnp.where(low, lanes(first, -32), second))
            for pp in range(2):
                planes[k + 4 * pp] = jnp.stack(regroup(part[pp], 0, 2, row))
                out_ref[a, k + 4 * pp] = planes[k + 4 * pp]
        count = 7 if a == 1 else 6
        for near, ref in ((from_even, even_ref), (~from_even, odd_ref)):
            for t, tile in enumerate(message(planes, near, count)):
                ref[FIRST_TILE[a] + t] = tile


def to_slab(received):
    vmem = pl.BlockSpec(memory_space=pltpu.VMEM)
    return pl.pallas_call(
        slab_kernel,
        out_shape=[shape_of(3, 8, 4), shape_of(MESSAGE, 4), shape_of(MESSAGE, 4)],
        in_specs=[vmem],
        out_specs=[vmem] * 3,
        compiler_params=pltpu.CompilerParams(vmem_limit_bytes=4 * 2**20),
        name="to_slab",
    )(received)


class Planes:
    def __init__(self, *segments):
        self.segments = [(first, first + ref.shape[0], ref) for first, ref in segments]

    def find(self, p, q):
        for first, last, ref in self.segments:
            low, high = max(p, first), min(q, last)
            if low < high:
                yield low, high, ref, slice(low - first, high - first)

    def get(self, p, q):
        pieces = [ref[place] for _, _, ref, place in self.find(p, q)]
        return pieces[0] if len(pieces) == 1 else jnp.concatenate(pieces, axis=0)

    def put(self, p, value):
        for low, high, ref, place in self.find(p, p + value.shape[0]):
            ref[place] = value[low - p : high - p]


def spans(first, last, size):
    return [(p, min(p + size, last)) for p in range(first, last, size)]


def x_up(value):
    return jnp.concatenate([value[:, 1:], rows(value[:, :1], -1)], axis=1)


def x_down(value):
    return jnp.concatenate([rows(value[:, -1:], 1), value[:, :-1]], axis=1)


def couple(v, p, q, cx, cy, cz, dup):
    here, by_x, by_y = v.get(p, q), cx.get(p, q), cy.get(p, q)
    total = by_x * x_up(here) + x_down(by_x * here)
    total = total + (by_y * lanes(here, -dup) + lanes(by_y * here, dup))
    return total + (cz.get(p, q) * v.get(p - 1, q - 1) + cz.get(p + 1, q + 1) * v.get(p + 1, q + 1))


def chebyshev_factors(count, lower):
    center = (UPPER_EIG + lower) / 2.0
    half_width = (UPPER_EIG - lower) / 2.0
    ratio = center / half_width
    old = 1.0 / ratio
    out = [(0.0, 1.0 / center)]
    for _ in range(count - 1):
        new = 1.0 / (2.0 * ratio - old)
        out.append((new * old, 2.0 * new / half_width))
        old = new
    return out


def sweep(new, now, before, factor, b, dinv, coeffs, p, q, dup, size):
    carry, gain = factor
    for p, q in spans(p, q, size):
        base = (1.0 + carry - gain) * now.get(p, q)
        if carry != 0.0 and before is not None:
            base = base - carry * before.get(p, q)
        new.put(p, (b.get(p, q) + couple(now, p, q, *coeffs, dup)) * (gain * dinv.get(p, q)) + base)


def close(v, last):
    v.put(last, lanes(v.get(last - 1, last), 64))


def smooth(pair, b, dinv, coeffs, factors, first, last, dup, size):
    before, now, spare = pair
    for number, factor in enumerate(factors):
        new = spare if before is None else before
        sweep(new, now, before, factor, b, dinv, coeffs, first + number, last, dup, size)
        close(new, last)
        before, now = now, new
    return now


def inverse(value):
    guess = pl.reciprocal(value, approx=True)
    return guess * (2.0 - value * guess)


def level_coefficients(beta, alpha, first, last, shift, dup, cx, cy, cz, dinv, diag, ends, seam, size):
    lane, row = lane_ids(), row_ids()
    y_last = (lane % 64) // dup == 64 // dup - 1
    y_first = (lane % 64) // dup == 0
    x_rim = jnp.where(row == 0, 0.5, 0.0), jnp.where(row == 7, 0.5, 0.0)
    for p, q in spans(first, last, size):
        here = beta.get(p, q)
        by_x = 0.5 * (here + x_up(here))
        by_x = jnp.concatenate([by_x[:, :-1], jnp.where(row == 7, 0.0, by_x[:, -1:])], axis=1)
        above = jnp.where(y_last, 0.0, lanes(here, -dup))
        below = jnp.where(y_first, 0.0, lanes(here, dup))
        by_y = jnp.where(y_last, 0.0, 0.5 * (here + above))
        face = 0.5 * (beta.get(p - 1, q - 1) + here)
        total = shift * alpha.get(p, q) + (by_x + x_down(by_x)) + (here + 0.5 * (above + below))
        total = total + (face + 0.5 * (here + beta.get(p + 1, q + 1)))
        groups = [total[:, i : i + 1] for i in range(total.shape[1])]
        groups[0] = groups[0] + here[:, :1] * x_rim[0]
        groups[-1] = groups[-1] + here[:, -1:] * x_rim[1]
        total = jnp.concatenate(groups, axis=1)
        cx.put(p, by_x)
        cy.put(p, by_y)
        cz.put(p, face)
        diag.put(p, total)
        dinv.put(p, inverse(jnp.where(total > 0.0, total, 1.0)))
    if first <= seam < last:
        cz.put(seam, cz.get(seam, seam + 1) * ends)
    else:
        cz.put(last, 0.5 * (beta.get(last - 1, last) + beta.get(last, last + 1)))


def restrict_pair(first, second, dup):
    lane = lane_ids()
    total = first + second
    total = jnp.concatenate([total[:, i : i + 1] + total[:, i + 1 : i + 2] for i in range(0, total.shape[1], 2)], axis=1)
    return total + jnp.where((lane // dup) % 2 == 0, lanes(total, -dup), lanes(total, dup))


def restrict(take, p, q, dup):
    fine = take(2 * p, 2 * q)
    fine = fine.reshape((q - p, 2) + fine.shape[1:])
    return restrict_pair(fine[:, 0], fine[:, 1], dup)


def ends_factor():
    x, y, z = position()
    slab = 8 * z + chunk_of(x, y, z)
    half = lane_ids() // 64
    end = ((half == 0) & (slab == 0)) | ((half == 1) & (slab == 8 * GZ - 1))
    return jnp.where(end, 0.0, 1.0)


def call(kernel, name, operands, out_shape, scratch_shapes, hbm_outputs=0):
    vmem = pl.BlockSpec(memory_space=pltpu.VMEM)
    return pl.pallas_call(
        kernel,
        out_shape=out_shape,
        in_specs=[vmem] * len(operands),
        out_specs=[pl.BlockSpec(memory_space=pl.ANY)] * hbm_outputs + [vmem] * (len(out_shape) - hbm_outputs),
        scratch_shapes=scratch_shapes,
        compiler_params=pltpu.CompilerParams(vmem_limit_bytes=16 * 2**20),
        name=name,
    )(*operands)


PRE_SHAPES = [(7, 4), (7, 4), (8, 4), (7, 4), (7, 4), (3, 2), (3, 2), (4, 2), (3, 2), (3, 2)]
MID_SHAPES = [(13, 4)] * 5 + [(7, 2)] * 5


def coefficient_planes(pre, mid):
    zero = [Planes(*([(4, mid[i])] if mid else []), *([(17, pre[i])] if pre else [])) for i in range(5)]
    one = [Planes(*([(2, mid[i])] if mid else []), *([(9, pre[i])] if pre else [])) for i in range(5, 10)]
    return zero, one


def pre_kernel(own, *refs):
    pre, (alpha1, beta1, v1, v2, v3, v4), (ghost, ghost1) = refs[:10], refs[10:16], refs[16:]
    zero, one = coefficient_planes(pre, None)
    alpha, beta = Planes((16, own.at[0])), Planes((16, own.at[1]), (24, ghost))
    alpha_one, beta_one = Planes((8, alpha1)), Planes((8, beta1), (12, ghost1))
    close(beta, PLANES)
    level_coefficients(beta, alpha, 17, PLANES, SHIFT_BASE, 1, *zero, None, 16, COEF_SPAN)
    beta_one.put(8, 0.125 * restrict(beta.get, 8, PLANES1, 1))
    alpha_one.put(8, 0.125 * restrict(alpha.get, 8, PLANES1, 1))
    close(beta_one, PLANES1)
    level_coefficients(beta_one, alpha_one, 9, PLANES1, SHIFT_BASE * 4.0, 2, *one, None, 8, COEF_SPAN1)
    b, coeffs, dinv = Planes((16, own.at[2])), zero[:3], zero[3]
    factors = chebyshev_factors(SWEEPS, SMOOTH_LOWER)
    iterates = [None, Planes((17, v1)), Planes((18, v2)), Planes((19, v3)), Planes((20, v4))]
    for p, q in spans(17, PLANES, 4):
        iterates[1].put(p, factors[0][1] * (b.get(p, q) * dinv.get(p, q)))
    close(iterates[1], PLANES)
    for i in range(2, 5):
        sweep(iterates[i], iterates[i - 1], iterates[i - 2], factors[i - 1], b, dinv, coeffs, 16 + i, PLANES, 1, SPAN)
        close(iterates[i], PLANES)


def mid_part(own, even, odd, beta1_own, alpha1_own, mid, beta_s, alpha_s, beta1_s, alpha1_s):
    _, from_even = halo_masks()
    zero, one = coefficient_planes(None, mid)
    for p in range(2, 16):
        beta_s[p] = halo_plane(even, odd, 1, 15 - p, from_even)
        if p >= 4:
            alpha_s[p] = halo_plane(even, odd, 0, 15 - p, from_even)
    beta, alpha = Planes((0, beta_s), (16, own.at[1])), Planes((0, alpha_s), (16, own.at[0]))
    ends = ends_factor()
    level_coefficients(beta, alpha, 4, 17, SHIFT_BASE, 1, *zero, ends, 16, COEF_SPAN)
    beta_one, alpha_one = Planes((0, beta1_s), (8, beta1_own)), Planes((0, alpha1_s), (8, alpha1_own))
    for p in range(1, 8):
        beta_one.put(p, 0.125 * restrict(beta.get, p, p + 1, 1))
        if p >= 2:
            alpha_one.put(p, 0.125 * restrict(alpha.get, p, p + 1, 1))
    level_coefficients(beta_one, alpha_one, 2, 9, SHIFT_BASE * 4.0, 2, *one, ends, 8, COEF_SPAN1)


def post_kernel(own, even, odd, *refs):
    pre, (alpha1, beta1, v1, v2, v3, v4), (gather, rim, halo_b, late, u1, b1) = refs[:10], refs[10:16], refs[16:22]
    mid, (f1, f2, f3, b1_s, w_a, w_b, tile_s, rim_s, sent), scratch_mid = refs[22:32], refs[32:41], refs[41:]
    mid_part(own, even, odd, beta1, alpha1, mid, *scratch_mid)
    lane = lane_ids()
    _, from_even = halo_masks()
    zero, one = coefficient_planes(pre, mid)
    coeffs, dinv, diag = zero[:3], zero[3], zero[4]
    b = Planes((4, halo_b), (16, own.at[2]))
    for p in range(4, 16):
        b.put(p, halo_plane(even, odd, 2, 15 - p, from_even)[None])
    factors = chebyshev_factors(SWEEPS, SMOOTH_LOWER)
    iterates = [
        None,
        Planes((4, f1), (17, v1)),
        Planes((5, f2), (18, v2)),
        Planes((6, f3), (19, v3)),
        Planes((7, late), (20, v4)),
    ]
    for p, q in spans(4, 17, 4):
        iterates[1].put(p, factors[0][1] * (b.get(p, q) * dinv.get(p, q)))
    for i in range(2, 5):
        sweep(iterates[i], iterates[i - 1], iterates[i - 2], factors[i - 1], b, dinv, coeffs, 3 + i, 16 + i, 1, SPAN)
    v = iterates[4]
    rim_s[0:20] = v.get(16, 21).reshape((20,) + TILE)
    copies = [pltpu.make_async_copy(rim_s.at[0:20], rim.at[0:20], sent.at[0])]
    copies[0].start()

    def residual(v, b, diag, coeffs, dup):
        return lambda p, q: (b.get(p, q) + couple(v, p, q, *coeffs, dup)) - diag.get(p, q) * v.get(p, q)

    b_one = Planes((4, b1_s), (8, b1))
    for p in range(4, PLANES1):
        b_one.put(p, 0.5 * restrict(residual(v, b, diag, coeffs, 1), p, p + 1, 1))
    coeffs, dinv, diag = one[:3], one[3], one[4]
    w, spare = Planes((0, w_a)), Planes((0, w_b))
    w.put(4, factors[0][1] * (b_one.get(4, PLANES1) * dinv.get(4, PLANES1)))
    close(w, PLANES1)
    w = smooth((None, w, spare), b_one, dinv, coeffs, factors[1:], 5, PLANES1, 2, SPAN1)
    b_two = 0.5 * restrict(residual(w, b_one, diag, coeffs, 2), 4, 6, 2)
    beta_two = 0.125 * restrict(Planes((8, beta1)).get, 4, 6, 2)
    alpha_two = 0.125 * restrict(Planes((8, alpha1)).get, 4, 6, 2)
    slot = lane % 4
    both = jnp.where(slot < 2, *(jnp.where(slot % 2 == 0, field[0, 0], field[1, 0]) for field in (b_two, beta_two)))
    last = jnp.where(slot % 2 == 0, alpha_two[0, 0], alpha_two[1, 0])
    last = jnp.where(slot[:4] < 2, last[:4], last[4:])
    for n in range(2):
        for i, part in enumerate((both[:4], both[4:], last)):
            tile_s[n, i] = part
    copies += [pltpu.make_async_copy(tile_s, gather.at[n : n + 2], sent.at[n + 1]) for n in range(0, COUNT, 2)]
    for copy in copies[1:]:
        copy.start()
    u1[...] = w.get(8, PLANES1)
    rim_s[20:28] = jnp.where(lane % 2 == 0, w.get(8, PLANES1), b_one.get(8, PLANES1)).reshape((8,) + TILE)
    copies.append(pltpu.make_async_copy(rim_s.at[20:28], rim.at[20:28], sent.at[COUNT + 1]))
    copies[-1].start()
    for copy in copies:
        copy.wait()


def down_pre(own):
    shapes = PRE_SHAPES + [(4, 2), (4, 2), (8, 4), (7, 4), (6, 4), (5, 4)]
    return call(pre_kernel, "down_pre", (own,), [shape_of(*n) for n in shapes], [scratch(1, 4), scratch(1, 2)])


def down_post(own, even, odd, pre):
    shapes = [shape_of(*n) for n in [(RIM,), (12, 4), (13, 4), (4, 2), (4, 2), *MID_SHAPES]]
    return call(
        post_kernel, "down_post", (own, even, odd, *pre), [jax.ShapeDtypeStruct((COUNT, 3, 4, 128), jnp.float32), *shapes],
        [
            scratch(13, 4), scratch(13, 4), scratch(13, 4), scratch(4, 2), scratch(13, 2), scratch(13, 2),
            pltpu.VMEM((2, 3, 4, 128), jnp.float32), scratch(28), pltpu.SemaphoreType.DMA((COUNT + 2,)),
            scratch(16, 4), scratch(16, 4), scratch(8, 2), scratch(8, 2),
        ],
        hbm_outputs=2,
    )


def outer(value, half):
    turned = lanes(value, 64)
    before = jnp.concatenate([lanes(value[-1:], 65), turned[:-1]], axis=0)
    after = jnp.concatenate([turned[1:], lanes(value[:1], 63)], axis=0)
    return jnp.where(half == 0, before, after), turned


def coarse_kernel(gathered, out, tiles_s, e2_s):
    lane, row = lane_ids(), row_ids()
    half = lane // 64
    x, y, z = position()
    for n in range(COUNT):
        tiles_s[n, 0] = jnp.concatenate([gathered[n, 0], gathered[n, 1]], axis=0)
        tiles_s[n, 1] = jnp.concatenate([gathered[n, 2], lanes(gathered[n, 2], -2)], axis=0)

    def collect(tile, slot):
        out = []
        for group in range(8):
            joined = None
            for q in range(GZ):
                natural = 7 - group if q % 2 else group
                rank, core = natural // 2, natural % 2
                n = ((rank ^ (rank >> 1)) * GY + core) * GZ + q
                piece = tiles_s[n, tile] if q == slot else lanes(tiles_s[n, tile], q - slot)
                joined = piece if joined is None else jnp.where(lane % 4 == q, piece, joined)
            out.append(joined)
        return jnp.stack(out)

    b_two, beta_two, alpha_two = ([collect(tile, slot + p) for p in range(2)] for tile, slot in ((0, 0), (0, 2), (1, 0)))
    slab = lax.broadcasted_iota(jnp.int32, (8,) + TILE, 0)
    end = ((slab == 0) & (lane % 4 == 0) & (half == 0)) | ((slab == 7) & (lane % 4 == 3) & (half == 1))

    def sides(beta, dx, dy):
        place = (lane % 64) // dy
        rims = row >= 8 - dx, row < dx, place == 64 // dy - 1, place == 0
        others = rows(beta, -dx), rows(beta, dx), lanes(beta, -dy), lanes(beta, dy)
        faces = [jnp.where(rim, 0.0, 0.5 * (beta + other)) for rim, other in zip(rims, others)]
        edge = jnp.where(rims[0] | rims[1], 0.5, 0.0) + jnp.where(rims[2] | rims[3], 0.5, 0.0)
        return faces, (faces[0] + faces[1]) + (faces[2] + faces[3]) + beta * edge

    def scaled(faces, inv):
        return [face * inv for face in faces]

    def flat(v, coeffs, dx, dy):
        x_above, x_below, y_above, y_below = coeffs
        total = x_above * rows(v, -dx) + x_below * rows(v, dx)
        return total + (y_above * lanes(v, -dy) + y_below * lanes(v, dy))

    faces_a, sum_a = sides(beta_two[0], 1, 4)
    faces_b, sum_b = sides(beta_two[1], 1, 4)
    middle = 0.5 * (beta_two[0] + beta_two[1])
    inner = 0.5 * (beta_two[1] + lanes(beta_two[1], 64))
    edge = 0.5 * (beta_two[0] + jnp.where(end, 0.0, outer(beta_two[0], half)[0]))
    shift = SHIFT_BASE * 16.0
    diag_a = shift * alpha_two[0] + sum_a + (middle + edge)
    diag_b = shift * alpha_two[1] + sum_b + (middle + inner)
    inv_a, inv_b = inverse(diag_a), inverse(diag_b)
    flat_a, flat_b = scaled(faces_a, inv_a), scaled(faces_b, inv_b)
    middle_a, middle_b = middle * inv_a, middle * inv_b
    rim_a, inner_b = jnp.where(end, 0.0, edge) * inv_a, inner * inv_b
    rhs_a, rhs_b = b_two[0] * inv_a, b_two[1] * inv_b

    def apply_two(va, vb):
        ta = flat(va, flat_a, 1, 4) + (middle_a * vb + rim_a * outer(va, half)[0])
        tb = flat(vb, flat_b, 1, 4) + (middle_b * va + inner_b * lanes(vb, 64))
        return ta, tb

    def sweeps_two(before, now, factors):
        for carry, gain in factors:
            totals = apply_two(*now)
            new = []
            for v, old, rhs, total in zip(now, before or (None, None), (rhs_a, rhs_b), totals):
                base = (1.0 + carry - gain) * v + gain * rhs
                if carry != 0.0 and old is not None:
                    base = base - carry * old
                new.append(base + gain * total)
            before, now = now, new
        return now

    factors = chebyshev_factors(SWEEPS, SMOOTH_LOWER)
    ua, ub = sweeps_two(None, (factors[0][1] * rhs_a, factors[0][1] * rhs_b), factors[1:])
    ta, tb = apply_two(ua, ub)

    def restrict_whole(first, second):
        total = first + second
        total = total + jnp.where(row % 2 == 0, rows(total, -1), rows(total, 1))
        return total + jnp.where((lane // 4) % 2 == 0, lanes(total, -4), lanes(total, 4))

    second = (lane // 4) % 2 == 1

    def pack_low(value):
        return jnp.where(second, value[4:], value[:4])

    def outer_low(value):
        turned = lanes(value, 64)
        first_one, last_one = value[:1], value[-1:]
        before = jnp.where(second, lanes(last_one, 68), lanes(last_one, 61))
        after = jnp.where(second, lanes(first_one, 67), lanes(first_one, 60))
        before = jnp.concatenate([before, turned[:-1]], axis=0)
        after = jnp.concatenate([turned[1:], after], axis=0)
        return jnp.where(half == 0, before, after), turned

    b_low = 0.5 * pack_low(restrict_whole(diag_a * (rhs_a + ta - ua), diag_b * (rhs_b + tb - ub)))
    beta_low = 0.125 * pack_low(restrict_whole(beta_two[0], beta_two[1]))
    alpha_low = 0.125 * pack_low(restrict_whole(alpha_two[0], alpha_two[1]))
    slab = lax.broadcasted_iota(jnp.int32, (4,) + TILE, 0) + jnp.where(second, 4, 0)
    end_low = ((slab == 0) & (lane % 4 == 0) & (half == 0)) | ((slab == 7) & (lane % 4 == 3) & (half == 1))
    faces_low, sum_low = sides(beta_low, 2, 8)
    beyond, turned = outer_low(beta_low)
    inner_low = 0.5 * (beta_low + turned)
    edge_low = 0.5 * (beta_low + jnp.where(end_low, 0.0, beyond))
    inv_low = inverse(SHIFT_BASE * 64.0 * alpha_low + sum_low + (inner_low + edge_low))
    flat_low = scaled(faces_low, inv_low)
    rim_low = jnp.where(end_low, 0.0, edge_low) * inv_low
    inner_low = inner_low * inv_low
    rhs_low = b_low * inv_low
    before = v = None
    for carry, gain in chebyshev_factors(BOTTOM, BOTTOM_LOWER):
        if v is None:
            v = gain * rhs_low
            continue
        beyond, turned = outer_low(v)
        base = (1.0 + carry - gain) * v + gain * rhs_low
        if before is not None:
            base = base - carry * before
        total = flat(v, flat_low, 2, 8) + (inner_low * turned + rim_low * beyond)
        before, v = v, base + gain * total
    v = jnp.concatenate([jnp.where(second, lanes(v, 4), v), jnp.where(second, v, lanes(v, -4))], axis=0)
    va, vb = sweeps_two(None, (ua + v, ub + v), factors)
    for group in range(8):
        e2_s[group, 0] = va[group]
        e2_s[group, 1] = vb[group]

    chunk = chunk_of(x, y, z)
    place = 8 * z + chunk

    def fetch(offset, p, turn=0):
        index = jnp.clip(place + offset, 0, COUNT - 1)
        tile, out = e2_s[index % 8, p], None
        for slot in range(4):
            piece = pltpu.roll(tile, (128 + slot + turn - index // 8) % 128, 1)
            out = piece if out is None else jnp.where(lane % 4 == slot, piece, out)
        return out

    first = half == 0
    out[0] = jnp.where(first, fetch(-1, 0), fetch(1, 0))
    out[1] = jnp.where(first, fetch(-1, 1), fetch(1, 1))
    out[2] = jnp.where(first, fetch(-1, 1, 64), fetch(1, 1, 64))
    out[3] = jnp.where(first, fetch(-1, 0, 64), fetch(1, 0, 64))
    out[4] = fetch(0, 0)
    out[5] = fetch(0, 1)


def coarse(gathered):
    vmem = pl.BlockSpec(memory_space=pltpu.VMEM)
    return pl.pallas_call(
        coarse_kernel,
        out_shape=shape_of(6),
        in_specs=[vmem],
        out_specs=vmem,
        scratch_shapes=[scratch(COUNT, 2), scratch(8, 2)],
        compiler_params=pltpu.CompilerParams(vmem_limit_bytes=8 * 2**20),
        name="coarse",
    )(gathered)


def up_kernel(e_two, rim_even, rim_odd, own, halo_b, late, u1, b1, v4, *refs):
    pre, mid, (out, v_a, v_b, w_a, w_b, bx_s) = refs[:10], refs[10:20], refs[20:]
    zero, one = coefficient_planes(pre, mid)
    lane, row = lane_ids(), row_ids()
    _, from_even = halo_masks()
    factors = chebyshev_factors(SWEEPS, SMOOTH_LOWER)

    for p in range(1, 8):
        if p >= 4:
            k = 7 - p
            both = lanes(jnp.where(from_even, rim_odd[20 + 2 * k : 22 + 2 * k], rim_even[20 + 2 * k : 22 + 2 * k]), 64)
        else:
            both = jnp.where(from_even, rim_even[20 + 2 * p : 22 + 2 * p], rim_odd[20 + 2 * p : 22 + 2 * p])
        w_a[p] = jnp.where(lane % 2 == 0, both, lanes(both, 1)) + e_two[p // 2]
        if p >= 2:
            bx_s[p] = jnp.where(lane % 2 == 0, lanes(both, -1), both)
    for p in range(8, PLANES1):
        w_a[p] = u1[p - 8] + e_two[p // 2]
    w_a[PLANES1] = lanes(w_a[PLANES1 - 1], 64)
    pair = (Planes((0, w_b)), Planes((0, w_a)), None)
    w = smooth(pair, Planes((0, bx_s), (8, b1)), one[3], one[:3], factors, 2, PLANES1, 2, SPAN1)

    for p in range(11, PLANES):
        if p >= 16:
            start = Planes((7, late), (20, v4)).get(p, p + 1)[0]
        else:
            k = 4 * (15 - p)
            start = lanes(jnp.where(from_even, rim_odd[k : k + 4], rim_even[k : k + 4]), 64)
        e_one = w.get(p // 2, p // 2 + 1)[0]
        e_one = jnp.concatenate([e_one[:1], e_one[:1], e_one[1:], e_one[1:]], axis=0)
        v_a[p] = start + e_one
    v_a[PLANES] = lanes(v_a[PLANES - 1], 64)
    b, diag, coeffs = Planes((4, halo_b), (16, own.at[2])), zero[4], zero[:3]
    v = smooth((Planes((0, v_b)), Planes((0, v_a)), None), b, zero[3], coeffs, factors, 12, PLANES, 1, SPAN)
    low = (lane // 32) % 2 == 0
    for k in range(4):
        for o in range(2):
            parts = []
            for pp in range(2):
                p = 16 + k + 4 * pp
                value = v.get(p, p + 1)
                if o == 1:
                    value = (b.get(p, p + 1) + couple(v, p, p + 1, *coeffs, 1)) - diag.get(p, p + 1) * value
                parts.append(regroup([value[0, i] for i in range(4)], 0, 2, row))
            for i in range(GX):
                one, two = parts[0][i], parts[1][i]
                out[2 * i, pl.ds(o * 32 + k * 8, 8), :] = jnp.where(low, one, lanes(two, 32))
                out[2 * i + 1, pl.ds(o * 32 + k * 8, 8), :] = jnp.where(low, lanes(one, -32), two)


def up(*operands):
    return call(
        up_kernel, "up_strokes", operands, [jax.ShapeDtypeStruct((8, 64, 128), jnp.float32)],
        [scratch(25, 4), scratch(25, 4), scratch(13, 2), scratch(13, 2), scratch(8, 2)],
    )[0]


def unpack_kernel(in_ref, v_ref, r_ref, fields, turned, staged, left):
    z = lax.axis_index("gz")
    lane = lane_ids()
    for x in range(GX):
        for y in range(GY):
            start = pl.multiple_of(chunk_of(x, y, z) * 64, 64)
            staged[pl.ds(start, 64), :] = in_ref[x * GY + y]
    copies = [pltpu.make_async_copy(fields.at[o], ref, left.at[o]) for o, ref in enumerate((v_ref, r_ref))]
    for o, copy in enumerate(copies):
        for xg in range(2):
            slot = turned.at[2 * o + xg]
            for k in range(4):
                tiles = [staged[pl.ds(o * 32 + k * 8 + 2 * x4 + xg, 8, stride=64), :] for x4 in range(4)]
                for g, tile in enumerate(regroup(tiles, 1, 32, lane)):
                    slot[pl.ds(depth_of(k, g), 8, stride=16), :] = tile
            fields[o, 4 * xg : 4 * xg + 4] = slot[...].T.reshape(4, 32, 128)
        copy.start()
    for copy in copies:
        copy.wait()


def unpack(received):
    vmem = pl.BlockSpec(memory_space=pltpu.VMEM)
    return pl.pallas_call(
        unpack_kernel,
        out_shape=[jax.ShapeDtypeStruct(BLOCK, jnp.float32)] * 2,
        in_specs=[vmem],
        out_specs=[pl.BlockSpec(memory_space=pltpu.HBM)] * 2,
        scratch_shapes=[
            pltpu.VMEM((2,) + BLOCK, jnp.float32),
            pltpu.VMEM((4, 128, 128), jnp.float32),
            pltpu.VMEM((512, 128), jnp.float32),
            pltpu.SemaphoreType.DMA((2,)),
        ],
        compiler_params=pltpu.CompilerParams(vmem_limit_bytes=4 * 2**20),
        name="unpack",
    )(received)


def slab_shards(right_side, alpha_coef, beta_coef):
    even_pairs, odd_pairs = swap_pairs(False), swap_pairs(True)
    packed = pack(jnp.stack([alpha_coef, beta_coef, right_side]))
    own, to_even, to_odd = to_slab(lax.all_to_all(packed, RING, 0, 0))
    even = lax.ppermute(to_even, ALL, even_pairs)
    odd = lax.ppermute(to_odd, ALL, odd_pairs)
    found = down_pre(own)
    pre, v4 = found[:10], found[15]
    gather, rim, halo_b, late, u1, b1, *mid = down_post(own, even, odd, found)
    rim_even = lax.ppermute(rim, ALL, even_pairs)
    rim_odd = lax.ppermute(rim, ALL, odd_pairs)
    kept = (own, halo_b, late, u1, b1, v4, *pre, *mid)
    result = up(coarse(lax.all_to_all(gather, ALL, 0, 0)), rim_even, rim_odd, *kept)
    return tuple(unpack(lax.all_to_all(result, RING, 0, 0)))


def solution(mesh):
    spec = P("gx", "gy", "gz")
    plain = jax.shard_map(shards, mesh=mesh, in_specs=(spec,) * 3, out_specs=(spec,) * 2, check_vma=False)
    slabs = jax.shard_map(slab_shards, mesh=mesh, in_specs=(spec,) * 3, out_specs=(spec,) * 2, check_vma=False)
    sizes = tuple(mesh.shape[axis] for axis in ALL)

    def run(right_side, alpha_coef, beta_coef):
        block = tuple(n // size for n, size in zip(right_side.shape, sizes))
        fits = sizes == (GX, GY, GZ) and block == BLOCK
        return (slabs if fits else plain)(right_side, alpha_coef, beta_coef)

    return run
```

```python
import jax
import jax.numpy as jnp
from jax import lax
from jax.experimental import pallas as pl
from jax.experimental.pallas import tpu as pltpu
from jax.sharding import PartitionSpec as P

LEVELS = 3
SWEEPS = 4
BOTTOM = 12


SHIFT_BASE = 0.01
UPPER_EIG = 2.0
SMOOTH_LOWER = 0.25
BOTTOM_LOWER = 0.02


def with_halo(block, sides, width):
    for axis, dim in sides:
        count = lax.axis_size(axis)
        forward = [(i, i + 1) for i in range(count - 1)]
        backward = [(target, source) for source, target in forward]
        low = lax.ppermute(
            lax.slice_in_dim(block, block.shape[dim] - width, None, axis=dim), axis, forward
        )
        high = lax.ppermute(lax.slice_in_dim(block, 0, width, axis=dim), axis, backward)
        block = jnp.concatenate([low, block, high], axis=dim)
    return block


def partner_2(array, axis, distance):
    return lax.ppermute(array, axis, [(i, i ^ 1 << distance) for i in range(lax.axis_size(axis))])


def split_padded(padded):
    return (
        padded[:-2, 1:-1, 1:-1],
        padded[2:, 1:-1, 1:-1],
        padded[1:-1, :-2, 1:-1],
        padded[1:-1, 2:, 1:-1],
        padded[1:-1, 1:-1, :-2],
        padded[1:-1, 1:-1, 2:],
    )


def zero_pad(field):
    return jnp.pad(field, 1)


def rim_iterate(field):
    return with_halo(field, (("gx", 0), ("gy", 1), ("gz", 2)), 1)


def rim_coefficient(field):
    return with_halo(field, (("gx", 0), ("gy", 1), ("gz", 2)), 1)


def level_operator(beta_level, alpha_level, padded_beta, shift):
    coeffs = tuple((0.5 * (beta_level + other) for other in split_padded(padded_beta)))
    diagonal = shift * alpha_level
    for coeff in coeffs:
        diagonal = diagonal + coeff
    return (coeffs, diagonal)


def apply_operator(field, operator, pad_field):
    coeffs, diagonal = operator
    others = split_padded(pad_field(field))
    total = coeffs[0] * others[0]
    for index in range(1, 6):
        total = total + coeffs[index] * others[index]
    return diagonal * field - total


def chebyshev(iterate, rhs_level, operator, count, lower, zero_start, pad_field):
    diagonal = operator[1]
    center = (UPPER_EIG + lower) / 2.0
    half_width = (UPPER_EIG - lower) / 2.0
    sigma_ratio = center / half_width
    rho_old = 1.0 / sigma_ratio
    if zero_start:
        remain = rhs_level
    else:
        remain = rhs_level - apply_operator(iterate, operator, pad_field)
    update = remain / diagonal / center
    iterate = iterate + update
    for sweep_index in range(count - 1):
        remain = rhs_level - apply_operator(iterate, operator, pad_field)
        rho_new = 1.0 / (2.0 * sigma_ratio - rho_old)
        update = rho_new * rho_old * update + 2.0 * rho_new / half_width * (remain / diagonal)
        iterate = iterate + update
        rho_old = rho_new
    return iterate


def restrict_mean(field):
    first, second, third = field.shape
    blocks = field.reshape(first // 2, 2, second // 2, 2, third // 2, 2)
    return jnp.sum(blocks, axis=(1, 3, 5)) * 0.125


def prolong_copy(field):
    return jnp.repeat(jnp.repeat(jnp.repeat(field, 2, axis=0), 2, axis=1), 2, axis=2)


def join_partner(packed, partner, device_index, bit_index, dim):
    position = device_index // 2**bit_index % 2
    lower_first = jnp.concatenate([packed, partner], axis=dim)
    upper_first = jnp.concatenate([partner, packed], axis=dim)
    return jnp.where(position == 0, lower_first, upper_first)


def shards(right_side, alpha_coef, beta_coef):
    betas = [beta_coef]
    alphas = [alpha_coef]
    for level in range(LEVELS):
        betas.append(restrict_mean(betas[-1]))
        alphas.append(restrict_mean(alphas[-1]))
    operators = []
    for level in range(LEVELS):
        padded_beta = rim_coefficient(betas[level])
        operators.append(
            level_operator(betas[level], alphas[level], padded_beta, SHIFT_BASE * 4.0**level)
        )
    rhs_levels = [right_side]
    smoothed = []
    for level in range(LEVELS):
        iterate = chebyshev(
            jnp.zeros_like(rhs_levels[level]),
            rhs_levels[level],
            operators[level],
            SWEEPS,
            SMOOTH_LOWER,
            True,
            rim_iterate,
        )
        remain = rhs_levels[level] - apply_operator(iterate, operators[level], rim_iterate)
        smoothed.append(iterate)
        rhs_levels.append(4.0 * restrict_mean(remain))
    coarse_rhs = rhs_levels[LEVELS]
    local_shape = coarse_rhs.shape
    packed = jnp.stack([coarse_rhs, betas[LEVELS], alphas[LEVELS]])
    index_x = lax.axis_index("gx")
    index_y = lax.axis_index("gy")
    index_z = lax.axis_index("gz")
    for bit_index in range(lax.axis_size("gx").bit_length() - 1):
        partner = partner_2(packed, "gx", bit_index)
        packed = join_partner(packed, partner, index_x, bit_index, 1)
    for bit_index in range(lax.axis_size("gy").bit_length() - 1):
        partner = partner_2(packed, "gy", bit_index)
        packed = join_partner(packed, partner, index_y, bit_index, 2)
    for bit_index in range(lax.axis_size("gz").bit_length() - 1):
        partner = partner_2(packed, "gz", bit_index)
        packed = join_partner(packed, partner, index_z, bit_index, 3)
    whole_rhs = packed[0]
    whole_beta = packed[1]
    whole_alpha = packed[2]
    bottom_operator = level_operator(
        whole_beta, whole_alpha, zero_pad(whole_beta), SHIFT_BASE * 4.0**LEVELS
    )
    whole_correction = chebyshev(
        jnp.zeros_like(whole_rhs), whole_rhs, bottom_operator, BOTTOM, BOTTOM_LOWER, True, zero_pad
    )
    starts = (index_x * local_shape[0], index_y * local_shape[1], index_z * local_shape[2])
    correction = lax.dynamic_slice(whole_correction, starts, local_shape)
    for level in range(LEVELS - 1, -1, -1):
        start_field = smoothed[level] + prolong_copy(correction)
        correction = chebyshev(
            start_field,
            rhs_levels[level],
            operators[level],
            SWEEPS,
            SMOOTH_LOWER,
            False,
            rim_iterate,
        )
    residual_field = right_side - apply_operator(correction, operators[0], rim_iterate)
    return (correction, residual_field)


GX, GY, GZ = 4, 2, 4
COUNT = GX * GY * GZ
RIM = 28
BLOCK = (8, 32, 128)
RING = ("gx", "gy")
ALL = ("gx", "gy", "gz")
TILE = (8, 128)
PLANES = 24
PLANES1 = 12
SPAN, SPAN1, COEF_SPAN, COEF_SPAN1 = 2, 4, 2, 4


def chunk_of(x, y, z):
    natural = 2 * (x ^ (x >> 1)) + y
    return natural + (z % 2) * (7 - 2 * natural)


def position():
    return lax.axis_index("gx"), lax.axis_index("gy"), lax.axis_index("gz")


def swap_pairs(odd):
    place = {}
    for x in range(GX):
        for y in range(GY):
            for z in range(GZ):
                place[8 * z + chunk_of(x, y, z)] = (x * GY + y) * GZ + z
    count = len(place)
    if odd:
        pairs = [(i, i + 1) for i in range(1, count - 1, 2)]
    else:
        pairs = [(i, i + 1) for i in range(0, count, 2)]
    return [(place[a], place[b]) for a, b in pairs] + [(place[b], place[a]) for a, b in pairs]


def lane_ids():
    return lax.broadcasted_iota(jnp.int32, TILE, 1)


def row_ids():
    return lax.broadcasted_iota(jnp.int32, TILE, 0)


def lanes(value, shift):
    return pltpu.roll(value, shift % 128, value.ndim - 1)


def rows(value, shift):
    return pltpu.roll(value, shift % 8, value.ndim - 2)


def regroup(tiles, axis, width, ids):
    move = lanes if axis == 1 else rows
    group = ids // width % 4
    odd, upper = group % 2 == 1, group >= 2
    a, b, c, d = tiles
    turned = move(jnp.where(odd, a, b), width)
    a, b = jnp.where(odd, turned, a), jnp.where(odd, b, turned)
    turned = move(jnp.where(odd, c, d), width)
    c, d = jnp.where(odd, turned, c), jnp.where(odd, d, turned)
    turned = move(jnp.where(upper, a, c), 2 * width)
    a, c = jnp.where(upper, turned, a), jnp.where(upper, c, turned)
    turned = move(jnp.where(upper, b, d), 2 * width)
    own = jnp.where(upper, d, b)
    inner = odd != upper
    return [a, jnp.where(inner, own, turned), c, jnp.where(inner, turned, own)]


def depth_of(k, group):
    half, part = group // 2, group % 2
    plane = k + 4 * part
    return 15 - plane if half else plane


def pack_kernel(fields, out_ref, turned, staged):
    z = lax.axis_index("gz")
    lane = lane_ids()
    for a in range(3):
        for xg in range(2):
            slot = turned.at[2 * a + xg]
            slot[...] = fields[a, 4 * xg : 4 * xg + 4].reshape(128, 128).T
            for k in range(4):
                tiles = [slot[pl.ds(depth_of(k, g), 8, stride=16), :] for g in range(4)]
                for x4, tile in enumerate(regroup(tiles, 1, 32, lane)):
                    staged[pl.ds(a * 32 + k * 8 + 2 * x4 + xg, 8, stride=96), :] = tile
    for x in range(GX):
        for y in range(GY):
            start = pl.multiple_of(chunk_of(x, y, z) * 96, 96)
            out_ref[x * GY + y] = staged[pl.ds(start, 96), :]


def pack(fields):
    return pl.pallas_call(
        pack_kernel,
        out_shape=jax.ShapeDtypeStruct((8, 96, 128), jnp.float32),
        in_specs=[pl.BlockSpec(memory_space=pltpu.VMEM)],
        out_specs=pl.BlockSpec(memory_space=pltpu.VMEM),
        scratch_shapes=[pltpu.VMEM((6, 128, 128), jnp.float32), pltpu.VMEM((768, 128), jnp.float32)],
        compiler_params=pltpu.CompilerParams(vmem_limit_bytes=4 * 2**20),
        name="pack",
    )(fields)


def shape_of(*dims):
    return jax.ShapeDtypeStruct(dims + TILE, jnp.float32)


def scratch(*dims):
    return pltpu.VMEM(dims + TILE, jnp.float32)


def halo_masks():
    x, y, z = position()
    chunk = chunk_of(x, y, z)
    half = lane_ids() // 64
    return chunk, (half + chunk % 2) == 1


PLACE = [(r, True) for r in range(6)] + [(4, False), (5, False), (3, False), (2, False), (1, False), (0, False)]
PLACE += [(6, False), (6, True)]
FIRST_TILE = (0, 6, 13)
MESSAGE = 19


def message(planes, near, count):
    tiles = [jnp.where(near, planes[t], planes[t + 4]) for t in range(4)]
    tiles += [jnp.where(near, planes[t], lanes(planes[t + 2], 64)) for t in (4, 5)]
    if count == 7:
        tiles.append(jnp.where(near, lanes(planes[2], 64), planes[3]))
    return tiles


def halo_plane(even, odd, a, r, from_even):
    tile, moved = PLACE[r]
    tile = FIRST_TILE[a] + tile
    if moved:
        return lanes(jnp.where(from_even, odd[tile], even[tile]), 64)
    return jnp.where(from_even, even[tile], odd[tile])


def slab_kernel(in_ref, out_ref, b_ref, even_ref, odd_ref):
    lane, row = lane_ids(), row_ids()
    low = (lane // 32) % 2 == 0
    _, from_even = halo_masks()
    for a in range(3):
        planes = [None] * 8
        for k in range(4):
            part = ([], [])
            for x in range(GX):
                first = in_ref[2 * x, pl.ds(a * 32 + k * 8, 8), :]
                second = in_ref[2 * x + 1, pl.ds(a * 32 + k * 8, 8), :]
                part[0].append(jnp.where(low, first, lanes(second, 32)))
                part[1].append(jnp.where(low, lanes(first, -32), second))
            for pp in range(2):
                planes[k + 4 * pp] = jnp.stack(regroup(part[pp], 0, 2, row))
                if a == 2:
                    b_ref[k + 4 * pp] = planes[k + 4 * pp]
                else:
                    out_ref[a, k + 4 * pp] = planes[k + 4 * pp]
        count = 7 if a == 1 else 6
        for near, ref in ((from_even, even_ref), (~from_even, odd_ref)):
            for t, tile in enumerate(message(planes, near, count)):
                ref[FIRST_TILE[a] + t] = tile


def to_slab(received):
    vmem = pl.BlockSpec(memory_space=pltpu.VMEM)
    return pl.pallas_call(
        slab_kernel,
        out_shape=[shape_of(2, 8, 4), shape_of(8, 4), shape_of(MESSAGE, 4), shape_of(MESSAGE, 4)],
        in_specs=[vmem],
        out_specs=[vmem] * 4,
        compiler_params=pltpu.CompilerParams(vmem_limit_bytes=4 * 2**20),
        name="to_slab",
    )(received)


class Planes:
    def __init__(self, *segments):
        self.segments = [(first, first + ref.shape[0], ref) for first, ref in segments]

    def find(self, p, q):
        for first, last, ref in self.segments:
            low, high = max(p, first), min(q, last)
            if low < high:
                yield low, high, ref, slice(low - first, high - first)

    def get(self, p, q):
        pieces = [ref[place] for _, _, ref, place in self.find(p, q)]
        return pieces[0] if len(pieces) == 1 else jnp.concatenate(pieces, axis=0)

    def put(self, p, value):
        for low, high, ref, place in self.find(p, p + value.shape[0]):
            ref[place] = value[low - p : high - p]


def spans(first, last, size):
    return [(p, min(p + size, last)) for p in range(first, last, size)]


def x_up(value):
    return jnp.concatenate([value[:, 1:], rows(value[:, :1], -1)], axis=1)


def x_down(value):
    return jnp.concatenate([rows(value[:, -1:], 1), value[:, :-1]], axis=1)


def couple(v, p, q, cx, cy, cz, dup):
    here, by_x, by_y = v.get(p, q), cx.get(p, q), cy.get(p, q)
    total = by_x * x_up(here) + x_down(by_x * here)
    total = total + (by_y * lanes(here, -dup) + lanes(by_y * here, dup))
    return total + (cz.get(p, q) * v.get(p - 1, q - 1) + cz.get(p + 1, q + 1) * v.get(p + 1, q + 1))


def chebyshev_factors(count, lower):
    center = (UPPER_EIG + lower) / 2.0
    half_width = (UPPER_EIG - lower) / 2.0
    ratio = center / half_width
    old = 1.0 / ratio
    out = [(0.0, 1.0 / center)]
    for _ in range(count - 1):
        new = 1.0 / (2.0 * ratio - old)
        out.append((new * old, 2.0 * new / half_width))
        old = new
    return out


def sweep(new, now, before, factor, b, dinv, coeffs, p, q, dup, size):
    carry, gain = factor
    for p, q in spans(p, q, size):
        base = (1.0 + carry - gain) * now.get(p, q)
        if carry != 0.0 and before is not None:
            base = base - carry * before.get(p, q)
        new.put(p, (b.get(p, q) + couple(now, p, q, *coeffs, dup)) * (gain * dinv.get(p, q)) + base)


def close(v, last):
    v.put(last, lanes(v.get(last - 1, last), 64))


def smooth(pair, b, dinv, coeffs, factors, first, last, dup, size):
    before, now, spare = pair
    for number, factor in enumerate(factors):
        new = spare if before is None else before
        sweep(new, now, before, factor, b, dinv, coeffs, first + number, last, dup, size)
        close(new, last)
        before, now = now, new
    return now


def inverse(value):
    guess = pl.reciprocal(value, approx=True)
    return guess * (2.0 - value * guess)


def level_coefficients(beta, alpha, first, last, shift, dup, cx, cy, cz, dinv, diag, ends, seam, size):
    lane, row = lane_ids(), row_ids()
    y_last = (lane % 64) // dup == 64 // dup - 1
    y_first = (lane % 64) // dup == 0
    x_rim = jnp.where(row == 0, 0.5, 0.0), jnp.where(row == 7, 0.5, 0.0)
    for p, q in spans(first, last, size):
        here = beta.get(p, q)
        by_x = 0.5 * (here + x_up(here))
        by_x = jnp.concatenate([by_x[:, :-1], jnp.where(row == 7, 0.0, by_x[:, -1:])], axis=1)
        above = jnp.where(y_last, 0.0, lanes(here, -dup))
        below = jnp.where(y_first, 0.0, lanes(here, dup))
        by_y = jnp.where(y_last, 0.0, 0.5 * (here + above))
        face = 0.5 * (beta.get(p - 1, q - 1) + here)
        total = shift * alpha.get(p, q) + (by_x + x_down(by_x)) + (here + 0.5 * (above + below))
        total = total + (face + 0.5 * (here + beta.get(p + 1, q + 1)))
        groups = [total[:, i : i + 1] for i in range(total.shape[1])]
        groups[0] = groups[0] + here[:, :1] * x_rim[0]
        groups[-1] = groups[-1] + here[:, -1:] * x_rim[1]
        total = jnp.concatenate(groups, axis=1)
        cx.put(p, by_x)
        cy.put(p, by_y)
        cz.put(p, face)
        diag.put(p, total)
        dinv.put(p, inverse(jnp.where(total > 0.0, total, 1.0)))
    if first <= seam < last:
        cz.put(seam, cz.get(seam, seam + 1) * ends)
    else:
        cz.put(last, 0.5 * (beta.get(last - 1, last) + beta.get(last, last + 1)))


def restrict_pair(first, second, dup):
    lane = lane_ids()
    total = first + second
    total = jnp.concatenate([total[:, i : i + 1] + total[:, i + 1 : i + 2] for i in range(0, total.shape[1], 2)], axis=1)
    return total + jnp.where((lane // dup) % 2 == 0, lanes(total, -dup), lanes(total, dup))


def restrict(take, p, q, dup):
    fine = take(2 * p, 2 * q)
    fine = fine.reshape((q - p, 2) + fine.shape[1:])
    return restrict_pair(fine[:, 0], fine[:, 1], dup)


def ends_factor():
    x, y, z = position()
    slab = 8 * z + chunk_of(x, y, z)
    half = lane_ids() // 64
    end = ((half == 0) & (slab == 0)) | ((half == 1) & (slab == 8 * GZ - 1))
    return jnp.where(end, 0.0, 1.0)


def call(kernel, name, operands, out_shape, scratch_shapes):
    vmem = pl.BlockSpec(memory_space=pltpu.VMEM)
    return pl.pallas_call(
        kernel,
        out_shape=out_shape,
        in_specs=[vmem] * len(operands),
        out_specs=[vmem] * len(out_shape),
        scratch_shapes=scratch_shapes,
        compiler_params=pltpu.CompilerParams(vmem_limit_bytes=16 * 2**20),
        name=name,
    )(*operands)


PRE_SHAPES = [(7, 4), (7, 4), (8, 4), (7, 4), (7, 4), (3, 2), (3, 2), (4, 2), (3, 2), (3, 2)]
MID_SHAPES = [(5, 4), (5, 4), (5, 4), (5, 4), (1, 4), (7, 2), (7, 2), (7, 2), (7, 2)]
LOW_SHAPES = [(8, 4), (8, 4), (8, 4), (8, 4), (12, 4), (7, 2)]


def coefficient_planes(pre, mid, low):
    zero, one = [], []
    for i in range(5):
        parts = [(4, low[i])] if low else []
        parts += [(16 if i == 4 else 12, mid[i])] if mid else []
        zero.append(Planes(*parts, *([(17, pre[i])] if pre else [])))
        parts = []
        if mid and i < 4:
            parts = [(2, mid[5 + i])]
        elif low and i == 4:
            parts = [(2, low[5])]
        one.append(Planes(*parts, *([(9, pre[5 + i])] if pre and len(pre) > 5 + i else [])))
    return zero, one


def pre_kernel(own, own_b, *refs):
    pre, (alpha1, beta1, v1, v2, v3, v4), (ghost, ghost1) = refs[:10], refs[10:16], refs[16:]
    zero, one = coefficient_planes(pre, None, None)
    alpha, beta = Planes((16, own.at[0])), Planes((16, own.at[1]), (24, ghost))
    alpha_one, beta_one = Planes((8, alpha1)), Planes((8, beta1), (12, ghost1))
    close(beta, PLANES)
    level_coefficients(beta, alpha, 17, PLANES, SHIFT_BASE, 1, *zero, None, 16, COEF_SPAN)
    beta_one.put(8, 0.125 * restrict(beta.get, 8, PLANES1, 1))
    alpha_one.put(8, 0.125 * restrict(alpha.get, 8, PLANES1, 1))
    close(beta_one, PLANES1)
    level_coefficients(beta_one, alpha_one, 9, PLANES1, SHIFT_BASE * 4.0, 2, *one, None, 8, COEF_SPAN1)
    b, coeffs, dinv = Planes((16, own_b)), zero[:3], zero[3]
    factors = chebyshev_factors(SWEEPS, SMOOTH_LOWER)
    iterates = [None, Planes((17, v1)), Planes((18, v2)), Planes((19, v3)), Planes((20, v4))]
    for p, q in spans(17, PLANES, 4):
        iterates[1].put(p, factors[0][1] * (b.get(p, q) * dinv.get(p, q)))
    close(iterates[1], PLANES)
    for i in range(2, 5):
        sweep(iterates[i], iterates[i - 1], iterates[i - 2], factors[i - 1], b, dinv, coeffs, 16 + i, PLANES, 1, SPAN)
        close(iterates[i], PLANES)


def mid_part(own, even, odd, beta1_own, alpha1_own, mid, low, beta_s, alpha_s, beta1_s, alpha1_s):
    _, from_even = halo_masks()
    zero, one = coefficient_planes(None, mid, low)
    for p in range(2, 16):
        beta_s[p] = halo_plane(even, odd, 1, 15 - p, from_even)
        if p >= 4:
            alpha_s[p] = halo_plane(even, odd, 0, 15 - p, from_even)
    beta, alpha = Planes((0, beta_s), (16, own.at[1])), Planes((0, alpha_s), (16, own.at[0]))
    ends = ends_factor()
    level_coefficients(beta, alpha, 4, 17, SHIFT_BASE, 1, *zero, ends, 16, COEF_SPAN)
    beta_one, alpha_one = Planes((0, beta1_s), (8, beta1_own)), Planes((0, alpha1_s), (8, alpha1_own))
    for p in range(1, 8):
        beta_one.put(p, 0.125 * restrict(beta.get, p, p + 1, 1))
        if p >= 2:
            alpha_one.put(p, 0.125 * restrict(alpha.get, p, p + 1, 1))
    level_coefficients(beta_one, alpha_one, 2, 9, SHIFT_BASE * 4.0, 2, *one, ends, 8, COEF_SPAN1)


def post_kernel(own, own_b, odd, even, *refs):
    pre, (alpha1, beta1, v1, v2, v3, v4), (gather, rim, halo_b, late, u1, b1) = refs[:10], refs[10:16], refs[16:22]
    mid, low, (f1, f2, f3, f4, low_b, b1_s, w_a, w_b), scratch_mid = refs[22:31], refs[31:37], refs[37:45], refs[45:]
    mid_part(own, even, odd, beta1, alpha1, mid, low, *scratch_mid)
    lane = lane_ids()
    _, from_even = halo_masks()
    zero, one = coefficient_planes(pre, mid, low)
    coeffs, dinv, diag = zero[:3], zero[3], zero[4]
    b = Planes((4, low_b), (12, halo_b), (16, own_b))
    for p in range(4, 16):
        b.put(p, halo_plane(even, odd, 2, 15 - p, from_even)[None])
    factors = chebyshev_factors(SWEEPS, SMOOTH_LOWER)
    iterates = [
        None,
        Planes((4, f1), (17, v1)),
        Planes((5, f2), (18, v2)),
        Planes((6, f3), (19, v3)),
        Planes((7, f4), (16, late), (20, v4)),
    ]
    for p, q in spans(4, 17, 4):
        iterates[1].put(p, factors[0][1] * (b.get(p, q) * dinv.get(p, q)))
    for i in range(2, 5):
        sweep(iterates[i], iterates[i - 1], iterates[i - 2], factors[i - 1], b, dinv, coeffs, 3 + i, 16 + i, 1, SPAN)
    v = iterates[4]
    rim[0:20] = v.get(16, 21).reshape((20,) + TILE)

    def residual(v, b, diag, coeffs, dup):
        return lambda p, q: (b.get(p, q) + couple(v, p, q, *coeffs, dup)) - diag.get(p, q) * v.get(p, q)

    b_one = Planes((4, b1_s), (8, b1))
    for p in range(4, PLANES1):
        b_one.put(p, 0.5 * restrict(residual(v, b, diag, coeffs, 1), p, p + 1, 1))
    coeffs, dinv, diag = one[:3], one[3], one[4]
    w, spare = Planes((0, w_a)), Planes((0, w_b))
    w.put(4, factors[0][1] * (b_one.get(4, PLANES1) * dinv.get(4, PLANES1)))
    close(w, PLANES1)
    w = smooth((None, w, spare), b_one, dinv, coeffs, factors[1:], 5, PLANES1, 2, SPAN1)
    b_two = 0.5 * restrict(residual(w, b_one, diag, coeffs, 2), 4, 6, 2)
    beta_two = 0.125 * restrict(Planes((8, beta1)).get, 4, 6, 2)
    alpha_two = 0.125 * restrict(Planes((8, alpha1)).get, 4, 6, 2)
    slot = lane % 4
    both = jnp.where(slot < 2, *(jnp.where(slot % 2 == 0, field[0, 0], field[1, 0]) for field in (b_two, beta_two)))
    last = jnp.where(slot % 2 == 0, alpha_two[0, 0], alpha_two[1, 0])
    last = jnp.where(slot[:4] < 2, last[:4], last[4:])
    for n in range(COUNT):
        for i, part in enumerate((both[:4], both[4:], last)):
            gather[n, i] = part
    u1[...] = w.get(8, PLANES1)
    rim[20:28] = jnp.where(lane % 2 == 0, w.get(8, PLANES1), b_one.get(8, PLANES1)).reshape((8,) + TILE)


def down_pre(own, own_b):
    shapes = PRE_SHAPES + [(4, 2), (4, 2), (8, 4), (7, 4), (6, 4), (5, 4)]
    return call(pre_kernel, "down_pre", (own, own_b), [shape_of(*n) for n in shapes], [scratch(1, 4), scratch(1, 2)])


def down_post(own, own_b, even, odd, pre):
    shapes = [shape_of(*n) for n in [(RIM,), (4, 4), (4, 4), (4, 2), (4, 2), *MID_SHAPES]]
    spare = [(13, 4), (13, 4), (13, 4), (9, 4), (8, 4), (4, 2), (13, 2), (13, 2), (16, 4), (16, 4), (8, 2), (8, 2)]
    return call(
        post_kernel, "down_post", (own, own_b, odd, even, *pre),
        [jax.ShapeDtypeStruct((COUNT, 3, 4, 128), jnp.float32), *shapes], [scratch(*n) for n in LOW_SHAPES + spare],
    )


def outer(value, half):
    turned = lanes(value, 64)
    before = jnp.concatenate([lanes(value[-1:], 65), turned[:-1]], axis=0)
    after = jnp.concatenate([turned[1:], lanes(value[:1], 63)], axis=0)
    return jnp.where(half == 0, before, after), turned


def coarse_kernel(gathered, out, tiles_s, e2_s):
    lane, row = lane_ids(), row_ids()
    half = lane // 64
    x, y, z = position()
    for n in range(COUNT):
        tiles_s[n, 0] = jnp.concatenate([gathered[n, 0], gathered[n, 1]], axis=0)
        tiles_s[n, 1] = jnp.concatenate([gathered[n, 2], lanes(gathered[n, 2], -2)], axis=0)

    def collect(tile, slot):
        out = []
        for group in range(8):
            joined = None
            for q in range(GZ):
                natural = 7 - group if q % 2 else group
                rank, core = natural // 2, natural % 2
                n = ((rank ^ (rank >> 1)) * GY + core) * GZ + q
                piece = tiles_s[n, tile] if q == slot else lanes(tiles_s[n, tile], q - slot)
                joined = piece if joined is None else jnp.where(lane % 4 == q, piece, joined)
            out.append(joined)
        return jnp.stack(out)

    b_two, beta_two, alpha_two = ([collect(tile, slot + p) for p in range(2)] for tile, slot in ((0, 0), (0, 2), (1, 0)))
    slab = lax.broadcasted_iota(jnp.int32, (8,) + TILE, 0)
    end = ((slab == 0) & (lane % 4 == 0) & (half == 0)) | ((slab == 7) & (lane % 4 == 3) & (half == 1))

    def sides(beta, dx, dy):
        place = (lane % 64) // dy
        rims = row >= 8 - dx, row < dx, place == 64 // dy - 1, place == 0
        others = rows(beta, -dx), rows(beta, dx), lanes(beta, -dy), lanes(beta, dy)
        faces = [jnp.where(rim, 0.0, 0.5 * (beta + other)) for rim, other in zip(rims, others)]
        edge = jnp.where(rims[0] | rims[1], 0.5, 0.0) + jnp.where(rims[2] | rims[3], 0.5, 0.0)
        return faces, (faces[0] + faces[1]) + (faces[2] + faces[3]) + beta * edge

    def scaled(faces, inv):
        return [face * inv for face in faces]

    def flat(v, coeffs, dx, dy):
        x_above, x_below, y_above, y_below = coeffs
        total = x_above * rows(v, -dx) + x_below * rows(v, dx)
        return total + (y_above * lanes(v, -dy) + y_below * lanes(v, dy))

    faces_a, sum_a = sides(beta_two[0], 1, 4)
    faces_b, sum_b = sides(beta_two[1], 1, 4)
    middle = 0.5 * (beta_two[0] + beta_two[1])
    inner = 0.5 * (beta_two[1] + lanes(beta_two[1], 64))
    edge = 0.5 * (beta_two[0] + jnp.where(end, 0.0, outer(beta_two[0], half)[0]))
    shift = SHIFT_BASE * 16.0
    diag_a = shift * alpha_two[0] + sum_a + (middle + edge)
    diag_b = shift * alpha_two[1] + sum_b + (middle + inner)
    inv_a, inv_b = inverse(diag_a), inverse(diag_b)
    flat_a, flat_b = scaled(faces_a, inv_a), scaled(faces_b, inv_b)
    middle_a, middle_b = middle * inv_a, middle * inv_b
    rim_a, inner_b = jnp.where(end, 0.0, edge) * inv_a, inner * inv_b
    rhs_a, rhs_b = b_two[0] * inv_a, b_two[1] * inv_b

    def apply_two(va, vb):
        ta = flat(va, flat_a, 1, 4) + (middle_a * vb + rim_a * outer(va, half)[0])
        tb = flat(vb, flat_b, 1, 4) + (middle_b * va + inner_b * lanes(vb, 64))
        return ta, tb

    def sweeps_two(before, now, factors):
        for carry, gain in factors:
            totals = apply_two(*now)
            new = []
            for v, old, rhs, total in zip(now, before or (None, None), (rhs_a, rhs_b), totals):
                base = (1.0 + carry - gain) * v + gain * rhs
                if carry != 0.0 and old is not None:
                    base = base - carry * old
                new.append(base + gain * total)
            before, now = now, new
        return now

    factors = chebyshev_factors(SWEEPS, SMOOTH_LOWER)
    ua, ub = sweeps_two(None, (factors[0][1] * rhs_a, factors[0][1] * rhs_b), factors[1:])
    ta, tb = apply_two(ua, ub)

    def restrict_whole(first, second):
        total = first + second
        total = total + jnp.where(row % 2 == 0, rows(total, -1), rows(total, 1))
        return total + jnp.where((lane // 4) % 2 == 0, lanes(total, -4), lanes(total, 4))

    second = (lane // 4) % 2 == 1

    def pack_low(value):
        return jnp.where(second, value[4:], value[:4])

    def outer_low(value):
        turned = lanes(value, 64)
        first_one, last_one = value[:1], value[-1:]
        before = jnp.where(second, lanes(last_one, 68), lanes(last_one, 61))
        after = jnp.where(second, lanes(first_one, 67), lanes(first_one, 60))
        before = jnp.concatenate([before, turned[:-1]], axis=0)
        after = jnp.concatenate([turned[1:], after], axis=0)
        return jnp.where(half == 0, before, after), turned

    b_low = 0.5 * pack_low(restrict_whole(diag_a * (rhs_a + ta - ua), diag_b * (rhs_b + tb - ub)))
    beta_low = 0.125 * pack_low(restrict_whole(beta_two[0], beta_two[1]))
    alpha_low = 0.125 * pack_low(restrict_whole(alpha_two[0], alpha_two[1]))
    slab = lax.broadcasted_iota(jnp.int32, (4,) + TILE, 0) + jnp.where(second, 4, 0)
    end_low = ((slab == 0) & (lane % 4 == 0) & (half == 0)) | ((slab == 7) & (lane % 4 == 3) & (half == 1))
    faces_low, sum_low = sides(beta_low, 2, 8)
    beyond, turned = outer_low(beta_low)
    inner_low = 0.5 * (beta_low + turned)
    edge_low = 0.5 * (beta_low + jnp.where(end_low, 0.0, beyond))
    inv_low = inverse(SHIFT_BASE * 64.0 * alpha_low + sum_low + (inner_low + edge_low))
    flat_low = scaled(faces_low, inv_low)
    rim_low = jnp.where(end_low, 0.0, edge_low) * inv_low
    inner_low = inner_low * inv_low
    rhs_low = b_low * inv_low
    before = v = None
    for carry, gain in chebyshev_factors(BOTTOM, BOTTOM_LOWER):
        if v is None:
            v = gain * rhs_low
            continue
        beyond, turned = outer_low(v)
        base = (1.0 + carry - gain) * v + gain * rhs_low
        if before is not None:
            base = base - carry * before
        total = flat(v, flat_low, 2, 8) + (inner_low * turned + rim_low * beyond)
        before, v = v, base + gain * total
    v = jnp.concatenate([jnp.where(second, lanes(v, 4), v), jnp.where(second, v, lanes(v, -4))], axis=0)
    va, vb = sweeps_two(None, (ua + v, ub + v), factors)
    for group in range(8):
        e2_s[group, 0] = va[group]
        e2_s[group, 1] = vb[group]

    chunk = chunk_of(x, y, z)
    place = 8 * z + chunk

    def fetch(offset, p, turn=0):
        index = jnp.clip(place + offset, 0, COUNT - 1)
        tile, out = e2_s[index % 8, p], None
        for slot in range(4):
            piece = pltpu.roll(tile, (128 + slot + turn - index // 8) % 128, 1)
            out = piece if out is None else jnp.where(lane % 4 == slot, piece, out)
        return out

    first = half == 0
    out[0] = jnp.where(first, fetch(-1, 0), fetch(1, 0))
    out[1] = jnp.where(first, fetch(-1, 1), fetch(1, 1))
    out[2] = jnp.where(first, fetch(-1, 1, 64), fetch(1, 1, 64))
    out[3] = jnp.where(first, fetch(-1, 0, 64), fetch(1, 0, 64))
    out[4] = fetch(0, 0)
    out[5] = fetch(0, 1)


def coarse(gathered):
    vmem = pl.BlockSpec(memory_space=pltpu.VMEM)
    return pl.pallas_call(
        coarse_kernel,
        out_shape=shape_of(6),
        in_specs=[vmem],
        out_specs=vmem,
        scratch_shapes=[scratch(COUNT, 2), scratch(8, 2)],
        compiler_params=pltpu.CompilerParams(vmem_limit_bytes=8 * 2**20),
        name="coarse",
    )(gathered)


def up_kernel(e_two, rim_even, rim_odd, own_b, halo_b, late, u1, b1, v4, *refs):
    pre, mid, (out, v_a, v_b, w_a, w_b, bx_s) = refs[:9], refs[9:18], refs[18:]
    zero, one = coefficient_planes(pre, mid, None)
    lane, row = lane_ids(), row_ids()
    _, from_even = halo_masks()
    factors = chebyshev_factors(SWEEPS, SMOOTH_LOWER)

    for p in range(1, 8):
        if p >= 4:
            k = 7 - p
            both = lanes(jnp.where(from_even, rim_odd[20 + 2 * k : 22 + 2 * k], rim_even[20 + 2 * k : 22 + 2 * k]), 64)
        else:
            both = jnp.where(from_even, rim_even[20 + 2 * p : 22 + 2 * p], rim_odd[20 + 2 * p : 22 + 2 * p])
        w_a[p] = jnp.where(lane % 2 == 0, both, lanes(both, 1)) + e_two[p // 2]
        if p >= 2:
            bx_s[p] = jnp.where(lane % 2 == 0, lanes(both, -1), both)
    for p in range(8, PLANES1):
        w_a[p] = u1[p - 8] + e_two[p // 2]
    w_a[PLANES1] = lanes(w_a[PLANES1 - 1], 64)
    pair = (Planes((0, w_b)), Planes((0, w_a)), None)
    w = smooth(pair, Planes((0, bx_s), (8, b1)), one[3], one[:3], factors, 2, PLANES1, 2, SPAN1)

    for p in range(11, PLANES):
        if p >= 16:
            start = Planes((16, late), (20, v4)).get(p, p + 1)[0]
        else:
            k = 4 * (15 - p)
            start = lanes(jnp.where(from_even, rim_odd[k : k + 4], rim_even[k : k + 4]), 64)
        e_one = w.get(p // 2, p // 2 + 1)[0]
        e_one = jnp.concatenate([e_one[:1], e_one[:1], e_one[1:], e_one[1:]], axis=0)
        v_a[p] = start + e_one
    v_a[PLANES] = lanes(v_a[PLANES - 1], 64)
    b, diag, coeffs = Planes((12, halo_b), (16, own_b)), zero[4], zero[:3]
    v = smooth((Planes((0, v_b)), Planes((0, v_a)), None), b, zero[3], coeffs, factors, 12, PLANES, 1, SPAN)
    low = (lane // 32) % 2 == 0
    for k in range(4):
        for o in range(2):
            parts = []
            for pp in range(2):
                p = 16 + k + 4 * pp
                value = v.get(p, p + 1)
                if o == 1:
                    value = (b.get(p, p + 1) + couple(v, p, p + 1, *coeffs, 1)) - diag.get(p, p + 1) * value
                parts.append(regroup([value[0, i] for i in range(4)], 0, 2, row))
            for i in range(GX):
                one, two = parts[0][i], parts[1][i]
                out[2 * i, pl.ds(o * 32 + k * 8, 8), :] = jnp.where(low, one, lanes(two, 32))
                out[2 * i + 1, pl.ds(o * 32 + k * 8, 8), :] = jnp.where(low, lanes(one, -32), two)


def up(*operands):
    return call(
        up_kernel, "up_strokes", operands, [jax.ShapeDtypeStruct((8, 64, 128), jnp.float32)],
        [scratch(25, 4), scratch(25, 4), scratch(13, 2), scratch(13, 2), scratch(8, 2)],
    )[0]


def unpack_kernel(in_ref, v_ref, r_ref, fields, turned, staged, left):
    z = lax.axis_index("gz")
    lane = lane_ids()
    for x in range(GX):
        for y in range(GY):
            start = pl.multiple_of(chunk_of(x, y, z) * 64, 64)
            staged[pl.ds(start, 64), :] = in_ref[x * GY + y]
    copies = [pltpu.make_async_copy(fields.at[o], ref, left.at[o]) for o, ref in enumerate((v_ref, r_ref))]
    for o, copy in enumerate(copies):
        for xg in range(2):
            slot = turned.at[2 * o + xg]
            for k in range(4):
                tiles = [staged[pl.ds(o * 32 + k * 8 + 2 * x4 + xg, 8, stride=64), :] for x4 in range(4)]
                for g, tile in enumerate(regroup(tiles, 1, 32, lane)):
                    slot[pl.ds(depth_of(k, g), 8, stride=16), :] = tile
            fields[o, 4 * xg : 4 * xg + 4] = slot[...].T.reshape(4, 32, 128)
        copy.start()
    for copy in copies:
        copy.wait()


def unpack(received):
    vmem = pl.BlockSpec(memory_space=pltpu.VMEM)
    return pl.pallas_call(
        unpack_kernel,
        out_shape=[jax.ShapeDtypeStruct(BLOCK, jnp.float32)] * 2,
        in_specs=[vmem],
        out_specs=[pl.BlockSpec(memory_space=pltpu.HBM)] * 2,
        scratch_shapes=[
            pltpu.VMEM((2,) + BLOCK, jnp.float32),
            pltpu.VMEM((4, 128, 128), jnp.float32),
            pltpu.VMEM((512, 128), jnp.float32),
            pltpu.SemaphoreType.DMA((2,)),
        ],
        compiler_params=pltpu.CompilerParams(vmem_limit_bytes=4 * 2**20),
        name="unpack",
    )(received)


def slab_shards(right_side, alpha_coef, beta_coef):
    even_pairs, odd_pairs = swap_pairs(False), swap_pairs(True)
    packed = pack(jnp.stack([alpha_coef, beta_coef, right_side]))
    own, own_b, to_even, to_odd = to_slab(lax.all_to_all(packed, RING, 0, 0))
    even = lax.ppermute(to_even, ALL, even_pairs)
    odd = lax.ppermute(to_odd, ALL, odd_pairs)
    found = down_pre(own, own_b)
    pre, v4 = found[:9], found[15]
    gather, rim, halo_b, late, u1, b1, *mid = down_post(own, own_b, even, odd, found)
    rim_even = lax.ppermute(rim, ALL, even_pairs)
    rim_odd = lax.ppermute(rim, ALL, odd_pairs)
    kept = (own_b, halo_b, late, u1, b1, v4, *pre, *mid)
    result = up(coarse(lax.all_to_all(gather, ALL, 0, 0)), rim_even, rim_odd, *kept)
    return tuple(unpack(lax.all_to_all(result, RING, 0, 0)))


def solution(mesh):
    spec = P("gx", "gy", "gz")
    plain = jax.shard_map(shards, mesh=mesh, in_specs=(spec,) * 3, out_specs=(spec,) * 2, check_vma=False)
    slabs = jax.shard_map(slab_shards, mesh=mesh, in_specs=(spec,) * 3, out_specs=(spec,) * 2, check_vma=False)
    sizes = tuple(mesh.shape[axis] for axis in ALL)

    def run(right_side, alpha_coef, beta_coef):
        block = tuple(n // size for n, size in zip(right_side.shape, sizes))
        fits = sizes == (GX, GY, GZ) and block == BLOCK
        return (slabs if fits else plain)(right_side, alpha_coef, beta_coef)

    return run
```

```python
import jax
import jax.numpy as jnp
from jax import lax
from jax.experimental import pallas as pl
from jax.experimental.pallas import tpu as pltpu
from jax.sharding import PartitionSpec as P

LEVELS = 3
SWEEPS = 4
BOTTOM = 12


SHIFT_BASE = 0.01
UPPER_EIG = 2.0
SMOOTH_LOWER = 0.25
BOTTOM_LOWER = 0.02


def with_halo(block, sides, width):
    for axis, dim in sides:
        count = lax.axis_size(axis)
        forward = [(i, i + 1) for i in range(count - 1)]
        backward = [(target, source) for source, target in forward]
        low = lax.ppermute(
            lax.slice_in_dim(block, block.shape[dim] - width, None, axis=dim), axis, forward
        )
        high = lax.ppermute(lax.slice_in_dim(block, 0, width, axis=dim), axis, backward)
        block = jnp.concatenate([low, block, high], axis=dim)
    return block


def partner_2(array, axis, distance):
    return lax.ppermute(array, axis, [(i, i ^ 1 << distance) for i in range(lax.axis_size(axis))])


def split_padded(padded):
    return (
        padded[:-2, 1:-1, 1:-1],
        padded[2:, 1:-1, 1:-1],
        padded[1:-1, :-2, 1:-1],
        padded[1:-1, 2:, 1:-1],
        padded[1:-1, 1:-1, :-2],
        padded[1:-1, 1:-1, 2:],
    )


def zero_pad(field):
    return jnp.pad(field, 1)


def rim_iterate(field):
    return with_halo(field, (("gx", 0), ("gy", 1), ("gz", 2)), 1)


def rim_coefficient(field):
    return with_halo(field, (("gx", 0), ("gy", 1), ("gz", 2)), 1)


def level_operator(beta_level, alpha_level, padded_beta, shift):
    coeffs = tuple((0.5 * (beta_level + other) for other in split_padded(padded_beta)))
    diagonal = shift * alpha_level
    for coeff in coeffs:
        diagonal = diagonal + coeff
    return (coeffs, diagonal)


def apply_operator(field, operator, pad_field):
    coeffs, diagonal = operator
    others = split_padded(pad_field(field))
    total = coeffs[0] * others[0]
    for index in range(1, 6):
        total = total + coeffs[index] * others[index]
    return diagonal * field - total


def chebyshev(iterate, rhs_level, operator, count, lower, zero_start, pad_field):
    diagonal = operator[1]
    center = (UPPER_EIG + lower) / 2.0
    half_width = (UPPER_EIG - lower) / 2.0
    sigma_ratio = center / half_width
    rho_old = 1.0 / sigma_ratio
    if zero_start:
        remain = rhs_level
    else:
        remain = rhs_level - apply_operator(iterate, operator, pad_field)
    update = remain / diagonal / center
    iterate = iterate + update
    for sweep_index in range(count - 1):
        remain = rhs_level - apply_operator(iterate, operator, pad_field)
        rho_new = 1.0 / (2.0 * sigma_ratio - rho_old)
        update = rho_new * rho_old * update + 2.0 * rho_new / half_width * (remain / diagonal)
        iterate = iterate + update
        rho_old = rho_new
    return iterate


def restrict_mean(field):
    first, second, third = field.shape
    blocks = field.reshape(first // 2, 2, second // 2, 2, third // 2, 2)
    return jnp.sum(blocks, axis=(1, 3, 5)) * 0.125


def prolong_copy(field):
    return jnp.repeat(jnp.repeat(jnp.repeat(field, 2, axis=0), 2, axis=1), 2, axis=2)


def join_partner(packed, partner, device_index, bit_index, dim):
    position = device_index // 2**bit_index % 2
    lower_first = jnp.concatenate([packed, partner], axis=dim)
    upper_first = jnp.concatenate([partner, packed], axis=dim)
    return jnp.where(position == 0, lower_first, upper_first)


def shards(right_side, alpha_coef, beta_coef):
    betas = [beta_coef]
    alphas = [alpha_coef]
    for level in range(LEVELS):
        betas.append(restrict_mean(betas[-1]))
        alphas.append(restrict_mean(alphas[-1]))
    operators = []
    for level in range(LEVELS):
        padded_beta = rim_coefficient(betas[level])
        operators.append(
            level_operator(betas[level], alphas[level], padded_beta, SHIFT_BASE * 4.0**level)
        )
    rhs_levels = [right_side]
    smoothed = []
    for level in range(LEVELS):
        iterate = chebyshev(
            jnp.zeros_like(rhs_levels[level]),
            rhs_levels[level],
            operators[level],
            SWEEPS,
            SMOOTH_LOWER,
            True,
            rim_iterate,
        )
        remain = rhs_levels[level] - apply_operator(iterate, operators[level], rim_iterate)
        smoothed.append(iterate)
        rhs_levels.append(4.0 * restrict_mean(remain))
    coarse_rhs = rhs_levels[LEVELS]
    local_shape = coarse_rhs.shape
    packed = jnp.stack([coarse_rhs, betas[LEVELS], alphas[LEVELS]])
    index_x = lax.axis_index("gx")
    index_y = lax.axis_index("gy")
    index_z = lax.axis_index("gz")
    for bit_index in range(lax.axis_size("gx").bit_length() - 1):
        partner = partner_2(packed, "gx", bit_index)
        packed = join_partner(packed, partner, index_x, bit_index, 1)
    for bit_index in range(lax.axis_size("gy").bit_length() - 1):
        partner = partner_2(packed, "gy", bit_index)
        packed = join_partner(packed, partner, index_y, bit_index, 2)
    for bit_index in range(lax.axis_size("gz").bit_length() - 1):
        partner = partner_2(packed, "gz", bit_index)
        packed = join_partner(packed, partner, index_z, bit_index, 3)
    whole_rhs = packed[0]
    whole_beta = packed[1]
    whole_alpha = packed[2]
    bottom_operator = level_operator(
        whole_beta, whole_alpha, zero_pad(whole_beta), SHIFT_BASE * 4.0**LEVELS
    )
    whole_correction = chebyshev(
        jnp.zeros_like(whole_rhs), whole_rhs, bottom_operator, BOTTOM, BOTTOM_LOWER, True, zero_pad
    )
    starts = (index_x * local_shape[0], index_y * local_shape[1], index_z * local_shape[2])
    correction = lax.dynamic_slice(whole_correction, starts, local_shape)
    for level in range(LEVELS - 1, -1, -1):
        start_field = smoothed[level] + prolong_copy(correction)
        correction = chebyshev(
            start_field,
            rhs_levels[level],
            operators[level],
            SWEEPS,
            SMOOTH_LOWER,
            False,
            rim_iterate,
        )
    residual_field = right_side - apply_operator(correction, operators[0], rim_iterate)
    return (correction, residual_field)


GX, GY, GZ = 4, 2, 4
COUNT = GX * GY * GZ
RIM = 28
BLOCK = (8, 32, 128)
RING = ("gy", "gx")
ALL = ("gx", "gy", "gz")
TILE = (8, 128)
PLANES = 24
PLANES1 = 12
SPAN, SPAN1, COEF_SPAN, COEF_SPAN1 = 2, 4, 2, 4


def chunk_of(x, y, z):
    natural = 2 * (x ^ (x >> 1)) + y
    return natural + (z % 2) * (7 - 2 * natural)


def position():
    return lax.axis_index("gx"), lax.axis_index("gy"), lax.axis_index("gz")


def swap_pairs(odd):
    place = {}
    for x in range(GX):
        for y in range(GY):
            for z in range(GZ):
                place[8 * z + chunk_of(x, y, z)] = (x * GY + y) * GZ + z
    count = len(place)
    if odd:
        pairs = [(i, i + 1) for i in range(1, count - 1, 2)]
    else:
        pairs = [(i, i + 1) for i in range(0, count, 2)]
    return [(place[a], place[b]) for a, b in pairs] + [(place[b], place[a]) for a, b in pairs]


def lane_ids():
    return lax.broadcasted_iota(jnp.int32, TILE, 1)


def row_ids():
    return lax.broadcasted_iota(jnp.int32, TILE, 0)


def lanes(value, shift):
    return pltpu.roll(value, shift % 128, value.ndim - 1)


def rows(value, shift):
    return pltpu.roll(value, shift % 8, value.ndim - 2)


def regroup(tiles, axis, width, ids):
    move = lanes if axis == 1 else rows
    group = ids // width % 4
    odd, upper = group % 2 == 1, group >= 2
    a, b, c, d = tiles
    turned = move(jnp.where(odd, a, b), width)
    a, b = jnp.where(odd, turned, a), jnp.where(odd, b, turned)
    turned = move(jnp.where(odd, c, d), width)
    c, d = jnp.where(odd, turned, c), jnp.where(odd, d, turned)
    turned = move(jnp.where(upper, a, c), 2 * width)
    a, c = jnp.where(upper, turned, a), jnp.where(upper, c, turned)
    turned = move(jnp.where(upper, b, d), 2 * width)
    own = jnp.where(upper, d, b)
    inner = odd != upper
    return [a, jnp.where(inner, own, turned), c, jnp.where(inner, turned, own)]


def depth_of(k, group):
    half, part = group // 2, group % 2
    plane = k + 4 * part
    return 15 - plane if half else plane


def pack_kernel(fields, out_ref, turned, staged):
    z = lax.axis_index("gz")
    lane = lane_ids()
    for a in range(3):
        for xg in range(2):
            slot = turned.at[2 * a + xg]
            slot[...] = fields[a, 4 * xg : 4 * xg + 4].reshape(128, 128).T
            for k in range(4):
                tiles = [slot[pl.ds(depth_of(k, g), 8, stride=16), :] for g in range(4)]
                for x4, tile in enumerate(regroup(tiles, 1, 32, lane)):
                    staged[pl.ds(a * 32 + k * 8 + 2 * x4 + xg, 8, stride=96), :] = tile
    for x in range(GX):
        for y in range(GY):
            start = pl.multiple_of(chunk_of(x, y, z) * 96, 96)
            out_ref[y * GX + x] = staged[pl.ds(start, 96), :]


def pack(fields):
    return pl.pallas_call(
        pack_kernel,
        out_shape=jax.ShapeDtypeStruct((8, 96, 128), jnp.float32),
        in_specs=[pl.BlockSpec(memory_space=pltpu.VMEM)],
        out_specs=pl.BlockSpec(memory_space=pltpu.VMEM),
        scratch_shapes=[pltpu.VMEM((6, 128, 128), jnp.float32), pltpu.VMEM((768, 128), jnp.float32)],
        compiler_params=pltpu.CompilerParams(vmem_limit_bytes=4 * 2**20),
        name="pack",
    )(fields)


def shape_of(*dims):
    return jax.ShapeDtypeStruct(dims + TILE, jnp.float32)


def scratch(*dims):
    return pltpu.VMEM(dims + TILE, jnp.float32)


def halo_masks():
    x, y, z = position()
    chunk = chunk_of(x, y, z)
    half = lane_ids() // 64
    return chunk, (half + chunk % 2) == 1


PLACE = [(r, True) for r in range(6)] + [(4, False), (5, False), (3, False), (2, False), (1, False), (0, False)]
PLACE += [(6, False), (6, True)]
FIRST_TILE = (0, 6, 13)
MESSAGE = 19


def message(planes, near, count):
    tiles = [jnp.where(near, planes[t], planes[t + 4]) for t in range(4)]
    tiles += [jnp.where(near, planes[t], lanes(planes[t + 2], 64)) for t in (4, 5)]
    if count == 7:
        tiles.append(jnp.where(near, lanes(planes[2], 64), planes[3]))
    return tiles


def halo_plane(even, odd, a, r, from_even):
    tile, moved = PLACE[r]
    tile = FIRST_TILE[a] + tile
    if moved:
        return lanes(jnp.where(from_even, odd[tile], even[tile]), 64)
    return jnp.where(from_even, even[tile], odd[tile])


def slab_kernel(in_ref, out_ref, b_ref, even_ref, odd_ref):
    lane, row = lane_ids(), row_ids()
    low = (lane // 32) % 2 == 0
    _, from_even = halo_masks()
    for a in range(3):
        planes = [None] * 8
        for k in range(4):
            part = ([], [])
            for x in range(GX):
                first = in_ref[x, pl.ds(a * 32 + k * 8, 8), :]
                second = in_ref[GX + x, pl.ds(a * 32 + k * 8, 8), :]
                part[0].append(jnp.where(low, first, lanes(second, 32)))
                part[1].append(jnp.where(low, lanes(first, -32), second))
            for pp in range(2):
                planes[k + 4 * pp] = jnp.stack(regroup(part[pp], 0, 2, row))
                if a == 2:
                    b_ref[k + 4 * pp] = planes[k + 4 * pp]
                else:
                    out_ref[a, k + 4 * pp] = planes[k + 4 * pp]
        count = 7 if a == 1 else 6
        for near, ref in ((from_even, even_ref), (~from_even, odd_ref)):
            for t, tile in enumerate(message(planes, near, count)):
                ref[FIRST_TILE[a] + t] = tile


def to_slab(received):
    vmem = pl.BlockSpec(memory_space=pltpu.VMEM)
    return pl.pallas_call(
        slab_kernel,
        out_shape=[shape_of(2, 8, 4), shape_of(8, 4), shape_of(MESSAGE, 4), shape_of(MESSAGE, 4)],
        in_specs=[vmem],
        out_specs=[vmem] * 4,
        compiler_params=pltpu.CompilerParams(vmem_limit_bytes=4 * 2**20),
        name="to_slab",
    )(received)


class Planes:
    def __init__(self, *segments):
        self.segments = [(first, first + ref.shape[0], ref) for first, ref in segments]

    def find(self, p, q):
        for first, last, ref in self.segments:
            low, high = max(p, first), min(q, last)
            if low < high:
                yield low, high, ref, slice(low - first, high - first)

    def get(self, p, q):
        pieces = [ref[place] for _, _, ref, place in self.find(p, q)]
        return pieces[0] if len(pieces) == 1 else jnp.concatenate(pieces, axis=0)

    def put(self, p, value):
        for low, high, ref, place in self.find(p, p + value.shape[0]):
            ref[place] = value[low - p : high - p]


def spans(first, last, size):
    return [(p, min(p + size, last)) for p in range(first, last, size)]


def x_up(value):
    return jnp.concatenate([value[:, 1:], rows(value[:, :1], -1)], axis=1)


def x_down(value):
    return jnp.concatenate([rows(value[:, -1:], 1), value[:, :-1]], axis=1)


def couple(v, p, q, cx, cy, cz, dup):
    here, by_x, by_y = v.get(p, q), cx.get(p, q), cy.get(p, q)
    total = by_x * x_up(here) + x_down(by_x * here)
    total = total + (by_y * lanes(here, -dup) + lanes(by_y * here, dup))
    return total + (cz.get(p, q) * v.get(p - 1, q - 1) + cz.get(p + 1, q + 1) * v.get(p + 1, q + 1))


def chebyshev_factors(count, lower):
    center = (UPPER_EIG + lower) / 2.0
    half_width = (UPPER_EIG - lower) / 2.0
    ratio = center / half_width
    old = 1.0 / ratio
    out = [(0.0, 1.0 / center)]
    for _ in range(count - 1):
        new = 1.0 / (2.0 * ratio - old)
        out.append((new * old, 2.0 * new / half_width))
        old = new
    return out


def sweep(new, now, before, factor, b, dinv, coeffs, p, q, dup, size):
    carry, gain = factor
    for p, q in spans(p, q, size):
        base = (1.0 + carry - gain) * now.get(p, q)
        if carry != 0.0 and before is not None:
            base = base - carry * before.get(p, q)
        new.put(p, (b.get(p, q) + couple(now, p, q, *coeffs, dup)) * (gain * dinv.get(p, q)) + base)


def close(v, last):
    v.put(last, lanes(v.get(last - 1, last), 64))


def smooth(pair, b, dinv, coeffs, factors, first, last, dup, size):
    before, now, spare = pair
    for number, factor in enumerate(factors):
        new = spare if before is None else before
        sweep(new, now, before, factor, b, dinv, coeffs, first + number, last, dup, size)
        close(new, last)
        before, now = now, new
    return now


def inverse(value):
    guess = pl.reciprocal(value, approx=True)
    return guess * (2.0 - value * guess)


def level_coefficients(beta, alpha, first, last, shift, dup, cx, cy, cz, dinv, diag, ends, seam, size):
    lane, row = lane_ids(), row_ids()
    y_last = (lane % 64) // dup == 64 // dup - 1
    y_first = (lane % 64) // dup == 0
    x_rim = jnp.where(row == 0, 0.5, 0.0), jnp.where(row == 7, 0.5, 0.0)
    for p, q in spans(first, last, size):
        here = beta.get(p, q)
        by_x = 0.5 * (here + x_up(here))
        by_x = jnp.concatenate([by_x[:, :-1], jnp.where(row == 7, 0.0, by_x[:, -1:])], axis=1)
        above = jnp.where(y_last, 0.0, lanes(here, -dup))
        below = jnp.where(y_first, 0.0, lanes(here, dup))
        by_y = jnp.where(y_last, 0.0, 0.5 * (here + above))
        face = 0.5 * (beta.get(p - 1, q - 1) + here)
        total = shift * alpha.get(p, q) + (by_x + x_down(by_x)) + (here + 0.5 * (above + below))
        total = total + (face + 0.5 * (here + beta.get(p + 1, q + 1)))
        groups = [total[:, i : i + 1] for i in range(total.shape[1])]
        groups[0] = groups[0] + here[:, :1] * x_rim[0]
        groups[-1] = groups[-1] + here[:, -1:] * x_rim[1]
        total = jnp.concatenate(groups, axis=1)
        cx.put(p, by_x)
        cy.put(p, by_y)
        cz.put(p, face)
        diag.put(p, total)
        dinv.put(p, inverse(jnp.where(total > 0.0, total, 1.0)))
    if first <= seam < last:
        cz.put(seam, cz.get(seam, seam + 1) * ends)
    else:
        cz.put(last, 0.5 * (beta.get(last - 1, last) + beta.get(last, last + 1)))


def restrict_pair(first, second, dup):
    lane = lane_ids()
    total = first + second
    total = jnp.concatenate([total[:, i : i + 1] + total[:, i + 1 : i + 2] for i in range(0, total.shape[1], 2)], axis=1)
    return total + jnp.where((lane // dup) % 2 == 0, lanes(total, -dup), lanes(total, dup))


def restrict(take, p, q, dup):
    fine = take(2 * p, 2 * q)
    fine = fine.reshape((q - p, 2) + fine.shape[1:])
    return restrict_pair(fine[:, 0], fine[:, 1], dup)


def ends_factor():
    x, y, z = position()
    slab = 8 * z + chunk_of(x, y, z)
    half = lane_ids() // 64
    end = ((half == 0) & (slab == 0)) | ((half == 1) & (slab == 8 * GZ - 1))
    return jnp.where(end, 0.0, 1.0)


def call(kernel, name, operands, out_shape, scratch_shapes):
    vmem = pl.BlockSpec(memory_space=pltpu.VMEM)
    return pl.pallas_call(
        kernel,
        out_shape=out_shape,
        in_specs=[vmem] * len(operands),
        out_specs=[vmem] * len(out_shape),
        scratch_shapes=scratch_shapes,
        compiler_params=pltpu.CompilerParams(vmem_limit_bytes=16 * 2**20),
        name=name,
    )(*operands)


PRE_SHAPES = [(7, 4), (7, 4), (8, 4), (7, 4), (7, 4), (3, 2), (3, 2), (4, 2), (3, 2), (3, 2)]
MID_SHAPES = [(5, 4), (5, 4), (5, 4), (5, 4), (1, 4), (7, 2), (7, 2), (7, 2), (7, 2)]
LOW_SHAPES = [(8, 4), (8, 4), (8, 4), (8, 4), (12, 4), (7, 2)]


def coefficient_planes(pre, mid, low):
    zero, one = [], []
    for i in range(5):
        parts = [(4, low[i])] if low else []
        parts += [(16 if i == 4 else 12, mid[i])] if mid else []
        zero.append(Planes(*parts, *([(17, pre[i])] if pre else [])))
        parts = []
        if mid and i < 4:
            parts = [(2, mid[5 + i])]
        elif low and i == 4:
            parts = [(2, low[5])]
        one.append(Planes(*parts, *([(9, pre[5 + i])] if pre and len(pre) > 5 + i else [])))
    return zero, one


def pre_kernel(own, own_b, *refs):
    pre, (alpha1, beta1, v1, v2, v3, v4), (ghost, ghost1) = refs[:10], refs[10:16], refs[16:]
    zero, one = coefficient_planes(pre, None, None)
    alpha, beta = Planes((16, own.at[0])), Planes((16, own.at[1]), (24, ghost))
    alpha_one, beta_one = Planes((8, alpha1)), Planes((8, beta1), (12, ghost1))
    close(beta, PLANES)
    level_coefficients(beta, alpha, 17, PLANES, SHIFT_BASE, 1, *zero, None, 16, COEF_SPAN)
    beta_one.put(8, 0.125 * restrict(beta.get, 8, PLANES1, 1))
    alpha_one.put(8, 0.125 * restrict(alpha.get, 8, PLANES1, 1))
    close(beta_one, PLANES1)
    level_coefficients(beta_one, alpha_one, 9, PLANES1, SHIFT_BASE * 4.0, 2, *one, None, 8, COEF_SPAN1)
    b, coeffs, dinv = Planes((16, own_b)), zero[:3], zero[3]
    factors = chebyshev_factors(SWEEPS, SMOOTH_LOWER)
    iterates = [None, Planes((17, v1)), Planes((18, v2)), Planes((19, v3)), Planes((20, v4))]
    for p, q in spans(17, PLANES, 4):
        iterates[1].put(p, factors[0][1] * (b.get(p, q) * dinv.get(p, q)))
    close(iterates[1], PLANES)
    for i in range(2, 5):
        sweep(iterates[i], iterates[i - 1], iterates[i - 2], factors[i - 1], b, dinv, coeffs, 16 + i, PLANES, 1, SPAN)
        close(iterates[i], PLANES)


def mid_part(own, even, odd, beta1_own, alpha1_own, mid, low, beta_s, alpha_s, beta1_s, alpha1_s):
    _, from_even = halo_masks()
    zero, one = coefficient_planes(None, mid, low)
    for p in range(2, 16):
        beta_s[p] = halo_plane(even, odd, 1, 15 - p, from_even)
        if p >= 4:
            alpha_s[p] = halo_plane(even, odd, 0, 15 - p, from_even)
    beta, alpha = Planes((0, beta_s), (16, own.at[1])), Planes((0, alpha_s), (16, own.at[0]))
    ends = ends_factor()
    level_coefficients(beta, alpha, 4, 17, SHIFT_BASE, 1, *zero, ends, 16, COEF_SPAN)
    beta_one, alpha_one = Planes((0, beta1_s), (8, beta1_own)), Planes((0, alpha1_s), (8, alpha1_own))
    for p in range(1, 8):
        beta_one.put(p, 0.125 * restrict(beta.get, p, p + 1, 1))
        if p >= 2:
            alpha_one.put(p, 0.125 * restrict(alpha.get, p, p + 1, 1))
    level_coefficients(beta_one, alpha_one, 2, 9, SHIFT_BASE * 4.0, 2, *one, ends, 8, COEF_SPAN1)


def post_kernel(own, own_b, odd, even, *refs):
    pre, (alpha1, beta1, v1, v2, v3, v4), (gather, rim, halo_b, late, u1, b1) = refs[:10], refs[10:16], refs[16:22]
    mid, low, (f1, f2, f3, f4, low_b, b1_s, w_a, w_b), scratch_mid = refs[22:31], refs[31:37], refs[37:45], refs[45:]
    mid_part(own, even, odd, beta1, alpha1, mid, low, *scratch_mid)
    lane = lane_ids()
    _, from_even = halo_masks()
    zero, one = coefficient_planes(pre, mid, low)
    coeffs, dinv, diag = zero[:3], zero[3], zero[4]
    b = Planes((4, low_b), (12, halo_b), (16, own_b))
    for p in range(4, 16):
        b.put(p, halo_plane(even, odd, 2, 15 - p, from_even)[None])
    factors = chebyshev_factors(SWEEPS, SMOOTH_LOWER)
    iterates = [
        None,
        Planes((4, f1), (17, v1)),
        Planes((5, f2), (18, v2)),
        Planes((6, f3), (19, v3)),
        Planes((7, f4), (16, late), (20, v4)),
    ]
    for p, q in spans(4, 17, 4):
        iterates[1].put(p, factors[0][1] * (b.get(p, q) * dinv.get(p, q)))
    for i in range(2, 5):
        sweep(iterates[i], iterates[i - 1], iterates[i - 2], factors[i - 1], b, dinv, coeffs, 3 + i, 16 + i, 1, SPAN)
    v = iterates[4]
    rim[0:20] = v.get(16, 21).reshape((20,) + TILE)

    def residual(v, b, diag, coeffs, dup):
        return lambda p, q: (b.get(p, q) + couple(v, p, q, *coeffs, dup)) - diag.get(p, q) * v.get(p, q)

    b_one = Planes((4, b1_s), (8, b1))
    for p in range(4, PLANES1):
        b_one.put(p, 0.5 * restrict(residual(v, b, diag, coeffs, 1), p, p + 1, 1))
    coeffs, dinv, diag = one[:3], one[3], one[4]
    w, spare = Planes((0, w_a)), Planes((0, w_b))
    w.put(4, factors[0][1] * (b_one.get(4, PLANES1) * dinv.get(4, PLANES1)))
    close(w, PLANES1)
    w = smooth((None, w, spare), b_one, dinv, coeffs, factors[1:], 5, PLANES1, 2, SPAN1)
    b_two = 0.5 * restrict(residual(w, b_one, diag, coeffs, 2), 4, 6, 2)
    beta_two = 0.125 * restrict(Planes((8, beta1)).get, 4, 6, 2)
    alpha_two = 0.125 * restrict(Planes((8, alpha1)).get, 4, 6, 2)
    slot = lane % 4
    both = jnp.where(slot < 2, *(jnp.where(slot % 2 == 0, field[0, 0], field[1, 0]) for field in (b_two, beta_two)))
    last = jnp.where(slot % 2 == 0, alpha_two[0, 0], alpha_two[1, 0])
    last = jnp.where(slot[:4] < 2, last[:4], last[4:])
    for n in range(COUNT):
        for i, part in enumerate((both[:4], both[4:], last)):
            gather[n, i] = part
    u1[...] = w.get(8, PLANES1)
    rim[20:28] = jnp.where(lane % 2 == 0, w.get(8, PLANES1), b_one.get(8, PLANES1)).reshape((8,) + TILE)


def down_pre(own, own_b):
    shapes = PRE_SHAPES + [(4, 2), (4, 2), (8, 4), (7, 4), (6, 4), (5, 4)]
    return call(pre_kernel, "down_pre", (own, own_b), [shape_of(*n) for n in shapes], [scratch(1, 4), scratch(1, 2)])


def down_post(own, own_b, even, odd, pre):
    shapes = [shape_of(*n) for n in [(RIM,), (4, 4), (4, 4), (4, 2), (4, 2), *MID_SHAPES]]
    spare = [(13, 4), (13, 4), (13, 4), (9, 4), (8, 4), (4, 2), (13, 2), (13, 2), (16, 4), (16, 4), (8, 2), (8, 2)]
    return call(
        post_kernel, "down_post", (own, own_b, odd, even, *pre),
        [jax.ShapeDtypeStruct((COUNT, 3, 4, 128), jnp.float32), *shapes], [scratch(*n) for n in LOW_SHAPES + spare],
    )


def outer(value, half):
    turned = lanes(value, 64)
    before = jnp.concatenate([lanes(value[-1:], 65), turned[:-1]], axis=0)
    after = jnp.concatenate([turned[1:], lanes(value[:1], 63)], axis=0)
    return jnp.where(half == 0, before, after), turned


def coarse_kernel(gathered, out, tiles_s, e2_s):
    lane, row = lane_ids(), row_ids()
    half = lane // 64
    x, y, z = position()
    for n in range(COUNT):
        tiles_s[n, 0] = jnp.concatenate([gathered[n, 0], gathered[n, 1]], axis=0)
        tiles_s[n, 1] = jnp.concatenate([gathered[n, 2], lanes(gathered[n, 2], -2)], axis=0)

    def collect(tile, slot):
        out = []
        for group in range(8):
            joined = None
            for q in range(GZ):
                natural = 7 - group if q % 2 else group
                rank, core = natural // 2, natural % 2
                n = ((rank ^ (rank >> 1)) * GZ + q) * GY + core
                piece = tiles_s[n, tile] if q == slot else lanes(tiles_s[n, tile], q - slot)
                joined = piece if joined is None else jnp.where(lane % 4 == q, piece, joined)
            out.append(joined)
        return jnp.stack(out)

    b_two, beta_two, alpha_two = ([collect(tile, slot + p) for p in range(2)] for tile, slot in ((0, 0), (0, 2), (1, 0)))
    slab = lax.broadcasted_iota(jnp.int32, (8,) + TILE, 0)
    end = ((slab == 0) & (lane % 4 == 0) & (half == 0)) | ((slab == 7) & (lane % 4 == 3) & (half == 1))

    def sides(beta, dx, dy):
        place = (lane % 64) // dy
        rims = row >= 8 - dx, row < dx, place == 64 // dy - 1, place == 0
        others = rows(beta, -dx), rows(beta, dx), lanes(beta, -dy), lanes(beta, dy)
        faces = [jnp.where(rim, 0.0, 0.5 * (beta + other)) for rim, other in zip(rims, others)]
        edge = jnp.where(rims[0] | rims[1], 0.5, 0.0) + jnp.where(rims[2] | rims[3], 0.5, 0.0)
        return faces, (faces[0] + faces[1]) + (faces[2] + faces[3]) + beta * edge

    def scaled(faces, inv):
        return [face * inv for face in faces]

    def flat(v, coeffs, dx, dy):
        x_above, x_below, y_above, y_below = coeffs
        total = x_above * rows(v, -dx) + x_below * rows(v, dx)
        return total + (y_above * lanes(v, -dy) + y_below * lanes(v, dy))

    faces_a, sum_a = sides(beta_two[0], 1, 4)
    faces_b, sum_b = sides(beta_two[1], 1, 4)
    middle = 0.5 * (beta_two[0] + beta_two[1])
    inner = 0.5 * (beta_two[1] + lanes(beta_two[1], 64))
    edge = 0.5 * (beta_two[0] + jnp.where(end, 0.0, outer(beta_two[0], half)[0]))
    shift = SHIFT_BASE * 16.0
    diag_a = shift * alpha_two[0] + sum_a + (middle + edge)
    diag_b = shift * alpha_two[1] + sum_b + (middle + inner)
    inv_a, inv_b = inverse(diag_a), inverse(diag_b)
    flat_a, flat_b = scaled(faces_a, inv_a), scaled(faces_b, inv_b)
    middle_a, middle_b = middle * inv_a, middle * inv_b
    rim_a, inner_b = jnp.where(end, 0.0, edge) * inv_a, inner * inv_b
    rhs_a, rhs_b = b_two[0] * inv_a, b_two[1] * inv_b

    def apply_two(va, vb):
        ta = flat(va, flat_a, 1, 4) + (middle_a * vb + rim_a * outer(va, half)[0])
        tb = flat(vb, flat_b, 1, 4) + (middle_b * va + inner_b * lanes(vb, 64))
        return ta, tb

    def sweeps_two(before, now, factors):
        for carry, gain in factors:
            totals = apply_two(*now)
            new = []
            for v, old, rhs, total in zip(now, before or (None, None), (rhs_a, rhs_b), totals):
                base = (1.0 + carry - gain) * v + gain * rhs
                if carry != 0.0 and old is not None:
                    base = base - carry * old
                new.append(base + gain * total)
            before, now = now, new
        return now

    factors = chebyshev_factors(SWEEPS, SMOOTH_LOWER)
    ua, ub = sweeps_two(None, (factors[0][1] * rhs_a, factors[0][1] * rhs_b), factors[1:])
    ta, tb = apply_two(ua, ub)

    def restrict_whole(first, second):
        total = first + second
        total = total + jnp.where(row % 2 == 0, rows(total, -1), rows(total, 1))
        return total + jnp.where((lane // 4) % 2 == 0, lanes(total, -4), lanes(total, 4))

    second = (lane // 4) % 2 == 1

    def pack_low(value):
        return jnp.where(second, value[4:], value[:4])

    def outer_low(value):
        turned = lanes(value, 64)
        first_one, last_one = value[:1], value[-1:]
        before = jnp.where(second, lanes(last_one, 68), lanes(last_one, 61))
        after = jnp.where(second, lanes(first_one, 67), lanes(first_one, 60))
        before = jnp.concatenate([before, turned[:-1]], axis=0)
        after = jnp.concatenate([turned[1:], after], axis=0)
        return jnp.where(half == 0, before, after), turned

    b_low = 0.5 * pack_low(restrict_whole(diag_a * (rhs_a + ta - ua), diag_b * (rhs_b + tb - ub)))
    beta_low = 0.125 * pack_low(restrict_whole(beta_two[0], beta_two[1]))
    alpha_low = 0.125 * pack_low(restrict_whole(alpha_two[0], alpha_two[1]))
    slab = lax.broadcasted_iota(jnp.int32, (4,) + TILE, 0) + jnp.where(second, 4, 0)
    end_low = ((slab == 0) & (lane % 4 == 0) & (half == 0)) | ((slab == 7) & (lane % 4 == 3) & (half == 1))
    faces_low, sum_low = sides(beta_low, 2, 8)
    beyond, turned = outer_low(beta_low)
    inner_low = 0.5 * (beta_low + turned)
    edge_low = 0.5 * (beta_low + jnp.where(end_low, 0.0, beyond))
    inv_low = inverse(SHIFT_BASE * 64.0 * alpha_low + sum_low + (inner_low + edge_low))
    flat_low = scaled(faces_low, inv_low)
    rim_low = jnp.where(end_low, 0.0, edge_low) * inv_low
    inner_low = inner_low * inv_low
    rhs_low = b_low * inv_low
    before = v = None
    for carry, gain in chebyshev_factors(BOTTOM, BOTTOM_LOWER):
        if v is None:
            v = gain * rhs_low
            continue
        beyond, turned = outer_low(v)
        base = (1.0 + carry - gain) * v + gain * rhs_low
        if before is not None:
            base = base - carry * before
        total = flat(v, flat_low, 2, 8) + (inner_low * turned + rim_low * beyond)
        before, v = v, base + gain * total
    v = jnp.concatenate([jnp.where(second, lanes(v, 4), v), jnp.where(second, v, lanes(v, -4))], axis=0)
    va, vb = sweeps_two(None, (ua + v, ub + v), factors)
    for group in range(8):
        e2_s[group, 0] = va[group]
        e2_s[group, 1] = vb[group]

    chunk = chunk_of(x, y, z)
    place = 8 * z + chunk

    def fetch(offset, p, turn=0):
        index = jnp.clip(place + offset, 0, COUNT - 1)
        tile, out = e2_s[index % 8, p], None
        for slot in range(4):
            piece = pltpu.roll(tile, (128 + slot + turn - index // 8) % 128, 1)
            out = piece if out is None else jnp.where(lane % 4 == slot, piece, out)
        return out

    first = half == 0
    out[0] = jnp.where(first, fetch(-1, 0), fetch(1, 0))
    out[1] = jnp.where(first, fetch(-1, 1), fetch(1, 1))
    out[2] = jnp.where(first, fetch(-1, 1, 64), fetch(1, 1, 64))
    out[3] = jnp.where(first, fetch(-1, 0, 64), fetch(1, 0, 64))
    out[4] = fetch(0, 0)
    out[5] = fetch(0, 1)


def coarse(gathered):
    vmem = pl.BlockSpec(memory_space=pltpu.VMEM)
    return pl.pallas_call(
        coarse_kernel,
        out_shape=shape_of(6),
        in_specs=[vmem],
        out_specs=vmem,
        scratch_shapes=[scratch(COUNT, 2), scratch(8, 2)],
        compiler_params=pltpu.CompilerParams(vmem_limit_bytes=8 * 2**20),
        name="coarse",
    )(gathered)


def up_kernel(e_two, rim_even, rim_odd, own_b, halo_b, late, u1, b1, v4, *refs):
    pre, mid, (out, v_a, v_b, w_a, w_b, bx_s) = refs[:9], refs[9:18], refs[18:]
    zero, one = coefficient_planes(pre, mid, None)
    lane, row = lane_ids(), row_ids()
    _, from_even = halo_masks()
    factors = chebyshev_factors(SWEEPS, SMOOTH_LOWER)

    for p in range(1, 8):
        if p >= 4:
            k = 7 - p
            both = lanes(jnp.where(from_even, rim_odd[20 + 2 * k : 22 + 2 * k], rim_even[20 + 2 * k : 22 + 2 * k]), 64)
        else:
            both = jnp.where(from_even, rim_even[20 + 2 * p : 22 + 2 * p], rim_odd[20 + 2 * p : 22 + 2 * p])
        w_a[p] = jnp.where(lane % 2 == 0, both, lanes(both, 1)) + e_two[p // 2]
        if p >= 2:
            bx_s[p] = jnp.where(lane % 2 == 0, lanes(both, -1), both)
    for p in range(8, PLANES1):
        w_a[p] = u1[p - 8] + e_two[p // 2]
    w_a[PLANES1] = lanes(w_a[PLANES1 - 1], 64)
    pair = (Planes((0, w_b)), Planes((0, w_a)), None)
    w = smooth(pair, Planes((0, bx_s), (8, b1)), one[3], one[:3], factors, 2, PLANES1, 2, SPAN1)

    for p in range(11, PLANES):
        if p >= 16:
            start = Planes((16, late), (20, v4)).get(p, p + 1)[0]
        else:
            k = 4 * (15 - p)
            start = lanes(jnp.where(from_even, rim_odd[k : k + 4], rim_even[k : k + 4]), 64)
        e_one = w.get(p // 2, p // 2 + 1)[0]
        e_one = jnp.concatenate([e_one[:1], e_one[:1], e_one[1:], e_one[1:]], axis=0)
        v_a[p] = start + e_one
    v_a[PLANES] = lanes(v_a[PLANES - 1], 64)
    b, diag, coeffs = Planes((12, halo_b), (16, own_b)), zero[4], zero[:3]
    v = smooth((Planes((0, v_b)), Planes((0, v_a)), None), b, zero[3], coeffs, factors, 12, PLANES, 1, SPAN)
    low = (lane // 32) % 2 == 0
    for k in range(4):
        for o in range(2):
            parts = []
            for pp in range(2):
                p = 16 + k + 4 * pp
                value = v.get(p, p + 1)
                if o == 1:
                    value = (b.get(p, p + 1) + couple(v, p, p + 1, *coeffs, 1)) - diag.get(p, p + 1) * value
                parts.append(regroup([value[0, i] for i in range(4)], 0, 2, row))
            for i in range(GX):
                one, two = parts[0][i], parts[1][i]
                out[i, pl.ds(o * 32 + k * 8, 8), :] = jnp.where(low, one, lanes(two, 32))
                out[GX + i, pl.ds(o * 32 + k * 8, 8), :] = jnp.where(low, lanes(one, -32), two)


def up(*operands):
    return call(
        up_kernel, "up_strokes", operands, [jax.ShapeDtypeStruct((8, 64, 128), jnp.float32)],
        [scratch(25, 4), scratch(25, 4), scratch(13, 2), scratch(13, 2), scratch(8, 2)],
    )[0]


def unpack_kernel(in_ref, v_ref, r_ref, fields, turned, staged, left):
    z = lax.axis_index("gz")
    lane = lane_ids()
    for x in range(GX):
        for y in range(GY):
            start = pl.multiple_of(chunk_of(x, y, z) * 64, 64)
            staged[pl.ds(start, 64), :] = in_ref[y * GX + x]
    copies = [pltpu.make_async_copy(fields.at[o], ref, left.at[o]) for o, ref in enumerate((v_ref, r_ref))]
    for o, copy in enumerate(copies):
        for xg in range(2):
            slot = turned.at[2 * o + xg]
            for k in range(4):
                tiles = [staged[pl.ds(o * 32 + k * 8 + 2 * x4 + xg, 8, stride=64), :] for x4 in range(4)]
                for g, tile in enumerate(regroup(tiles, 1, 32, lane)):
                    slot[pl.ds(depth_of(k, g), 8, stride=16), :] = tile
            fields[o, 4 * xg : 4 * xg + 4] = slot[...].T.reshape(4, 32, 128)
        copy.start()
    for copy in copies:
        copy.wait()


def unpack(received):
    vmem = pl.BlockSpec(memory_space=pltpu.VMEM)
    return pl.pallas_call(
        unpack_kernel,
        out_shape=[jax.ShapeDtypeStruct(BLOCK, jnp.float32)] * 2,
        in_specs=[vmem],
        out_specs=[pl.BlockSpec(memory_space=pltpu.HBM)] * 2,
        scratch_shapes=[
            pltpu.VMEM((2,) + BLOCK, jnp.float32),
            pltpu.VMEM((4, 128, 128), jnp.float32),
            pltpu.VMEM((512, 128), jnp.float32),
            pltpu.SemaphoreType.DMA((2,)),
        ],
        compiler_params=pltpu.CompilerParams(vmem_limit_bytes=4 * 2**20),
        name="unpack",
    )(received)


def slab_shards(right_side, alpha_coef, beta_coef):
    even_pairs, odd_pairs = swap_pairs(False), swap_pairs(True)
    packed = pack(jnp.stack([alpha_coef, beta_coef, right_side]))
    own, own_b, to_even, to_odd = to_slab(lax.all_to_all(packed, RING, 0, 0))
    even = lax.ppermute(to_even, ALL, even_pairs)
    odd = lax.ppermute(to_odd, ALL, odd_pairs)
    found = down_pre(own, own_b)
    pre, v4 = found[:9], found[15]
    gather, rim, halo_b, late, u1, b1, *mid = down_post(own, own_b, even, odd, found)
    rim_even = lax.ppermute(rim, ALL, even_pairs)
    rim_odd = lax.ppermute(rim, ALL, odd_pairs)
    kept = (own_b, halo_b, late, u1, b1, v4, *pre, *mid)
    result = up(coarse(lax.all_to_all(gather, ("gx", "gz", "gy"), 0, 0)), rim_even, rim_odd, *kept)
    return tuple(unpack(lax.all_to_all(result, RING, 0, 0)))


def solution(mesh):
    spec = P("gx", "gy", "gz")
    plain = jax.shard_map(shards, mesh=mesh, in_specs=(spec,) * 3, out_specs=(spec,) * 2, check_vma=False)
    slabs = jax.shard_map(slab_shards, mesh=mesh, in_specs=(spec,) * 3, out_specs=(spec,) * 2, check_vma=False)
    sizes = tuple(mesh.shape[axis] for axis in ALL)

    def run(right_side, alpha_coef, beta_coef):
        block = tuple(n // size for n, size in zip(right_side.shape, sizes))
        fits = sizes == (GX, GY, GZ) and block == BLOCK
        return (slabs if fits else plain)(right_side, alpha_coef, beta_coef)

    return run
```

```python
import jax
import jax.numpy as jnp
from jax import lax
from jax.experimental import pallas as pl
from jax.experimental.pallas import tpu as pltpu
from jax.sharding import PartitionSpec as P

LEVELS = 3
SWEEPS = 4
BOTTOM = 12


SHIFT_BASE = 0.01
UPPER_EIG = 2.0
SMOOTH_LOWER = 0.25
BOTTOM_LOWER = 0.02


def with_halo(block, sides, width):
    for axis, dim in sides:
        count = lax.axis_size(axis)
        forward = [(i, i + 1) for i in range(count - 1)]
        backward = [(target, source) for source, target in forward]
        low = lax.ppermute(
            lax.slice_in_dim(block, block.shape[dim] - width, None, axis=dim), axis, forward
        )
        high = lax.ppermute(lax.slice_in_dim(block, 0, width, axis=dim), axis, backward)
        block = jnp.concatenate([low, block, high], axis=dim)
    return block


def partner_2(array, axis, distance):
    return lax.ppermute(array, axis, [(i, i ^ 1 << distance) for i in range(lax.axis_size(axis))])


def split_padded(padded):
    return (
        padded[:-2, 1:-1, 1:-1],
        padded[2:, 1:-1, 1:-1],
        padded[1:-1, :-2, 1:-1],
        padded[1:-1, 2:, 1:-1],
        padded[1:-1, 1:-1, :-2],
        padded[1:-1, 1:-1, 2:],
    )


def zero_pad(field):
    return jnp.pad(field, 1)


def rim_iterate(field):
    return with_halo(field, (("gx", 0), ("gy", 1), ("gz", 2)), 1)


def rim_coefficient(field):
    return with_halo(field, (("gx", 0), ("gy", 1), ("gz", 2)), 1)


def level_operator(beta_level, alpha_level, padded_beta, shift):
    coeffs = tuple((0.5 * (beta_level + other) for other in split_padded(padded_beta)))
    diagonal = shift * alpha_level
    for coeff in coeffs:
        diagonal = diagonal + coeff
    return (coeffs, diagonal)


def apply_operator(field, operator, pad_field):
    coeffs, diagonal = operator
    others = split_padded(pad_field(field))
    total = coeffs[0] * others[0]
    for index in range(1, 6):
        total = total + coeffs[index] * others[index]
    return diagonal * field - total


def chebyshev(iterate, rhs_level, operator, count, lower, zero_start, pad_field):
    diagonal = operator[1]
    center = (UPPER_EIG + lower) / 2.0
    half_width = (UPPER_EIG - lower) / 2.0
    sigma_ratio = center / half_width
    rho_old = 1.0 / sigma_ratio
    if zero_start:
        remain = rhs_level
    else:
        remain = rhs_level - apply_operator(iterate, operator, pad_field)
    update = remain / diagonal / center
    iterate = iterate + update
    for sweep_index in range(count - 1):
        remain = rhs_level - apply_operator(iterate, operator, pad_field)
        rho_new = 1.0 / (2.0 * sigma_ratio - rho_old)
        update = rho_new * rho_old * update + 2.0 * rho_new / half_width * (remain / diagonal)
        iterate = iterate + update
        rho_old = rho_new
    return iterate


def restrict_mean(field):
    first, second, third = field.shape
    blocks = field.reshape(first // 2, 2, second // 2, 2, third // 2, 2)
    return jnp.sum(blocks, axis=(1, 3, 5)) * 0.125


def prolong_copy(field):
    return jnp.repeat(jnp.repeat(jnp.repeat(field, 2, axis=0), 2, axis=1), 2, axis=2)


def join_partner(packed, partner, device_index, bit_index, dim):
    position = device_index // 2**bit_index % 2
    lower_first = jnp.concatenate([packed, partner], axis=dim)
    upper_first = jnp.concatenate([partner, packed], axis=dim)
    return jnp.where(position == 0, lower_first, upper_first)


def shards(right_side, alpha_coef, beta_coef):
    betas = [beta_coef]
    alphas = [alpha_coef]
    for level in range(LEVELS):
        betas.append(restrict_mean(betas[-1]))
        alphas.append(restrict_mean(alphas[-1]))
    operators = []
    for level in range(LEVELS):
        padded_beta = rim_coefficient(betas[level])
        operators.append(
            level_operator(betas[level], alphas[level], padded_beta, SHIFT_BASE * 4.0**level)
        )
    rhs_levels = [right_side]
    smoothed = []
    for level in range(LEVELS):
        iterate = chebyshev(
            jnp.zeros_like(rhs_levels[level]),
            rhs_levels[level],
            operators[level],
            SWEEPS,
            SMOOTH_LOWER,
            True,
            rim_iterate,
        )
        remain = rhs_levels[level] - apply_operator(iterate, operators[level], rim_iterate)
        smoothed.append(iterate)
        rhs_levels.append(4.0 * restrict_mean(remain))
    coarse_rhs = rhs_levels[LEVELS]
    local_shape = coarse_rhs.shape
    packed = jnp.stack([coarse_rhs, betas[LEVELS], alphas[LEVELS]])
    index_x = lax.axis_index("gx")
    index_y = lax.axis_index("gy")
    index_z = lax.axis_index("gz")
    for bit_index in range(lax.axis_size("gx").bit_length() - 1):
        partner = partner_2(packed, "gx", bit_index)
        packed = join_partner(packed, partner, index_x, bit_index, 1)
    for bit_index in range(lax.axis_size("gy").bit_length() - 1):
        partner = partner_2(packed, "gy", bit_index)
        packed = join_partner(packed, partner, index_y, bit_index, 2)
    for bit_index in range(lax.axis_size("gz").bit_length() - 1):
        partner = partner_2(packed, "gz", bit_index)
        packed = join_partner(packed, partner, index_z, bit_index, 3)
    whole_rhs = packed[0]
    whole_beta = packed[1]
    whole_alpha = packed[2]
    bottom_operator = level_operator(
        whole_beta, whole_alpha, zero_pad(whole_beta), SHIFT_BASE * 4.0**LEVELS
    )
    whole_correction = chebyshev(
        jnp.zeros_like(whole_rhs), whole_rhs, bottom_operator, BOTTOM, BOTTOM_LOWER, True, zero_pad
    )
    starts = (index_x * local_shape[0], index_y * local_shape[1], index_z * local_shape[2])
    correction = lax.dynamic_slice(whole_correction, starts, local_shape)
    for level in range(LEVELS - 1, -1, -1):
        start_field = smoothed[level] + prolong_copy(correction)
        correction = chebyshev(
            start_field,
            rhs_levels[level],
            operators[level],
            SWEEPS,
            SMOOTH_LOWER,
            False,
            rim_iterate,
        )
    residual_field = right_side - apply_operator(correction, operators[0], rim_iterate)
    return (correction, residual_field)


GX, GY, GZ = 4, 2, 4
COUNT = GX * GY * GZ
RIM = 28
BLOCK = (8, 32, 128)
RING = ("gy", "gx")
ALL = ("gx", "gy", "gz")
TILE = (8, 128)
PLANES = 24
PLANES1 = 12
SPAN, SPAN1, COEF_SPAN, COEF_SPAN1 = 2, 4, 2, 4


def chunk_of(x, y, z):
    natural = 2 * (x ^ (x >> 1)) + y
    return natural + (z % 2) * (7 - 2 * natural)


def position():
    return lax.axis_index("gx"), lax.axis_index("gy"), lax.axis_index("gz")


def swap_pairs(odd):
    place = {}
    for x in range(GX):
        for y in range(GY):
            for z in range(GZ):
                place[8 * z + chunk_of(x, y, z)] = (x * GY + y) * GZ + z
    count = len(place)
    if odd:
        pairs = [(i, i + 1) for i in range(1, count - 1, 2)]
    else:
        pairs = [(i, i + 1) for i in range(0, count, 2)]
    return [(place[a], place[b]) for a, b in pairs] + [(place[b], place[a]) for a, b in pairs]


def lane_ids():
    return lax.broadcasted_iota(jnp.int32, TILE, 1)


def row_ids():
    return lax.broadcasted_iota(jnp.int32, TILE, 0)


def lanes(value, shift):
    return pltpu.roll(value, shift % 128, value.ndim - 1)


def rows(value, shift):
    return pltpu.roll(value, shift % 8, value.ndim - 2)


def regroup(tiles, axis, width, ids):
    move = lanes if axis == 1 else rows
    group = ids // width % 4
    odd, upper = group % 2 == 1, group >= 2
    a, b, c, d = tiles
    turned = move(jnp.where(odd, a, b), width)
    a, b = jnp.where(odd, turned, a), jnp.where(odd, b, turned)
    turned = move(jnp.where(odd, c, d), width)
    c, d = jnp.where(odd, turned, c), jnp.where(odd, d, turned)
    turned = move(jnp.where(upper, a, c), 2 * width)
    a, c = jnp.where(upper, turned, a), jnp.where(upper, c, turned)
    turned = move(jnp.where(upper, b, d), 2 * width)
    own = jnp.where(upper, d, b)
    inner = odd != upper
    return [a, jnp.where(inner, own, turned), c, jnp.where(inner, turned, own)]


def depth_of(k, group):
    half, part = group // 2, group % 2
    plane = k + 4 * part
    return 15 - plane if half else plane


def pack_kernel(fields, out_ref, turned, staged):
    z = lax.axis_index("gz")
    lane = lane_ids()
    trade = lane < jnp.where(lax.axis_index("gy") == 0, 128, 0)
    for a in range(3):
        for xg in range(2):
            slot = turned.at[2 * a + xg]
            slot[...] = fields[a, 4 * xg : 4 * xg + 4].reshape(128, 128).T
            for k in range(4):
                tiles = [slot[pl.ds(depth_of(k, g), 8, stride=16), :] for g in range(4)]
                a1, a3 = tiles[1], tiles[3]
                tiles[1], tiles[3] = jnp.where(trade, a3, a1), jnp.where(trade, a1, a3)
                for x4, tile in enumerate(regroup(tiles, 1, 32, lane)):
                    staged[pl.ds(a * 32 + k * 8 + 2 * x4 + xg, 8, stride=96), :] = tile
    for x in range(GX):
        for y in range(GY):
            start = pl.multiple_of(chunk_of(x, y, z) * 96, 96)
            out_ref[y * GX + x] = staged[pl.ds(start, 96), :]


def pack(fields):
    return pl.pallas_call(
        pack_kernel,
        out_shape=jax.ShapeDtypeStruct((8, 96, 128), jnp.float32),
        in_specs=[pl.BlockSpec(memory_space=pltpu.VMEM)],
        out_specs=pl.BlockSpec(memory_space=pltpu.VMEM),
        scratch_shapes=[pltpu.VMEM((6, 128, 128), jnp.float32), pltpu.VMEM((768, 128), jnp.float32)],
        compiler_params=pltpu.CompilerParams(vmem_limit_bytes=4 * 2**20),
        name="pack",
    )(fields)


def shape_of(*dims):
    return jax.ShapeDtypeStruct(dims + TILE, jnp.float32)


def scratch(*dims):
    return pltpu.VMEM(dims + TILE, jnp.float32)


def halo_masks():
    x, y, z = position()
    chunk = chunk_of(x, y, z)
    half = lane_ids() // 64
    return chunk, (half + chunk % 2) == 1


PLACE = [(r, True) for r in range(6)] + [(4, False), (5, False), (3, False), (2, False), (1, False), (0, False)]
PLACE += [(6, False), (6, True)]
FIRST_TILE = (0, 6, 13)
MESSAGE = 19


def message(planes, near, count):
    tiles = [jnp.where(near, planes[t], planes[t + 4]) for t in range(4)]
    tiles += [jnp.where(near, planes[t], lanes(planes[t + 2], 64)) for t in (4, 5)]
    if count == 7:
        tiles.append(jnp.where(near, lanes(planes[2], 64), planes[3]))
    return tiles


def halo_plane(even, odd, a, r, from_even):
    tile, moved = PLACE[r]
    tile = FIRST_TILE[a] + tile
    if moved:
        return lanes(jnp.where(from_even, odd[tile], even[tile]), 64)
    return jnp.where(from_even, even[tile], odd[tile])


def slab_kernel(in_ref, out_ref, b_ref, even_ref, odd_ref):
    lane, row = lane_ids(), row_ids()
    low = (lane // 32) % 2 == 0
    _, from_even = halo_masks()
    for a in range(3):
        planes = [None] * 8
        for k in range(4):
            part = ([], [])
            for x in range(GX):
                first = in_ref[x, pl.ds(a * 32 + k * 8, 8), :]
                second = in_ref[GX + x, pl.ds(a * 32 + k * 8, 8), :]
                turned = lanes(jnp.where(low, second, first), 32)
                part[0].append(jnp.where(low, first, turned))
                part[1].append(jnp.where(low, turned, second))
            for pp in range(2):
                planes[k + 4 * pp] = jnp.stack(regroup(part[pp], 0, 2, row))
                if a == 2:
                    b_ref[k + 4 * pp] = planes[k + 4 * pp]
                else:
                    out_ref[a, k + 4 * pp] = planes[k + 4 * pp]
        count = 7 if a == 1 else 6
        for near, ref in ((from_even, even_ref), (~from_even, odd_ref)):
            for t, tile in enumerate(message(planes, near, count)):
                ref[FIRST_TILE[a] + t] = tile


def to_slab(received):
    vmem = pl.BlockSpec(memory_space=pltpu.VMEM)
    return pl.pallas_call(
        slab_kernel,
        out_shape=[shape_of(2, 8, 4), shape_of(8, 4), shape_of(MESSAGE, 4), shape_of(MESSAGE, 4)],
        in_specs=[vmem],
        out_specs=[vmem] * 4,
        compiler_params=pltpu.CompilerParams(vmem_limit_bytes=4 * 2**20),
        name="to_slab",
    )(received)


class Planes:
    def __init__(self, *segments):
        self.segments = [(first, first + ref.shape[0], ref) for first, ref in segments]

    def find(self, p, q):
        for first, last, ref in self.segments:
            low, high = max(p, first), min(q, last)
            if low < high:
                yield low, high, ref, slice(low - first, high - first)

    def get(self, p, q):
        pieces = [ref[place] for _, _, ref, place in self.find(p, q)]
        return pieces[0] if len(pieces) == 1 else jnp.concatenate(pieces, axis=0)

    def put(self, p, value):
        for low, high, ref, place in self.find(p, p + value.shape[0]):
            ref[place] = value[low - p : high - p]


def spans(first, last, size):
    return [(p, min(p + size, last)) for p in range(first, last, size)]


def x_up(value):
    return jnp.concatenate([value[:, 1:], rows(value[:, :1], -1)], axis=1)


def x_down(value):
    return jnp.concatenate([rows(value[:, -1:], 1), value[:, :-1]], axis=1)


def couple(v, p, q, cx, cy, cz, dup):
    here, by_x, by_y = v.get(p, q), cx.get(p, q), cy.get(p, q)
    total = by_x * x_up(here) + x_down(by_x * here)
    total = total + (by_y * lanes(here, -dup) + lanes(by_y * here, dup))
    return total + (cz.get(p, q) * v.get(p - 1, q - 1) + cz.get(p + 1, q + 1) * v.get(p + 1, q + 1))


def chebyshev_factors(count, lower):
    center = (UPPER_EIG + lower) / 2.0
    half_width = (UPPER_EIG - lower) / 2.0
    ratio = center / half_width
    old = 1.0 / ratio
    out = [(0.0, 1.0 / center)]
    for _ in range(count - 1):
        new = 1.0 / (2.0 * ratio - old)
        out.append((new * old, 2.0 * new / half_width))
        old = new
    return out


def sweep(new, now, before, factor, b, dinv, coeffs, p, q, dup, size):
    carry, gain = factor
    for p, q in spans(p, q, size):
        base = (1.0 + carry - gain) * now.get(p, q)
        if carry != 0.0 and before is not None:
            base = base - carry * before.get(p, q)
        new.put(p, (b.get(p, q) + couple(now, p, q, *coeffs, dup)) * (gain * dinv.get(p, q)) + base)


def close(v, last):
    v.put(last, lanes(v.get(last - 1, last), 64))


def smooth(pair, b, dinv, coeffs, factors, first, last, dup, size):
    before, now, spare = pair
    for number, factor in enumerate(factors):
        new = spare if before is None else before
        sweep(new, now, before, factor, b, dinv, coeffs, first + number, last, dup, size)
        close(new, last)
        before, now = now, new
    return now


def inverse(value):
    guess = pl.reciprocal(value, approx=True)
    return guess * (2.0 - value * guess)


def level_coefficients(beta, alpha, first, last, shift, dup, cx, cy, cz, dinv, diag, ends, seam, size):
    lane, row = lane_ids(), row_ids()
    y_last = (lane % 64) // dup == 64 // dup - 1
    y_first = (lane % 64) // dup == 0
    x_rim = jnp.where(row == 0, 0.5, 0.0), jnp.where(row == 7, 0.5, 0.0)
    for p, q in spans(first, last, size):
        here = beta.get(p, q)
        by_x = 0.5 * (here + x_up(here))
        by_x = jnp.concatenate([by_x[:, :-1], jnp.where(row == 7, 0.0, by_x[:, -1:])], axis=1)
        above = jnp.where(y_last, 0.0, lanes(here, -dup))
        below = jnp.where(y_first, 0.0, lanes(here, dup))
        by_y = jnp.where(y_last, 0.0, 0.5 * (here + above))
        face = 0.5 * (beta.get(p - 1, q - 1) + here)
        total = shift * alpha.get(p, q) + (by_x + x_down(by_x)) + (here + 0.5 * (above + below))
        total = total + (face + 0.5 * (here + beta.get(p + 1, q + 1)))
        groups = [total[:, i : i + 1] for i in range(total.shape[1])]
        groups[0] = groups[0] + here[:, :1] * x_rim[0]
        groups[-1] = groups[-1] + here[:, -1:] * x_rim[1]
        total = jnp.concatenate(groups, axis=1)
        cx.put(p, by_x)
        cy.put(p, by_y)
        cz.put(p, face)
        diag.put(p, total)
        dinv.put(p, inverse(jnp.where(total > 0.0, total, 1.0)))
    if first <= seam < last:
        cz.put(seam, cz.get(seam, seam + 1) * ends)
    else:
        cz.put(last, 0.5 * (beta.get(last - 1, last) + beta.get(last, last + 1)))


def restrict_pair(first, second, dup):
    lane = lane_ids()
    total = first + second
    total = jnp.concatenate([total[:, i : i + 1] + total[:, i + 1 : i + 2] for i in range(0, total.shape[1], 2)], axis=1)
    return total + jnp.where((lane // dup) % 2 == 0, lanes(total, -dup), lanes(total, dup))


def restrict(take, p, q, dup):
    fine = take(2 * p, 2 * q)
    fine = fine.reshape((q - p, 2) + fine.shape[1:])
    return restrict_pair(fine[:, 0], fine[:, 1], dup)


def ends_factor():
    x, y, z = position()
    slab = 8 * z + chunk_of(x, y, z)
    half = lane_ids() // 64
    end = ((half == 0) & (slab == 0)) | ((half == 1) & (slab == 8 * GZ - 1))
    return jnp.where(end, 0.0, 1.0)


def call(kernel, name, operands, out_shape, scratch_shapes):
    vmem = pl.BlockSpec(memory_space=pltpu.VMEM)
    return pl.pallas_call(
        kernel,
        out_shape=out_shape,
        in_specs=[vmem] * len(operands),
        out_specs=[vmem] * len(out_shape),
        scratch_shapes=scratch_shapes,
        compiler_params=pltpu.CompilerParams(vmem_limit_bytes=16 * 2**20),
        name=name,
    )(*operands)


PRE_SHAPES = [(7, 4), (7, 4), (8, 4), (7, 4), (7, 4), (3, 2), (3, 2), (4, 2), (3, 2), (3, 2)]
MID_SHAPES = [(5, 4), (5, 4), (5, 4), (5, 4), (1, 4), (7, 2), (7, 2), (7, 2), (7, 2)]
LOW_SHAPES = [(8, 4), (8, 4), (8, 4), (8, 4), (12, 4), (7, 2)]


def coefficient_planes(pre, mid, low):
    zero, one = [], []
    for i in range(5):
        parts = [(4, low[i])] if low else []
        parts += [(16 if i == 4 else 12, mid[i])] if mid else []
        zero.append(Planes(*parts, *([(17, pre[i])] if pre else [])))
        parts = []
        if mid and i < 4:
            parts = [(2, mid[5 + i])]
        elif low and i == 4:
            parts = [(2, low[5])]
        one.append(Planes(*parts, *([(9, pre[5 + i])] if pre and len(pre) > 5 + i else [])))
    return zero, one


def pre_kernel(own, own_b, *refs):
    pre, (alpha1, beta1, v1, v2, v3, v4), (ghost, ghost1) = refs[:10], refs[10:16], refs[16:]
    zero, one = coefficient_planes(pre, None, None)
    alpha, beta = Planes((16, own.at[0])), Planes((16, own.at[1]), (24, ghost))
    alpha_one, beta_one = Planes((8, alpha1)), Planes((8, beta1), (12, ghost1))
    close(beta, PLANES)
    level_coefficients(beta, alpha, 17, PLANES, SHIFT_BASE, 1, *zero, None, 16, COEF_SPAN)
    beta_one.put(8, 0.125 * restrict(beta.get, 8, PLANES1, 1))
    alpha_one.put(8, 0.125 * restrict(alpha.get, 8, PLANES1, 1))
    close(beta_one, PLANES1)
    level_coefficients(beta_one, alpha_one, 9, PLANES1, SHIFT_BASE * 4.0, 2, *one, None, 8, COEF_SPAN1)
    b, coeffs, dinv = Planes((16, own_b)), zero[:3], zero[3]
    factors = chebyshev_factors(SWEEPS, SMOOTH_LOWER)
    iterates = [None, Planes((17, v1)), Planes((18, v2)), Planes((19, v3)), Planes((20, v4))]
    for p, q in spans(17, PLANES, 4):
        iterates[1].put(p, factors[0][1] * (b.get(p, q) * dinv.get(p, q)))
    close(iterates[1], PLANES)
    for i in range(2, 5):
        sweep(iterates[i], iterates[i - 1], iterates[i - 2], factors[i - 1], b, dinv, coeffs, 16 + i, PLANES, 1, SPAN)
        close(iterates[i], PLANES)


def mid_part(own, even, odd, beta1_own, alpha1_own, mid, low, beta_s, alpha_s, beta1_s, alpha1_s):
    _, from_even = halo_masks()
    zero, one = coefficient_planes(None, mid, low)
    for p in range(2, 16):
        beta_s[p] = halo_plane(even, odd, 1, 15 - p, from_even)
        if p >= 4:
            alpha_s[p] = halo_plane(even, odd, 0, 15 - p, from_even)
    beta, alpha = Planes((0, beta_s), (16, own.at[1])), Planes((0, alpha_s), (16, own.at[0]))
    ends = ends_factor()
    level_coefficients(beta, alpha, 4, 17, SHIFT_BASE, 1, *zero, ends, 16, COEF_SPAN)
    beta_one, alpha_one = Planes((0, beta1_s), (8, beta1_own)), Planes((0, alpha1_s), (8, alpha1_own))
    for p in range(1, 8):
        beta_one.put(p, 0.125 * restrict(beta.get, p, p + 1, 1))
        if p >= 2:
            alpha_one.put(p, 0.125 * restrict(alpha.get, p, p + 1, 1))
    level_coefficients(beta_one, alpha_one, 2, 9, SHIFT_BASE * 4.0, 2, *one, ends, 8, COEF_SPAN1)


def post_kernel(own, own_b, odd, even, *refs):
    pre, (alpha1, beta1, v1, v2, v3, v4), (gather, rim, halo_b, late, u1, b1) = refs[:10], refs[10:16], refs[16:22]
    mid, low, (f1, f2, f3, f4, low_b, b1_s, w_a, w_b), scratch_mid = refs[22:31], refs[31:37], refs[37:45], refs[45:]
    mid_part(own, even, odd, beta1, alpha1, mid, low, *scratch_mid)
    lane = lane_ids()
    _, from_even = halo_masks()
    zero, one = coefficient_planes(pre, mid, low)
    coeffs, dinv, diag = zero[:3], zero[3], zero[4]
    b = Planes((4, low_b), (12, halo_b), (16, own_b))
    for p in range(4, 16):
        b.put(p, halo_plane(even, odd, 2, 15 - p, from_even)[None])
    factors = chebyshev_factors(SWEEPS, SMOOTH_LOWER)
    iterates = [
        None,
        Planes((4, f1), (17, v1)),
        Planes((5, f2), (18, v2)),
        Planes((6, f3), (19, v3)),
        Planes((7, f4), (16, late), (20, v4)),
    ]
    for p, q in spans(4, 17, 4):
        iterates[1].put(p, factors[0][1] * (b.get(p, q) * dinv.get(p, q)))
    for i in range(2, 5):
        sweep(iterates[i], iterates[i - 1], iterates[i - 2], factors[i - 1], b, dinv, coeffs, 3 + i, 16 + i, 1, SPAN)
    v = iterates[4]
    rim[0:20] = v.get(16, 21).reshape((20,) + TILE)

    def residual(v, b, diag, coeffs, dup):
        return lambda p, q: (b.get(p, q) + couple(v, p, q, *coeffs, dup)) - diag.get(p, q) * v.get(p, q)

    b_one = Planes((4, b1_s), (8, b1))
    for p in range(4, PLANES1):
        b_one.put(p, 0.5 * restrict(residual(v, b, diag, coeffs, 1), p, p + 1, 1))
    coeffs, dinv, diag = one[:3], one[3], one[4]
    w, spare = Planes((0, w_a)), Planes((0, w_b))
    w.put(4, factors[0][1] * (b_one.get(4, PLANES1) * dinv.get(4, PLANES1)))
    close(w, PLANES1)
    w = smooth((None, w, spare), b_one, dinv, coeffs, factors[1:], 5, PLANES1, 2, SPAN1)
    b_two = 0.5 * restrict(residual(w, b_one, diag, coeffs, 2), 4, 6, 2)
    beta_two = 0.125 * restrict(Planes((8, beta1)).get, 4, 6, 2)
    alpha_two = 0.125 * restrict(Planes((8, alpha1)).get, 4, 6, 2)
    slot = lane % 4
    both = jnp.where(slot < 2, *(jnp.where(slot % 2 == 0, field[0, 0], field[1, 0]) for field in (b_two, beta_two)))
    last = jnp.where(slot % 2 == 0, alpha_two[0, 0], alpha_two[1, 0])
    last = jnp.where(slot[:4] < 2, last[:4], last[4:])
    for n in range(COUNT):
        for i, part in enumerate((both[:4], both[4:], last)):
            gather[n, i] = part
    u1[...] = w.get(8, PLANES1)
    rim[20:28] = jnp.where(lane % 2 == 0, w.get(8, PLANES1), b_one.get(8, PLANES1)).reshape((8,) + TILE)


def down_pre(own, own_b):
    shapes = PRE_SHAPES + [(4, 2), (4, 2), (8, 4), (7, 4), (6, 4), (5, 4)]
    return call(pre_kernel, "down_pre", (own, own_b), [shape_of(*n) for n in shapes], [scratch(1, 4), scratch(1, 2)])


def down_post(own, own_b, even, odd, pre):
    shapes = [shape_of(*n) for n in [(RIM,), (4, 4), (4, 4), (4, 2), (4, 2), *MID_SHAPES]]
    spare = [(13, 4), (13, 4), (13, 4), (9, 4), (8, 4), (4, 2), (13, 2), (13, 2), (16, 4), (16, 4), (8, 2), (8, 2)]
    return call(
        post_kernel, "down_post", (own, own_b, odd, even, *pre),
        [jax.ShapeDtypeStruct((COUNT, 3, 4, 128), jnp.float32), *shapes], [scratch(*n) for n in LOW_SHAPES + spare],
    )


def outer(value, half):
    turned = lanes(value, 64)
    before = jnp.concatenate([lanes(value[-1:], 65), turned[:-1]], axis=0)
    after = jnp.concatenate([turned[1:], lanes(value[:1], 63)], axis=0)
    return jnp.where(half == 0, before, after), turned


def coarse_kernel(gathered, out, tiles_s, e2_s):
    lane, row = lane_ids(), row_ids()
    half = lane // 64
    x, y, z = position()
    for n in range(COUNT):
        tiles_s[n, 0] = jnp.concatenate([gathered[n, 0], gathered[n, 1]], axis=0)
        tiles_s[n, 1] = jnp.concatenate([gathered[n, 2], lanes(gathered[n, 2], -2)], axis=0)

    def collect(tile, slot):
        out = []
        for group in range(8):
            joined = None
            for q in range(GZ):
                natural = 7 - group if q % 2 else group
                rank, core = natural // 2, natural % 2
                n = ((rank ^ (rank >> 1)) * GZ + q) * GY + core
                piece = tiles_s[n, tile] if q == slot else lanes(tiles_s[n, tile], q - slot)
                joined = piece if joined is None else jnp.where(lane % 4 == q, piece, joined)
            out.append(joined)
        return jnp.stack(out)

    b_two, beta_two, alpha_two = ([collect(tile, slot + p) for p in range(2)] for tile, slot in ((0, 0), (0, 2), (1, 0)))
    slab = lax.broadcasted_iota(jnp.int32, (8,) + TILE, 0)
    end = ((slab == 0) & (lane % 4 == 0) & (half == 0)) | ((slab == 7) & (lane % 4 == 3) & (half == 1))

    def sides(beta, dx, dy):
        place = (lane % 64) // dy
        rims = row >= 8 - dx, row < dx, place == 64 // dy - 1, place == 0
        others = rows(beta, -dx), rows(beta, dx), lanes(beta, -dy), lanes(beta, dy)
        faces = [jnp.where(rim, 0.0, 0.5 * (beta + other)) for rim, other in zip(rims, others)]
        edge = jnp.where(rims[0] | rims[1], 0.5, 0.0) + jnp.where(rims[2] | rims[3], 0.5, 0.0)
        return faces, (faces[0] + faces[1]) + (faces[2] + faces[3]) + beta * edge

    def scaled(faces, inv):
        return [face * inv for face in faces]

    def flat(v, coeffs, dx, dy):
        x_above, x_below, y_above, y_below = coeffs
        total = x_above * rows(v, -dx) + x_below * rows(v, dx)
        return total + (y_above * lanes(v, -dy) + y_below * lanes(v, dy))

    faces_a, sum_a = sides(beta_two[0], 1, 4)
    faces_b, sum_b = sides(beta_two[1], 1, 4)
    middle = 0.5 * (beta_two[0] + beta_two[1])
    inner = 0.5 * (beta_two[1] + lanes(beta_two[1], 64))
    edge = 0.5 * (beta_two[0] + jnp.where(end, 0.0, outer(beta_two[0], half)[0]))
    shift = SHIFT_BASE * 16.0
    diag_a = shift * alpha_two[0] + sum_a + (middle + edge)
    diag_b = shift * alpha_two[1] + sum_b + (middle + inner)
    inv_a, inv_b = inverse(diag_a), inverse(diag_b)
    flat_a, flat_b = scaled(faces_a, inv_a), scaled(faces_b, inv_b)
    middle_a, middle_b = middle * inv_a, middle * inv_b
    rim_a, inner_b = jnp.where(end, 0.0, edge) * inv_a, inner * inv_b
    rhs_a, rhs_b = b_two[0] * inv_a, b_two[1] * inv_b

    def apply_two(va, vb):
        ta = flat(va, flat_a, 1, 4) + (middle_a * vb + rim_a * outer(va, half)[0])
        tb = flat(vb, flat_b, 1, 4) + (middle_b * va + inner_b * lanes(vb, 64))
        return ta, tb

    def sweeps_two(before, now, factors):
        for carry, gain in factors:
            totals = apply_two(*now)
            new = []
            for v, old, rhs, total in zip(now, before or (None, None), (rhs_a, rhs_b), totals):
                base = (1.0 + carry - gain) * v + gain * rhs
                if carry != 0.0 and old is not None:
                    base = base - carry * old
                new.append(base + gain * total)
            before, now = now, new
        return now

    factors = chebyshev_factors(SWEEPS, SMOOTH_LOWER)
    ua, ub = sweeps_two(None, (factors[0][1] * rhs_a, factors[0][1] * rhs_b), factors[1:])
    ta, tb = apply_two(ua, ub)

    def restrict_whole(first, second):
        total = first + second
        total = total + jnp.where(row % 2 == 0, rows(total, -1), rows(total, 1))
        return total + jnp.where((lane // 4) % 2 == 0, lanes(total, -4), lanes(total, 4))

    second = (lane // 4) % 2 == 1

    def pack_low(value):
        return jnp.where(second, value[4:], value[:4])

    def outer_low(value):
        turned = lanes(value, 64)
        first_one, last_one = value[:1], value[-1:]
        before = jnp.where(second, lanes(last_one, 68), lanes(last_one, 61))
        after = jnp.where(second, lanes(first_one, 67), lanes(first_one, 60))
        before = jnp.concatenate([before, turned[:-1]], axis=0)
        after = jnp.concatenate([turned[1:], after], axis=0)
        return jnp.where(half == 0, before, after), turned

    b_low = 0.5 * pack_low(restrict_whole(diag_a * (rhs_a + ta - ua), diag_b * (rhs_b + tb - ub)))
    beta_low = 0.125 * pack_low(restrict_whole(beta_two[0], beta_two[1]))
    alpha_low = 0.125 * pack_low(restrict_whole(alpha_two[0], alpha_two[1]))
    slab = lax.broadcasted_iota(jnp.int32, (4,) + TILE, 0) + jnp.where(second, 4, 0)
    end_low = ((slab == 0) & (lane % 4 == 0) & (half == 0)) | ((slab == 7) & (lane % 4 == 3) & (half == 1))
    faces_low, sum_low = sides(beta_low, 2, 8)
    beyond, turned = outer_low(beta_low)
    inner_low = 0.5 * (beta_low + turned)
    edge_low = 0.5 * (beta_low + jnp.where(end_low, 0.0, beyond))
    inv_low = inverse(SHIFT_BASE * 64.0 * alpha_low + sum_low + (inner_low + edge_low))
    flat_low = scaled(faces_low, inv_low)
    rim_low = jnp.where(end_low, 0.0, edge_low) * inv_low
    inner_low = inner_low * inv_low
    rhs_low = b_low * inv_low
    before = v = None
    for carry, gain in chebyshev_factors(BOTTOM, BOTTOM_LOWER):
        if v is None:
            v = gain * rhs_low
            continue
        beyond, turned = outer_low(v)
        base = (1.0 + carry - gain) * v + gain * rhs_low
        if before is not None:
            base = base - carry * before
        total = flat(v, flat_low, 2, 8) + (inner_low * turned + rim_low * beyond)
        before, v = v, base + gain * total
    v = jnp.concatenate([jnp.where(second, lanes(v, 4), v), jnp.where(second, v, lanes(v, -4))], axis=0)
    va, vb = sweeps_two(None, (ua + v, ub + v), factors)
    for group in range(8):
        e2_s[group, 0] = va[group]
        e2_s[group, 1] = vb[group]

    chunk = chunk_of(x, y, z)
    place = 8 * z + chunk

    def fetch(offset, p, turn=0):
        index = jnp.clip(place + offset, 0, COUNT - 1)
        tile, out = e2_s[index % 8, p], None
        for slot in range(4):
            piece = pltpu.roll(tile, (128 + slot + turn - index // 8) % 128, 1)
            out = piece if out is None else jnp.where(lane % 4 == slot, piece, out)
        return out

    first = half == 0
    out[0] = jnp.where(first, fetch(-1, 0), fetch(1, 0))
    out[1] = jnp.where(first, fetch(-1, 1), fetch(1, 1))
    out[2] = jnp.where(first, fetch(-1, 1, 64), fetch(1, 1, 64))
    out[3] = jnp.where(first, fetch(-1, 0, 64), fetch(1, 0, 64))
    out[4] = fetch(0, 0)
    out[5] = fetch(0, 1)


def coarse(gathered):
    vmem = pl.BlockSpec(memory_space=pltpu.VMEM)
    return pl.pallas_call(
        coarse_kernel,
        out_shape=shape_of(6),
        in_specs=[vmem],
        out_specs=vmem,
        scratch_shapes=[scratch(COUNT, 2), scratch(8, 2)],
        compiler_params=pltpu.CompilerParams(vmem_limit_bytes=8 * 2**20),
        name="coarse",
    )(gathered)


def up_kernel(e_two, rim_even, rim_odd, own_b, halo_b, late, u1, b1, v4, *refs):
    pre, mid, (out, v_a, v_b, w_a, w_b, bx_s) = refs[:9], refs[9:18], refs[18:]
    zero, one = coefficient_planes(pre, mid, None)
    lane, row = lane_ids(), row_ids()
    _, from_even = halo_masks()
    factors = chebyshev_factors(SWEEPS, SMOOTH_LOWER)

    for p in range(1, 8):
        if p >= 4:
            k = 7 - p
            both = lanes(jnp.where(from_even, rim_odd[20 + 2 * k : 22 + 2 * k], rim_even[20 + 2 * k : 22 + 2 * k]), 64)
        else:
            both = jnp.where(from_even, rim_even[20 + 2 * p : 22 + 2 * p], rim_odd[20 + 2 * p : 22 + 2 * p])
        w_a[p] = jnp.where(lane % 2 == 0, both, lanes(both, 1)) + e_two[p // 2]
        if p >= 2:
            bx_s[p] = jnp.where(lane % 2 == 0, lanes(both, -1), both)
    for p in range(8, PLANES1):
        w_a[p] = u1[p - 8] + e_two[p // 2]
    w_a[PLANES1] = lanes(w_a[PLANES1 - 1], 64)
    pair = (Planes((0, w_b)), Planes((0, w_a)), None)
    w = smooth(pair, Planes((0, bx_s), (8, b1)), one[3], one[:3], factors, 2, PLANES1, 2, SPAN1)

    for p in range(11, PLANES):
        if p >= 16:
            start = Planes((16, late), (20, v4)).get(p, p + 1)[0]
        else:
            k = 4 * (15 - p)
            start = lanes(jnp.where(from_even, rim_odd[k : k + 4], rim_even[k : k + 4]), 64)
        e_one = w.get(p // 2, p // 2 + 1)[0]
        e_one = jnp.concatenate([e_one[:1], e_one[:1], e_one[1:], e_one[1:]], axis=0)
        v_a[p] = start + e_one
    v_a[PLANES] = lanes(v_a[PLANES - 1], 64)
    b, diag, coeffs = Planes((12, halo_b), (16, own_b)), zero[4], zero[:3]
    v = smooth((Planes((0, v_b)), Planes((0, v_a)), None), b, zero[3], coeffs, factors, 12, PLANES, 1, SPAN)
    low = (lane // 32) % 2 == 0
    for k in range(4):
        for o in range(2):
            parts = []
            for pp in range(2):
                p = 16 + k + 4 * pp
                value = v.get(p, p + 1)
                if o == 1:
                    value = (b.get(p, p + 1) + couple(v, p, p + 1, *coeffs, 1)) - diag.get(p, p + 1) * value
                parts.append(regroup([value[0, i] for i in range(4)], 0, 2, row))
            for i in range(GX):
                one, two = parts[0][i], parts[1][i]
                turned = lanes(jnp.where(low, two, one), 32)
                out[i, pl.ds(o * 32 + k * 8, 8), :] = jnp.where(low, one, turned)
                out[GX + i, pl.ds(o * 32 + k * 8, 8), :] = jnp.where(low, turned, two)


def up(*operands):
    return call(
        up_kernel, "up_strokes", operands, [jax.ShapeDtypeStruct((8, 64, 128), jnp.float32)],
        [scratch(25, 4), scratch(25, 4), scratch(13, 2), scratch(13, 2), scratch(8, 2)],
    )[0]


def unpack_kernel(in_ref, v_ref, r_ref, fields, turned, staged, left):
    z = lax.axis_index("gz")
    lane = lane_ids()
    trade = lane < jnp.where(lax.axis_index("gy") == 1, 128, 0)
    for x in range(GX):
        for y in range(GY):
            start = pl.multiple_of(chunk_of(x, y, z) * 64, 64)
            staged[pl.ds(start, 64), :] = in_ref[y * GX + x]
    copies = [pltpu.make_async_copy(fields.at[o], ref, left.at[o]) for o, ref in enumerate((v_ref, r_ref))]
    for o, copy in enumerate(copies):
        for xg in range(2):
            slot = turned.at[2 * o + xg]
            for k in range(4):
                tiles = [staged[pl.ds(o * 32 + k * 8 + 2 * x4 + xg, 8, stride=64), :] for x4 in range(4)]
                tiles = regroup(tiles, 1, 32, lane)
                a0, a2 = tiles[0], tiles[2]
                tiles[0], tiles[2] = jnp.where(trade, a2, a0), jnp.where(trade, a0, a2)
                for g, tile in enumerate(tiles):
                    slot[pl.ds(depth_of(k, g), 8, stride=16), :] = tile
            fields[o, 4 * xg : 4 * xg + 4] = slot[...].T.reshape(4, 32, 128)
        copy.start()
    for copy in copies:
        copy.wait()


def unpack(received):
    vmem = pl.BlockSpec(memory_space=pltpu.VMEM)
    return pl.pallas_call(
        unpack_kernel,
        out_shape=[jax.ShapeDtypeStruct(BLOCK, jnp.float32)] * 2,
        in_specs=[vmem],
        out_specs=[pl.BlockSpec(memory_space=pltpu.HBM)] * 2,
        scratch_shapes=[
            pltpu.VMEM((2,) + BLOCK, jnp.float32),
            pltpu.VMEM((4, 128, 128), jnp.float32),
            pltpu.VMEM((512, 128), jnp.float32),
            pltpu.SemaphoreType.DMA((2,)),
        ],
        compiler_params=pltpu.CompilerParams(vmem_limit_bytes=4 * 2**20),
        name="unpack",
    )(received)


def slab_shards(right_side, alpha_coef, beta_coef):
    even_pairs, odd_pairs = swap_pairs(False), swap_pairs(True)
    packed = pack(jnp.stack([alpha_coef, beta_coef, right_side]))
    own, own_b, to_even, to_odd = to_slab(lax.all_to_all(packed, RING, 0, 0))
    even = lax.ppermute(to_even, ALL, even_pairs)
    odd = lax.ppermute(to_odd, ALL, odd_pairs)
    found = down_pre(own, own_b)
    pre, v4 = found[:9], found[15]
    gather, rim, halo_b, late, u1, b1, *mid = down_post(own, own_b, even, odd, found)
    rim_even = lax.ppermute(rim, ALL, even_pairs)
    rim_odd = lax.ppermute(rim, ALL, odd_pairs)
    kept = (own_b, halo_b, late, u1, b1, v4, *pre, *mid)
    result = up(coarse(lax.all_to_all(gather, ("gx", "gz", "gy"), 0, 0)), rim_even, rim_odd, *kept)
    return tuple(unpack(lax.all_to_all(result, RING, 0, 0)))


def solution(mesh):
    spec = P("gx", "gy", "gz")
    plain = jax.shard_map(shards, mesh=mesh, in_specs=(spec,) * 3, out_specs=(spec,) * 2, check_vma=False)
    slabs = jax.shard_map(slab_shards, mesh=mesh, in_specs=(spec,) * 3, out_specs=(spec,) * 2, check_vma=False)
    sizes = tuple(mesh.shape[axis] for axis in ALL)

    def run(right_side, alpha_coef, beta_coef):
        block = tuple(n // size for n, size in zip(right_side.shape, sizes))
        fits = sizes == (GX, GY, GZ) and block == BLOCK
        return (slabs if fits else plain)(right_side, alpha_coef, beta_coef)

    return run
```

```python
import jax
import jax.numpy as jnp
from jax import lax
from jax.experimental import pallas as pl
from jax.experimental.pallas import tpu as pltpu
from jax.sharding import PartitionSpec as P

LEVELS = 3
SWEEPS = 4
BOTTOM = 12


SHIFT_BASE = 0.01
UPPER_EIG = 2.0
SMOOTH_LOWER = 0.25
BOTTOM_LOWER = 0.02


def with_halo(block, sides, width):
    for axis, dim in sides:
        count = lax.axis_size(axis)
        forward = [(i, i + 1) for i in range(count - 1)]
        backward = [(target, source) for source, target in forward]
        low = lax.ppermute(
            lax.slice_in_dim(block, block.shape[dim] - width, None, axis=dim), axis, forward
        )
        high = lax.ppermute(lax.slice_in_dim(block, 0, width, axis=dim), axis, backward)
        block = jnp.concatenate([low, block, high], axis=dim)
    return block


def partner_2(array, axis, distance):
    return lax.ppermute(array, axis, [(i, i ^ 1 << distance) for i in range(lax.axis_size(axis))])


def split_padded(padded):
    return (
        padded[:-2, 1:-1, 1:-1],
        padded[2:, 1:-1, 1:-1],
        padded[1:-1, :-2, 1:-1],
        padded[1:-1, 2:, 1:-1],
        padded[1:-1, 1:-1, :-2],
        padded[1:-1, 1:-1, 2:],
    )


def zero_pad(field):
    return jnp.pad(field, 1)


def rim_iterate(field):
    return with_halo(field, (("gx", 0), ("gy", 1), ("gz", 2)), 1)


def rim_coefficient(field):
    return with_halo(field, (("gx", 0), ("gy", 1), ("gz", 2)), 1)


def level_operator(beta_level, alpha_level, padded_beta, shift):
    coeffs = tuple((0.5 * (beta_level + other) for other in split_padded(padded_beta)))
    diagonal = shift * alpha_level
    for coeff in coeffs:
        diagonal = diagonal + coeff
    return (coeffs, diagonal)


def apply_operator(field, operator, pad_field):
    coeffs, diagonal = operator
    others = split_padded(pad_field(field))
    total = coeffs[0] * others[0]
    for index in range(1, 6):
        total = total + coeffs[index] * others[index]
    return diagonal * field - total


def chebyshev(iterate, rhs_level, operator, count, lower, zero_start, pad_field):
    diagonal = operator[1]
    center = (UPPER_EIG + lower) / 2.0
    half_width = (UPPER_EIG - lower) / 2.0
    sigma_ratio = center / half_width
    rho_old = 1.0 / sigma_ratio
    if zero_start:
        remain = rhs_level
    else:
        remain = rhs_level - apply_operator(iterate, operator, pad_field)
    update = remain / diagonal / center
    iterate = iterate + update
    for sweep_index in range(count - 1):
        remain = rhs_level - apply_operator(iterate, operator, pad_field)
        rho_new = 1.0 / (2.0 * sigma_ratio - rho_old)
        update = rho_new * rho_old * update + 2.0 * rho_new / half_width * (remain / diagonal)
        iterate = iterate + update
        rho_old = rho_new
    return iterate


def restrict_mean(field):
    first, second, third = field.shape
    blocks = field.reshape(first // 2, 2, second // 2, 2, third // 2, 2)
    return jnp.sum(blocks, axis=(1, 3, 5)) * 0.125


def prolong_copy(field):
    return jnp.repeat(jnp.repeat(jnp.repeat(field, 2, axis=0), 2, axis=1), 2, axis=2)


def join_partner(packed, partner, device_index, bit_index, dim):
    position = device_index // 2**bit_index % 2
    lower_first = jnp.concatenate([packed, partner], axis=dim)
    upper_first = jnp.concatenate([partner, packed], axis=dim)
    return jnp.where(position == 0, lower_first, upper_first)


def shards(right_side, alpha_coef, beta_coef):
    betas = [beta_coef]
    alphas = [alpha_coef]
    for level in range(LEVELS):
        betas.append(restrict_mean(betas[-1]))
        alphas.append(restrict_mean(alphas[-1]))
    operators = []
    for level in range(LEVELS):
        padded_beta = rim_coefficient(betas[level])
        operators.append(
            level_operator(betas[level], alphas[level], padded_beta, SHIFT_BASE * 4.0**level)
        )
    rhs_levels = [right_side]
    smoothed = []
    for level in range(LEVELS):
        iterate = chebyshev(
            jnp.zeros_like(rhs_levels[level]),
            rhs_levels[level],
            operators[level],
            SWEEPS,
            SMOOTH_LOWER,
            True,
            rim_iterate,
        )
        remain = rhs_levels[level] - apply_operator(iterate, operators[level], rim_iterate)
        smoothed.append(iterate)
        rhs_levels.append(4.0 * restrict_mean(remain))
    coarse_rhs = rhs_levels[LEVELS]
    local_shape = coarse_rhs.shape
    packed = jnp.stack([coarse_rhs, betas[LEVELS], alphas[LEVELS]])
    index_x = lax.axis_index("gx")
    index_y = lax.axis_index("gy")
    index_z = lax.axis_index("gz")
    for bit_index in range(lax.axis_size("gx").bit_length() - 1):
        partner = partner_2(packed, "gx", bit_index)
        packed = join_partner(packed, partner, index_x, bit_index, 1)
    for bit_index in range(lax.axis_size("gy").bit_length() - 1):
        partner = partner_2(packed, "gy", bit_index)
        packed = join_partner(packed, partner, index_y, bit_index, 2)
    for bit_index in range(lax.axis_size("gz").bit_length() - 1):
        partner = partner_2(packed, "gz", bit_index)
        packed = join_partner(packed, partner, index_z, bit_index, 3)
    whole_rhs = packed[0]
    whole_beta = packed[1]
    whole_alpha = packed[2]
    bottom_operator = level_operator(
        whole_beta, whole_alpha, zero_pad(whole_beta), SHIFT_BASE * 4.0**LEVELS
    )
    whole_correction = chebyshev(
        jnp.zeros_like(whole_rhs), whole_rhs, bottom_operator, BOTTOM, BOTTOM_LOWER, True, zero_pad
    )
    starts = (index_x * local_shape[0], index_y * local_shape[1], index_z * local_shape[2])
    correction = lax.dynamic_slice(whole_correction, starts, local_shape)
    for level in range(LEVELS - 1, -1, -1):
        start_field = smoothed[level] + prolong_copy(correction)
        correction = chebyshev(
            start_field,
            rhs_levels[level],
            operators[level],
            SWEEPS,
            SMOOTH_LOWER,
            False,
            rim_iterate,
        )
    residual_field = right_side - apply_operator(correction, operators[0], rim_iterate)
    return (correction, residual_field)


GX, GY, GZ = 4, 2, 4
COUNT = GX * GY * GZ
RIM = 28
BLOCK = (8, 32, 128)
RING = ("gy", "gx")
ALL = ("gx", "gy", "gz")
TILE = (8, 128)
PLANES = 24
PLANES1 = 12
SPAN, SPAN1, COEF_SPAN, COEF_SPAN1 = 2, 4, 2, 4


def chunk_of(x, y, z):
    natural = 2 * (x ^ (x >> 1)) + y
    return natural + (z % 2) * (7 - 2 * natural)


def position():
    return lax.axis_index("gx"), lax.axis_index("gy"), lax.axis_index("gz")


def swap_pairs(odd):
    place = {}
    for x in range(GX):
        for y in range(GY):
            for z in range(GZ):
                place[8 * z + chunk_of(x, y, z)] = (x * GY + y) * GZ + z
    count = len(place)
    if odd:
        pairs = [(i, i + 1) for i in range(1, count - 1, 2)]
    else:
        pairs = [(i, i + 1) for i in range(0, count, 2)]
    return [(place[a], place[b]) for a, b in pairs] + [(place[b], place[a]) for a, b in pairs]


def lane_ids():
    return lax.broadcasted_iota(jnp.int32, TILE, 1)


def row_ids():
    return lax.broadcasted_iota(jnp.int32, TILE, 0)


def lanes(value, shift):
    return pltpu.roll(value, shift % 128, value.ndim - 1)


def rows(value, shift):
    return pltpu.roll(value, shift % 8, value.ndim - 2)


def regroup(tiles, axis, width, ids):
    move = lanes if axis == 1 else rows
    group = ids // width % 4
    odd, upper = group % 2 == 1, group >= 2
    a, b, c, d = tiles
    turned = move(jnp.where(odd, a, b), width)
    a, b = jnp.where(odd, turned, a), jnp.where(odd, b, turned)
    turned = move(jnp.where(odd, c, d), width)
    c, d = jnp.where(odd, turned, c), jnp.where(odd, d, turned)
    turned = move(jnp.where(upper, a, c), 2 * width)
    a, c = jnp.where(upper, turned, a), jnp.where(upper, c, turned)
    turned = move(jnp.where(upper, b, d), 2 * width)
    own = jnp.where(upper, d, b)
    inner = odd != upper
    return [a, jnp.where(inner, own, turned), c, jnp.where(inner, turned, own)]


def depth_of(k, group):
    half, part = group // 2, group % 2
    plane = k + 4 * part
    return 15 - plane if half else plane


def pack_kernel(fields, out_ref, turned, staged):
    z = lax.axis_index("gz")
    lane = lane_ids()
    trade = lane < jnp.where(lax.axis_index("gy") == 0, 128, 0)
    for a in range(3):
        for xg in range(2):
            slot = turned.at[2 * a + xg]
            slot[...] = fields[a, 4 * xg : 4 * xg + 4].reshape(128, 128).T
            for k in range(4):
                tiles = [slot[pl.ds(depth_of(k, g), 8, stride=16), :] for g in range(4)]
                a1, a3 = tiles[1], tiles[3]
                tiles[1], tiles[3] = jnp.where(trade, a3, a1), jnp.where(trade, a1, a3)
                for x4, tile in enumerate(regroup(tiles, 1, 32, lane)):
                    staged[pl.ds(a * 32 + k * 8 + 2 * x4 + xg, 8, stride=96), :] = tile
    for x in range(GX):
        for y in range(GY):
            start = pl.multiple_of(chunk_of(x, y, z) * 96, 96)
            out_ref[y * GX + x] = staged[pl.ds(start, 96), :]


def pack(fields):
    return pl.pallas_call(
        pack_kernel,
        out_shape=jax.ShapeDtypeStruct((8, 96, 128), jnp.float32),
        in_specs=[pl.BlockSpec(memory_space=pltpu.VMEM)],
        out_specs=pl.BlockSpec(memory_space=pltpu.VMEM),
        scratch_shapes=[pltpu.VMEM((6, 128, 128), jnp.float32), pltpu.VMEM((768, 128), jnp.float32)],
        compiler_params=pltpu.CompilerParams(vmem_limit_bytes=4 * 2**20),
        name="pack",
    )(fields)


def shape_of(*dims):
    return jax.ShapeDtypeStruct(dims + TILE, jnp.float32)


def scratch(*dims):
    return pltpu.VMEM(dims + TILE, jnp.float32)


def halo_masks():
    x, y, z = position()
    chunk = chunk_of(x, y, z)
    half = lane_ids() // 64
    return chunk, (half + chunk % 2) == 1


PLACE = [(r, True) for r in range(6)] + [(4, False), (5, False), (3, False), (2, False), (1, False), (0, False)]
PLACE += [(6, False), (6, True)]
FIRST_TILE = (0, 6, 13)
MESSAGE = 19


def message(planes, near, count):
    tiles = [jnp.where(near, planes[t], planes[t + 4]) for t in range(4)]
    tiles += [jnp.where(near, planes[t], lanes(planes[t + 2], 64)) for t in (4, 5)]
    if count == 7:
        tiles.append(jnp.where(near, lanes(planes[2], 64), planes[3]))
    return tiles


def halo_plane(even, odd, a, r, from_even):
    tile, moved = PLACE[r]
    tile = FIRST_TILE[a] + tile
    if moved:
        return lanes(jnp.where(from_even, odd[tile], even[tile]), 64)
    return jnp.where(from_even, even[tile], odd[tile])


def slab_kernel(in_ref, out_ref, b_ref, even_ref, odd_ref):
    lane, row = lane_ids(), row_ids()
    low = (lane // 32) % 2 == 0
    _, from_even = halo_masks()
    for a in range(3):
        planes = [None] * 8
        for k in range(4):
            part = ([], [])
            for x in range(GX):
                first = in_ref[x, pl.ds(a * 32 + k * 8, 8), :]
                second = in_ref[GX + x, pl.ds(a * 32 + k * 8, 8), :]
                turned = lanes(jnp.where(low, second, first), 32)
                part[0].append(jnp.where(low, first, turned))
                part[1].append(jnp.where(low, turned, second))
            for pp in range(2):
                planes[k + 4 * pp] = jnp.stack(regroup(part[pp], 0, 2, row))
                if a == 2:
                    b_ref[k + 4 * pp] = planes[k + 4 * pp]
                else:
                    out_ref[a, k + 4 * pp] = planes[k + 4 * pp]
        count = 7 if a == 1 else 6
        for near, ref in ((from_even, even_ref), (~from_even, odd_ref)):
            for t, tile in enumerate(message(planes, near, count)):
                ref[FIRST_TILE[a] + t] = tile


def to_slab(received):
    vmem = pl.BlockSpec(memory_space=pltpu.VMEM)
    return pl.pallas_call(
        slab_kernel,
        out_shape=[shape_of(2, 8, 4), shape_of(8, 4), shape_of(MESSAGE, 4), shape_of(MESSAGE, 4)],
        in_specs=[vmem],
        out_specs=[vmem] * 4,
        compiler_params=pltpu.CompilerParams(vmem_limit_bytes=4 * 2**20),
        name="to_slab",
    )(received)


class Planes:
    def __init__(self, *segments):
        self.segments = [(first, first + ref.shape[0], ref) for first, ref in segments]

    def find(self, p, q):
        for first, last, ref in self.segments:
            low, high = max(p, first), min(q, last)
            if low < high:
                yield low, high, ref, slice(low - first, high - first)

    def get(self, p, q):
        pieces = [ref[place] for _, _, ref, place in self.find(p, q)]
        return pieces[0] if len(pieces) == 1 else jnp.concatenate(pieces, axis=0)

    def put(self, p, value):
        for low, high, ref, place in self.find(p, p + value.shape[0]):
            ref[place] = value[low - p : high - p]


def spans(first, last, size):
    return [(p, min(p + size, last)) for p in range(first, last, size)]


def x_up(value):
    return jnp.concatenate([value[:, 1:], rows(value[:, :1], -1)], axis=1)


def x_down(value):
    return jnp.concatenate([rows(value[:, -1:], 1), value[:, :-1]], axis=1)


def couple(v, p, q, cx, cy, cz, dup):
    here, by_x, by_y = v.get(p, q), cx.get(p, q), cy.get(p, q)
    total = by_x * x_up(here) + x_down(by_x * here)
    total = total + (by_y * lanes(here, -dup) + lanes(by_y * here, dup))
    return total + (cz.get(p, q) * v.get(p - 1, q - 1) + cz.get(p + 1, q + 1) * v.get(p + 1, q + 1))


def chebyshev_factors(count, lower):
    center = (UPPER_EIG + lower) / 2.0
    half_width = (UPPER_EIG - lower) / 2.0
    ratio = center / half_width
    old = 1.0 / ratio
    out = [(0.0, 1.0 / center)]
    for _ in range(count - 1):
        new = 1.0 / (2.0 * ratio - old)
        out.append((new * old, 2.0 * new / half_width))
        old = new
    return out


def sweep(new, now, before, factor, b, dinv, coeffs, p, q, dup, size):
    carry, gain = factor
    for p, q in spans(p, q, size):
        base = (1.0 + carry - gain) * now.get(p, q)
        if carry != 0.0 and before is not None:
            base = base - carry * before.get(p, q)
        new.put(p, (b.get(p, q) + couple(now, p, q, *coeffs, dup)) * (gain * dinv.get(p, q)) + base)


def close(v, last):
    v.put(last, lanes(v.get(last - 1, last), 64))


def smooth(pair, b, dinv, coeffs, factors, first, last, dup, size):
    before, now, spare = pair
    for number, factor in enumerate(factors):
        new = spare if before is None else before
        sweep(new, now, before, factor, b, dinv, coeffs, first + number, last, dup, size)
        close(new, last)
        before, now = now, new
    return now


def inverse(value):
    guess = pl.reciprocal(value, approx=True)
    return guess * (2.0 - value * guess)


def level_coefficients(beta, alpha, first, last, shift, dup, cx, cy, cz, dinv, diag, ends, seam, size):
    lane, row = lane_ids(), row_ids()
    y_last = (lane % 64) // dup == 64 // dup - 1
    y_first = (lane % 64) // dup == 0
    x_rim = jnp.where(row == 0, 0.5, 0.0), jnp.where(row == 7, 0.5, 0.0)
    for p, q in spans(first, last, size):
        here = beta.get(p, q)
        by_x = 0.5 * (here + x_up(here))
        by_x = jnp.concatenate([by_x[:, :-1], jnp.where(row == 7, 0.0, by_x[:, -1:])], axis=1)
        above = jnp.where(y_last, 0.0, lanes(here, -dup))
        below = jnp.where(y_first, 0.0, lanes(here, dup))
        by_y = jnp.where(y_last, 0.0, 0.5 * (here + above))
        face = 0.5 * (beta.get(p - 1, q - 1) + here)
        total = shift * alpha.get(p, q) + (by_x + x_down(by_x)) + (here + 0.5 * (above + below))
        total = total + (face + 0.5 * (here + beta.get(p + 1, q + 1)))
        groups = [total[:, i : i + 1] for i in range(total.shape[1])]
        groups[0] = groups[0] + here[:, :1] * x_rim[0]
        groups[-1] = groups[-1] + here[:, -1:] * x_rim[1]
        total = jnp.concatenate(groups, axis=1)
        cx.put(p, by_x)
        cy.put(p, by_y)
        cz.put(p, face)
        diag.put(p, total)
        dinv.put(p, inverse(jnp.where(total > 0.0, total, 1.0)))
    if first <= seam < last:
        cz.put(seam, cz.get(seam, seam + 1) * ends)
    else:
        cz.put(last, 0.5 * (beta.get(last - 1, last) + beta.get(last, last + 1)))


def restrict_pair(first, second, dup):
    lane = lane_ids()
    total = first + second
    total = jnp.concatenate([total[:, i : i + 1] + total[:, i + 1 : i + 2] for i in range(0, total.shape[1], 2)], axis=1)
    return total + jnp.where((lane // dup) % 2 == 0, lanes(total, -dup), lanes(total, dup))


def restrict(take, p, q, dup):
    fine = take(2 * p, 2 * q)
    fine = fine.reshape((q - p, 2) + fine.shape[1:])
    return restrict_pair(fine[:, 0], fine[:, 1], dup)


def ends_factor():
    x, y, z = position()
    slab = 8 * z + chunk_of(x, y, z)
    half = lane_ids() // 64
    end = ((half == 0) & (slab == 0)) | ((half == 1) & (slab == 8 * GZ - 1))
    return jnp.where(end, 0.0, 1.0)


def call(kernel, name, operands, out_shape, scratch_shapes):
    vmem = pl.BlockSpec(memory_space=pltpu.VMEM)
    return pl.pallas_call(
        kernel,
        out_shape=out_shape,
        in_specs=[vmem] * len(operands),
        out_specs=[vmem] * len(out_shape),
        scratch_shapes=scratch_shapes,
        compiler_params=pltpu.CompilerParams(vmem_limit_bytes=16 * 2**20),
        name=name,
    )(*operands)


PRE_SHAPES = [(7, 4), (7, 4), (8, 4), (7, 4), (7, 4), (3, 2), (3, 2), (4, 2), (3, 2), (3, 2)]
MID_SHAPES = [(5, 4), (5, 4), (5, 4), (5, 4), (1, 4), (7, 2), (7, 2), (7, 2), (7, 2)]
LOW_SHAPES = [(8, 4), (8, 4), (8, 4), (8, 4), (12, 4), (7, 2)]


def coefficient_planes(pre, mid, low):
    zero, one = [], []
    for i in range(5):
        parts = [(4, low[i])] if low else []
        parts += [(16 if i == 4 else 12, mid[i])] if mid else []
        zero.append(Planes(*parts, *([(17, pre[i])] if pre else [])))
        parts = []
        if mid and i < 4:
            parts = [(2, mid[5 + i])]
        elif low and i == 4:
            parts = [(2, low[5])]
        one.append(Planes(*parts, *([(9, pre[5 + i])] if pre and len(pre) > 5 + i else [])))
    return zero, one


def pre_kernel(own, own_b, *refs):
    pre, (alpha1, beta1, v1, v2, v3, v4), (ghost, ghost1) = refs[:10], refs[10:16], refs[16:]
    zero, one = coefficient_planes(pre, None, None)
    alpha, beta = Planes((16, own.at[0])), Planes((16, own.at[1]), (24, ghost))
    alpha_one, beta_one = Planes((8, alpha1)), Planes((8, beta1), (12, ghost1))
    close(beta, PLANES)
    level_coefficients(beta, alpha, 17, PLANES, SHIFT_BASE, 1, *zero, None, 16, COEF_SPAN)
    beta_one.put(8, 0.125 * restrict(beta.get, 8, PLANES1, 1))
    alpha_one.put(8, 0.125 * restrict(alpha.get, 8, PLANES1, 1))
    close(beta_one, PLANES1)
    level_coefficients(beta_one, alpha_one, 9, PLANES1, SHIFT_BASE * 4.0, 2, *one, None, 8, COEF_SPAN1)
    b, coeffs, dinv = Planes((16, own_b)), zero[:3], zero[3]
    factors = chebyshev_factors(SWEEPS, SMOOTH_LOWER)
    iterates = [None, Planes((17, v1)), Planes((18, v2)), Planes((19, v3)), Planes((20, v4))]
    for p, q in spans(17, PLANES, 4):
        iterates[1].put(p, factors[0][1] * (b.get(p, q) * dinv.get(p, q)))
    close(iterates[1], PLANES)
    for i in range(2, 5):
        sweep(iterates[i], iterates[i - 1], iterates[i - 2], factors[i - 1], b, dinv, coeffs, 16 + i, PLANES, 1, SPAN)
        close(iterates[i], PLANES)


def mid_part(own, even, odd, beta1_own, alpha1_own, mid, low, beta_s, alpha_s, beta1_s, alpha1_s):
    _, from_even = halo_masks()
    zero, one = coefficient_planes(None, mid, low)
    for p in range(2, 16):
        beta_s[p] = halo_plane(even, odd, 1, 15 - p, from_even)
        if p >= 4:
            alpha_s[p] = halo_plane(even, odd, 0, 15 - p, from_even)
    beta, alpha = Planes((0, beta_s), (16, own.at[1])), Planes((0, alpha_s), (16, own.at[0]))
    ends = ends_factor()
    level_coefficients(beta, alpha, 4, 17, SHIFT_BASE, 1, *zero, ends, 16, COEF_SPAN)
    beta_one, alpha_one = Planes((0, beta1_s), (8, beta1_own)), Planes((0, alpha1_s), (8, alpha1_own))
    for p in range(1, 8):
        beta_one.put(p, 0.125 * restrict(beta.get, p, p + 1, 1))
        if p >= 2:
            alpha_one.put(p, 0.125 * restrict(alpha.get, p, p + 1, 1))
    level_coefficients(beta_one, alpha_one, 2, 9, SHIFT_BASE * 4.0, 2, *one, ends, 8, COEF_SPAN1)


def post_kernel(own, own_b, odd, even, *refs):
    pre, (alpha1, beta1, v1, v2, v3, v4), (gather, rim, halo_b, late, u1, b1) = refs[:10], refs[10:16], refs[16:22]
    mid, low, (f1, f2, f3, f4, low_b, b1_s, w_a, w_b), scratch_mid = refs[22:31], refs[31:37], refs[37:45], refs[45:]
    mid_part(own, even, odd, beta1, alpha1, mid, low, *scratch_mid)
    lane = lane_ids()
    _, from_even = halo_masks()
    zero, one = coefficient_planes(pre, mid, low)
    coeffs, dinv, diag = zero[:3], zero[3], zero[4]
    b = Planes((4, low_b), (12, halo_b), (16, own_b))
    for p in range(4, 16):
        b.put(p, halo_plane(even, odd, 2, 15 - p, from_even)[None])
    factors = chebyshev_factors(SWEEPS, SMOOTH_LOWER)
    iterates = [
        None,
        Planes((4, f1), (17, v1)),
        Planes((5, f2), (18, v2)),
        Planes((6, f3), (19, v3)),
        Planes((7, f4), (16, late), (20, v4)),
    ]
    for p, q in spans(4, 17, 4):
        iterates[1].put(p, factors[0][1] * (b.get(p, q) * dinv.get(p, q)))
    for i in range(2, 5):
        sweep(iterates[i], iterates[i - 1], iterates[i - 2], factors[i - 1], b, dinv, coeffs, 3 + i, 16 + i, 1, SPAN)
    v = iterates[4]
    rim[0:20] = v.get(16, 21).reshape((20,) + TILE)

    def residual(v, b, diag, coeffs, dup):
        return lambda p, q: (b.get(p, q) + couple(v, p, q, *coeffs, dup)) - diag.get(p, q) * v.get(p, q)

    b_one = Planes((4, b1_s), (8, b1))
    for p in range(4, PLANES1):
        b_one.put(p, 0.5 * restrict(residual(v, b, diag, coeffs, 1), p, p + 1, 1))
    coeffs, dinv, diag = one[:3], one[3], one[4]
    w, spare = Planes((0, w_a)), Planes((0, w_b))
    w.put(4, factors[0][1] * (b_one.get(4, PLANES1) * dinv.get(4, PLANES1)))
    close(w, PLANES1)
    w = smooth((None, w, spare), b_one, dinv, coeffs, factors[1:], 5, PLANES1, 2, SPAN1)
    b_two = 0.5 * restrict(residual(w, b_one, diag, coeffs, 2), 4, 6, 2)
    beta_two = 0.125 * restrict(Planes((8, beta1)).get, 4, 6, 2)
    alpha_two = 0.125 * restrict(Planes((8, alpha1)).get, 4, 6, 2)
    slot = lane % 4
    both = jnp.where(slot < 2, *(jnp.where(slot % 2 == 0, field[0, 0], field[1, 0]) for field in (b_two, beta_two)))
    last = jnp.where(slot % 2 == 0, alpha_two[0, 0], alpha_two[1, 0])
    last = jnp.where(slot[:4] < 2, last[:4], last[4:])
    for n in range(COUNT):
        for i, part in enumerate((both[:4], both[4:], last)):
            gather[n, i] = part
    u1[...] = w.get(8, PLANES1)
    rim[20:28] = jnp.where(lane % 2 == 0, w.get(8, PLANES1), b_one.get(8, PLANES1)).reshape((8,) + TILE)


def down_pre(own, own_b):
    shapes = PRE_SHAPES + [(4, 2), (4, 2), (8, 4), (7, 4), (6, 4), (5, 4)]
    return call(pre_kernel, "down_pre", (own, own_b), [shape_of(*n) for n in shapes], [scratch(1, 4), scratch(1, 2)])


def down_post(own, own_b, even, odd, pre):
    shapes = [shape_of(*n) for n in [(RIM,), (4, 4), (4, 4), (4, 2), (4, 2), *MID_SHAPES]]
    spare = [(13, 4), (13, 4), (13, 4), (9, 4), (8, 4), (4, 2), (13, 2), (13, 2), (16, 4), (16, 4), (8, 2), (8, 2)]
    return call(
        post_kernel, "down_post", (own, own_b, odd, even, *pre),
        [jax.ShapeDtypeStruct((COUNT, 3, 4, 128), jnp.float32), *shapes], [scratch(*n) for n in LOW_SHAPES + spare],
    )


def outer(value, half):
    turned = lanes(value, 64)
    before = jnp.concatenate([lanes(value[-1:], 65), turned[:-1]], axis=0)
    after = jnp.concatenate([turned[1:], lanes(value[:1], 63)], axis=0)
    return jnp.where(half == 0, before, after), turned


def coarse_kernel(gathered, out, tiles_s, e2_s):
    lane, row = lane_ids(), row_ids()
    half = lane // 64
    x, y, z = position()
    for n in range(COUNT):
        tiles_s[n, 0] = jnp.concatenate([gathered[n, 0], gathered[n, 1]], axis=0)
        tiles_s[n, 1] = jnp.concatenate([gathered[n, 2], lanes(gathered[n, 2], -2)], axis=0)

    def collect(tile, slot):
        out = []
        for group in range(8):
            joined = None
            for q in range(GZ):
                natural = 7 - group if q % 2 else group
                rank, core = natural // 2, natural % 2
                n = ((rank ^ (rank >> 1)) * GZ + q) * GY + core
                piece = tiles_s[n, tile] if q == slot else lanes(tiles_s[n, tile], q - slot)
                joined = piece if joined is None else jnp.where(lane % 4 == q, piece, joined)
            out.append(joined)
        return jnp.stack(out)

    b_two, beta_two, alpha_two = ([collect(tile, slot + p) for p in range(2)] for tile, slot in ((0, 0), (0, 2), (1, 0)))
    slab = lax.broadcasted_iota(jnp.int32, (8,) + TILE, 0)
    end = ((slab == 0) & (lane % 4 == 0) & (half == 0)) | ((slab == 7) & (lane % 4 == 3) & (half == 1))

    def sides(beta, dx, dy):
        place = (lane % 64) // dy
        rims = row >= 8 - dx, row < dx, place == 64 // dy - 1, place == 0
        others = rows(beta, -dx), rows(beta, dx), lanes(beta, -dy), lanes(beta, dy)
        faces = [jnp.where(rim, 0.0, 0.5 * (beta + other)) for rim, other in zip(rims, others)]
        edge = jnp.where(rims[0] | rims[1], 0.5, 0.0) + jnp.where(rims[2] | rims[3], 0.5, 0.0)
        return faces, (faces[0] + faces[1]) + (faces[2] + faces[3]) + beta * edge

    def scaled(faces, inv):
        return [face * inv for face in faces]

    def flat(v, coeffs, dx, dy):
        x_above, x_below, y_above, y_below = coeffs
        total = x_above * rows(v, -dx) + x_below * rows(v, dx)
        return total + (y_above * lanes(v, -dy) + y_below * lanes(v, dy))

    faces_a, sum_a = sides(beta_two[0], 1, 4)
    faces_b, sum_b = sides(beta_two[1], 1, 4)
    middle = 0.5 * (beta_two[0] + beta_two[1])
    inner = 0.5 * (beta_two[1] + lanes(beta_two[1], 64))
    edge = 0.5 * (beta_two[0] + jnp.where(end, 0.0, outer(beta_two[0], half)[0]))
    shift = SHIFT_BASE * 16.0
    diag_a = shift * alpha_two[0] + sum_a + (middle + edge)
    diag_b = shift * alpha_two[1] + sum_b + (middle + inner)
    inv_a, inv_b = inverse(diag_a), inverse(diag_b)
    flat_a, flat_b = scaled(faces_a, inv_a), scaled(faces_b, inv_b)
    middle_a, middle_b = middle * inv_a, middle * inv_b
    rim_a, inner_b = jnp.where(end, 0.0, edge) * inv_a, inner * inv_b
    rhs_a, rhs_b = b_two[0] * inv_a, b_two[1] * inv_b

    def apply_two(va, vb):
        ta = flat(va, flat_a, 1, 4) + (middle_a * vb + rim_a * outer(va, half)[0])
        tb = flat(vb, flat_b, 1, 4) + (middle_b * va + inner_b * lanes(vb, 64))
        return ta, tb

    def sweeps_two(before, now, factors):
        for carry, gain in factors:
            totals = apply_two(*now)
            new = []
            for v, old, rhs, total in zip(now, before or (None, None), (rhs_a, rhs_b), totals):
                base = (1.0 + carry - gain) * v + gain * rhs
                if carry != 0.0 and old is not None:
                    base = base - carry * old
                new.append(base + gain * total)
            before, now = now, new
        return now

    factors = chebyshev_factors(SWEEPS, SMOOTH_LOWER)
    ua, ub = sweeps_two(None, (factors[0][1] * rhs_a, factors[0][1] * rhs_b), factors[1:])
    ta, tb = apply_two(ua, ub)

    def restrict_whole(first, second):
        total = first + second
        total = total + jnp.where(row % 2 == 0, rows(total, -1), rows(total, 1))
        return total + jnp.where((lane // 4) % 2 == 0, lanes(total, -4), lanes(total, 4))

    second = (lane // 4) % 2 == 1

    def pack_low(value):
        return jnp.where(second, value[4:], value[:4])

    def outer_low(value):
        turned = lanes(value, 64)
        first_one, last_one = value[:1], value[-1:]
        before = jnp.where(second, lanes(last_one, 68), lanes(last_one, 61))
        after = jnp.where(second, lanes(first_one, 67), lanes(first_one, 60))
        before = jnp.concatenate([before, turned[:-1]], axis=0)
        after = jnp.concatenate([turned[1:], after], axis=0)
        return jnp.where(half == 0, before, after), turned

    b_low = 0.5 * pack_low(restrict_whole(diag_a * (rhs_a + ta - ua), diag_b * (rhs_b + tb - ub)))
    beta_low = 0.125 * pack_low(restrict_whole(beta_two[0], beta_two[1]))
    alpha_low = 0.125 * pack_low(restrict_whole(alpha_two[0], alpha_two[1]))
    slab = lax.broadcasted_iota(jnp.int32, (4,) + TILE, 0) + jnp.where(second, 4, 0)
    end_low = ((slab == 0) & (lane % 4 == 0) & (half == 0)) | ((slab == 7) & (lane % 4 == 3) & (half == 1))
    faces_low, sum_low = sides(beta_low, 2, 8)
    beyond, turned = outer_low(beta_low)
    inner_low = 0.5 * (beta_low + turned)
    edge_low = 0.5 * (beta_low + jnp.where(end_low, 0.0, beyond))
    inv_low = inverse(SHIFT_BASE * 64.0 * alpha_low + sum_low + (inner_low + edge_low))
    flat_low = scaled(faces_low, inv_low)
    rim_low = jnp.where(end_low, 0.0, edge_low) * inv_low
    inner_low = inner_low * inv_low
    rhs_low = b_low * inv_low
    before = v = None
    for carry, gain in chebyshev_factors(BOTTOM, BOTTOM_LOWER):
        if v is None:
            v = gain * rhs_low
            continue
        beyond, turned = outer_low(v)
        base = (1.0 + carry - gain) * v + gain * rhs_low
        if before is not None:
            base = base - carry * before
        base = base + gain * (flat_low[0] * rows(v, -2) + flat_low[1] * rows(v, 2))
        total = flat_low[2] * lanes(v, -8) + flat_low[3] * lanes(v, 8)
        before, v = v, base + gain * (total + (inner_low * turned + rim_low * beyond))
    v = jnp.concatenate([jnp.where(second, lanes(v, 4), v), jnp.where(second, v, lanes(v, -4))], axis=0)
    va, vb = sweeps_two(None, (ua + v, ub + v), factors)
    for group in range(8):
        e2_s[group, 0] = va[group]
        e2_s[group, 1] = vb[group]

    chunk = chunk_of(x, y, z)
    place = 8 * z + chunk

    def fetch(offset, p, turn=0):
        index = jnp.clip(place + offset, 0, COUNT - 1)
        tile, out = e2_s[index % 8, p], None
        for slot in range(4):
            piece = pltpu.roll(tile, (128 + slot + turn - index // 8) % 128, 1)
            out = piece if out is None else jnp.where(lane % 4 == slot, piece, out)
        return out

    first = half == 0
    out[0] = jnp.where(first, fetch(-1, 0), fetch(1, 0))
    out[1] = jnp.where(first, fetch(-1, 1), fetch(1, 1))
    out[2] = jnp.where(first, fetch(-1, 1, 64), fetch(1, 1, 64))
    out[3] = jnp.where(first, fetch(-1, 0, 64), fetch(1, 0, 64))
    out[4] = fetch(0, 0)
    out[5] = fetch(0, 1)


def coarse(gathered):
    vmem = pl.BlockSpec(memory_space=pltpu.VMEM)
    return pl.pallas_call(
        coarse_kernel,
        out_shape=shape_of(6),
        in_specs=[vmem],
        out_specs=vmem,
        scratch_shapes=[scratch(COUNT, 2), scratch(8, 2)],
        compiler_params=pltpu.CompilerParams(vmem_limit_bytes=8 * 2**20),
        name="coarse",
    )(gathered)


def up_kernel(e_two, rim_even, rim_odd, own_b, halo_b, late, u1, b1, v4, *refs):
    pre, mid, (out, v_a, v_b, w_a, w_b, bx_s) = refs[:9], refs[9:18], refs[18:]
    zero, one = coefficient_planes(pre, mid, None)
    lane, row = lane_ids(), row_ids()
    _, from_even = halo_masks()
    factors = chebyshev_factors(SWEEPS, SMOOTH_LOWER)

    for p in range(1, 8):
        if p >= 4:
            k = 7 - p
            both = lanes(jnp.where(from_even, rim_odd[20 + 2 * k : 22 + 2 * k], rim_even[20 + 2 * k : 22 + 2 * k]), 64)
        else:
            both = jnp.where(from_even, rim_even[20 + 2 * p : 22 + 2 * p], rim_odd[20 + 2 * p : 22 + 2 * p])
        w_a[p] = jnp.where(lane % 2 == 0, both, lanes(both, 1)) + e_two[p // 2]
        if p >= 2:
            bx_s[p] = jnp.where(lane % 2 == 0, lanes(both, -1), both)
    for p in range(8, PLANES1):
        w_a[p] = u1[p - 8] + e_two[p // 2]
    w_a[PLANES1] = lanes(w_a[PLANES1 - 1], 64)
    pair = (Planes((0, w_b)), Planes((0, w_a)), None)
    w = smooth(pair, Planes((0, bx_s), (8, b1)), one[3], one[:3], factors, 2, PLANES1, 2, SPAN1)

    for p in range(11, PLANES):
        if p >= 16:
            start = Planes((16, late), (20, v4)).get(p, p + 1)[0]
        else:
            k = 4 * (15 - p)
            start = lanes(jnp.where(from_even, rim_odd[k : k + 4], rim_even[k : k + 4]), 64)
        e_one = w.get(p // 2, p // 2 + 1)[0]
        e_one = jnp.concatenate([e_one[:1], e_one[:1], e_one[1:], e_one[1:]], axis=0)
        v_a[p] = start + e_one
    v_a[PLANES] = lanes(v_a[PLANES - 1], 64)
    b, diag, coeffs = Planes((12, halo_b), (16, own_b)), zero[4], zero[:3]
    v = smooth((Planes((0, v_b)), Planes((0, v_a)), None), b, zero[3], coeffs, factors, 12, PLANES, 1, SPAN)
    low = (lane // 32) % 2 == 0
    for k in range(4):
        for o in range(2):
            parts = []
            for pp in range(2):
                p = 16 + k + 4 * pp
                value = v.get(p, p + 1)
                if o == 1:
                    value = (b.get(p, p + 1) + couple(v, p, p + 1, *coeffs, 1)) - diag.get(p, p + 1) * value
                parts.append(regroup([value[0, i] for i in range(4)], 0, 2, row))
            for i in range(GX):
                one, two = parts[0][i], parts[1][i]
                turned = lanes(jnp.where(low, two, one), 32)
                out[i, pl.ds(o * 32 + k * 8, 8), :] = jnp.where(low, one, turned)
                out[GX + i, pl.ds(o * 32 + k * 8, 8), :] = jnp.where(low, turned, two)


def up(*operands):
    return call(
        up_kernel, "up_strokes", operands, [jax.ShapeDtypeStruct((8, 64, 128), jnp.float32)],
        [scratch(25, 4), scratch(25, 4), scratch(13, 2), scratch(13, 2), scratch(8, 2)],
    )[0]


def unpack_kernel(in_ref, v_ref, r_ref, fields, turned, staged, left):
    z = lax.axis_index("gz")
    lane = lane_ids()
    trade = lane < jnp.where(lax.axis_index("gy") == 1, 128, 0)
    for x in range(GX):
        for y in range(GY):
            start = pl.multiple_of(chunk_of(x, y, z) * 64, 64)
            staged[pl.ds(start, 64), :] = in_ref[y * GX + x]
    copies = [pltpu.make_async_copy(fields.at[o], ref, left.at[o]) for o, ref in enumerate((v_ref, r_ref))]
    for o, copy in enumerate(copies):
        for xg in range(2):
            slot = turned.at[2 * o + xg]
            for k in range(4):
                tiles = [staged[pl.ds(o * 32 + k * 8 + 2 * x4 + xg, 8, stride=64), :] for x4 in range(4)]
                tiles = regroup(tiles, 1, 32, lane)
                a0, a2 = tiles[0], tiles[2]
                tiles[0], tiles[2] = jnp.where(trade, a2, a0), jnp.where(trade, a0, a2)
                for g, tile in enumerate(tiles):
                    slot[pl.ds(depth_of(k, g), 8, stride=16), :] = tile
            fields[o, 4 * xg : 4 * xg + 4] = slot[...].T.reshape(4, 32, 128)
        copy.start()
    for copy in copies:
        copy.wait()


def unpack(received):
    vmem = pl.BlockSpec(memory_space=pltpu.VMEM)
    return pl.pallas_call(
        unpack_kernel,
        out_shape=[jax.ShapeDtypeStruct(BLOCK, jnp.float32)] * 2,
        in_specs=[vmem],
        out_specs=[pl.BlockSpec(memory_space=pltpu.HBM)] * 2,
        scratch_shapes=[
            pltpu.VMEM((2,) + BLOCK, jnp.float32),
            pltpu.VMEM((4, 128, 128), jnp.float32),
            pltpu.VMEM((512, 128), jnp.float32),
            pltpu.SemaphoreType.DMA((2,)),
        ],
        compiler_params=pltpu.CompilerParams(vmem_limit_bytes=4 * 2**20),
        name="unpack",
    )(received)


def slab_shards(right_side, alpha_coef, beta_coef):
    even_pairs, odd_pairs = swap_pairs(False), swap_pairs(True)
    packed = pack(jnp.stack([alpha_coef, beta_coef, right_side]))
    own, own_b, to_even, to_odd = to_slab(lax.all_to_all(packed, RING, 0, 0))
    even = lax.ppermute(to_even, ALL, even_pairs)
    odd = lax.ppermute(to_odd, ALL, odd_pairs)
    found = down_pre(own, own_b)
    pre, v4 = found[:9], found[15]
    gather, rim, halo_b, late, u1, b1, *mid = down_post(own, own_b, even, odd, found)
    rim_even = lax.ppermute(rim, ALL, even_pairs)
    rim_odd = lax.ppermute(rim, ALL, odd_pairs)
    kept = (own_b, halo_b, late, u1, b1, v4, *pre, *mid)
    result = up(coarse(lax.all_to_all(gather, ("gx", "gz", "gy"), 0, 0)), rim_even, rim_odd, *kept)
    return tuple(unpack(lax.all_to_all(result, RING, 0, 0)))


def solution(mesh):
    spec = P("gx", "gy", "gz")
    plain = jax.shard_map(shards, mesh=mesh, in_specs=(spec,) * 3, out_specs=(spec,) * 2, check_vma=False)
    slabs = jax.shard_map(slab_shards, mesh=mesh, in_specs=(spec,) * 3, out_specs=(spec,) * 2, check_vma=False)
    sizes = tuple(mesh.shape[axis] for axis in ALL)

    def run(right_side, alpha_coef, beta_coef):
        block = tuple(n // size for n, size in zip(right_side.shape, sizes))
        fits = sizes == (GX, GY, GZ) and block == BLOCK
        return (slabs if fits else plain)(right_side, alpha_coef, beta_coef)

    return run
```
